32 devices in a mesh: dp: 4 (over y, x), head: 8 (over z, core).
Axes of the slice: x: 2, y: 2, z: 4, core: 2. Of those that a mesh axis runs over, the one named last changes fastest.
Arguments:
- block_input: bfloat16 [16384, 1536], P(('dp', 'head')), may hold values from -6 to 6
- lengths: int32 [4, 4], P('dp'), may hold values from 1 to 2048, 4096 in all within a row
- norm_gain: float32 [1536], replicated, may hold values from 0.5 to 1.5
- in_gate: bfloat16 [1536, 3072], P('dp', 'head'), may hold values from -0.15625 to 0.15625
- in_value: bfloat16 [1536, 3072], P('dp', 'head'), may hold values from -0.15625 to 0.15625
- in_states: bfloat16 [1536, 256], P('dp', 'head'), may hold values from -0.15625 to 0.15625
- in_steps: bfloat16 [1536, 48], P('dp', 'head'), may hold values from -0.15625 to 0.15625
- conv_value: float32 [4, 3072], P(None, 'head'), may hold values from -3 to 3
- conv_value_bias: float32 [3072], P('head'), may hold values from -3 to 3
- conv_states: float32 [4, 256], P(None, 'head'), may hold values from -3 to 3
- conv_states_bias: float32 [256], P('head'), may hold values from -3 to 3
- step_bias: float32 [48], P('head'), may hold values from -6 to -2
- decay_log: float32 [48], P('head'), may hold values from 0 to 2.77
- skip_gain: float32 [48], P('head'), may hold values from 0.5 to 1.5
- gate_gain: float32 [3072], P('head'), may hold values from 0.5 to 1.5
- out_proj: bfloat16 [1536, 3072], P('dp', 'head'), may hold values from -0.109375 to 0.109375
- cotangent: bfloat16 [16384, 1536], P(('dp', 'head')), may hold values from -6 to 6
Outputs:
- out: bfloat16 [16384, 1536], P(('dp', 'head'))
- input_grad: bfloat16 [16384, 1536], P(('dp', 'head'))
- grad_norm_gain: float32 [1536], replicated
- grad_in_gate: float32 [1536, 3072], P('dp', 'head')
- grad_in_value: float32 [1536, 3072], P('dp', 'head')
- grad_in_states: float32 [1536, 256], P('dp', 'head')
- grad_in_steps: float32 [1536, 48], P('dp', 'head')
- grad_conv_value: float32 [4, 3072], P(None, 'head')
- grad_conv_value_bias: float32 [3072], P('head')
- grad_conv_states: float32 [4, 256], P(None, 'head')
- grad_conv_states_bias: float32 [256], P('head')
- grad_step_bias: float32 [48], P('head')
- grad_decay_log: float32 [48], P('head')
- grad_skip_gain: float32 [48], P('head')
- grad_gate_gain: float32 [3072], P('head')
- grad_out_proj: float32 [1536, 3072], P('dp', 'head')
The draws below stay inside these ranges and needn't reach their ends.
Inputs may be any that keep to these rules, and one draw needn't show every extreme that they name: Each row holds, in order, the lengths of the 4 sequences packed into one group of 4096 tokens; a row sums to 4096, and its longest sequence has exactly half of 4096 tokens.
All inputs are finite; a program needn't handle non-finite values.
Results may differ from the reference program's by a relative error of at most 0.012.
Values may be sent and summed in bfloat16 or wider, within the bound.
A program may use at most 320 MiB of HBM per device.

```python
import math
from functools import partial
import jax
import jax.numpy as jnp
import numpy as np
from jax import lax

D = 1536
H = 48
STATE = 128
CONV = 4
SPAN = 256
TOK_DEV = 4096
SEQ_DEV = 4
INNER = 3072
GROUPS = 4
TOKENS = 16384


def shard_levels(rng, dims, shards, low, high):
    def one(axis_at, parts):
        heights = jax.random.uniform(jax.random.fold_in(jax.random.fold_in(rng, 6), axis_at), (parts,), jnp.float32, low / len(shards), high / len(shards))
        return jnp.repeat(jnp.exp(heights), dims[axis_at] // parts).reshape((-1,) + (1,) * (len(dims) - axis_at - 1))

    gain = one(*shards[0])
    for cut in shards[1:]:
        gain = gain * one(*cut)
    return gain


def split_up(number_of, total, most, lean):
    loads = [(1 << 20) // math.isqrt(rank ** lean) + 1 for rank in range(2, number_of + 1)]
    rest, holding = total - most - (number_of - 1), [1] * (number_of - 1)
    while rest > 0:
        movable = [i for i in range(number_of - 1) if holding[i] < most]
        mass, remaining = sum([loads[i] for i in movable]), rest
        for i in movable:
            addition = min(most - holding[i], max(1, remaining * loads[i] // mass), rest)
            holding[i] = holding[i] + addition
            rest = rest - addition
    return np.array([most] + holding)


def ragged(key, amount, total, limit, slope):
    if amount == 2:
        one = jax.random.randint(key, (), max(1, total - limit), min(limit, total - 1) + 1)
        return jnp.stack([one, total - one])
    tallies = jnp.asarray(split_up(amount, total, limit, slope), jnp.int32)
    pairs = (amount - 1) // 2
    giver, sink = tallies[1:1 + 2 * pairs:2], tallies[2:2 + 2 * pairs:2]
    room = jnp.minimum(giver - 1, limit - sink)
    moved = jax.random.randint(jax.random.fold_in(key, 1), (pairs,), 0, 1 << 20) % (room + 1)
    tallies = tallies.at[1:1 + 2 * pairs:2].set(giver - moved).at[2:2 + 2 * pairs:2].set(sink + moved)
    return tallies[jax.random.permutation(jax.random.fold_in(key, 2), amount)]


def centred(rng, dims, deviation, most, cuts=(), kind=jnp.bfloat16):
    loudness = shard_levels(rng, dims, cuts, -0.22, 0.18) if cuts else 1.0
    entries = jax.random.normal(rng, dims, jnp.float32) * deviation * loudness
    return jnp.minimum(jnp.maximum(entries, -most), most).astype(kind)


def setup_inputs(seed: int = 0) -> dict:
    splits = jax.random.split(jax.random.key(seed), 18)
    block_input = centred(splits[0], (TOKENS, D), 1.0, 6.0, ((0, 32),))
    lengths = jax.vmap(lambda own: ragged(own, SEQ_DEV, TOK_DEV, TOK_DEV // 2, 2))(jax.random.split(splits[1], GROUPS)).reshape((GROUPS, SEQ_DEV)).astype(jnp.int32)
    norm_gain = jnp.clip(1.0 + 0.1 * jax.random.normal(splits[2], (D,), jnp.float32), 0.5, 1.5)
    in_gate = centred(splits[3], (D, INNER), D ** -0.5, 0.15625, ((0, 4), (1, 8)))
    in_value = centred(splits[4], (D, INNER), D ** -0.5, 0.15625, ((0, 4), (1, 8)))
    in_states = centred(splits[5], (D, 2 * STATE), D ** -0.5, 0.15625, ((0, 4), (1, 8)))
    in_steps = centred(splits[6], (D, H), D ** -0.5, 0.15625, ((0, 4), (1, 8)))
    conv_value = centred(splits[7], (CONV, INNER), CONV ** -0.5, 3.0, ((1, 8),), jnp.float32)
    conv_value_bias = centred(splits[8], (INNER,), 0.5, 3.0, ((0, 8),), jnp.float32)
    conv_states = centred(splits[9], (CONV, 2 * STATE), CONV ** -0.5, 3.0, ((1, 8),), jnp.float32)
    conv_states_bias = centred(splits[10], (2 * STATE,), 0.5, 3.0, ((0, 8),), jnp.float32)
    step_bias = jnp.clip(-6.0 + 4.0 * jax.random.uniform(splits[11], (H,), jnp.float32) ** shard_levels(splits[11], (H,), ((0, 8),), -0.2, 0.2), -6.0, -2.0)
    decay_log = jnp.clip(2.77 * jax.random.uniform(splits[12], (H,), jnp.float32) ** shard_levels(splits[12], (H,), ((0, 8),), -0.2, 0.2), 0.0, 2.77)
    skip_gain = jnp.clip(0.5 + 1.0 * jax.random.uniform(splits[13], (H,), jnp.float32) ** shard_levels(splits[13], (H,), ((0, 8),), -0.2, 0.2), 0.5, 1.5)
    gate_gain = jnp.clip(1.0 + 0.1 * jax.random.normal(splits[14], (INNER,), jnp.float32), 0.5, 1.5)
    out_proj = centred(splits[15], (D, INNER), INNER ** -0.5, 0.109375, ((0, 4), (1, 8)))
    cotangent = centred(splits[16], (TOKENS, D), 1.0, 6.0, ((0, 32),))
    return {"block_input": block_input, "lengths": lengths, "norm_gain": norm_gain, "in_gate": in_gate, "in_value": in_value, "in_states": in_states, "in_steps": in_steps, "conv_value": conv_value, "conv_value_bias": conv_value_bias, "conv_states": conv_states, "conv_states_bias": conv_states_bias, "step_bias": step_bias, "decay_log": decay_log, "skip_gain": skip_gain, "gate_gain": gate_gain, "out_proj": out_proj, "cotangent": cotangent}


EPSILON = 1e-05
HIGHEST = lax.Precision.HIGHEST

@jax.custom_vjp
def low(v):
    return lax.optimization_barrier(v.astype(jnp.bfloat16)).astype(jnp.float32)

@jax.custom_vjp
def low_back(v):
    return v

def low_keep(v):
    return (low(v), None)

def low_pass(kept, grad):
    return (grad,)

def back_keep(v):
    return (v, None)

def back_low(kept, grad):
    return (low(grad),)
low.defvjp(low_keep, low_pass)
low_back.defvjp(back_keep, back_low)

def segment_numbers(lengths, count):
    ends = jnp.cumsum(lengths, axis=1).astype(jnp.int32)
    places = jnp.arange(count, dtype=jnp.int32)
    return lax.optimization_barrier(jnp.sum((places[None, :, None] >= ends[:, None, :]).astype(jnp.int32), axis=2))

def causal_conv(source, weight, offset_bias, segment):
    tap_count = weight.shape[0]
    length = source.shape[0]
    running = offset_bias[None, :] + weight[tap_count - 1][None, :] * source
    for offset in range(1, tap_count):
        shifted = jnp.pad(source, ((offset, 0), (0, 0)))[:length]
        earlier = jnp.pad(segment, (offset, 0), constant_values=-1)[:length]
        matching = (earlier == segment).astype(jnp.float32)
        running = running + weight[tap_count - 1 - offset][None, :] * shifted * matching[:, None]
    return jax.nn.silu(running)

def state_space(values, steps, rates, keys_in, query_in, segment, block):
    count = values.shape[0] // block
    heads = values.shape[1]
    width = values.shape[2]
    pieces = (values.reshape(count, block, heads, width), steps.reshape(count, block, heads), keys_in.reshape(count, block, -1), query_in.reshape(count, block, -1), segment.reshape(count, block))
    lower_mask = jnp.tril(jnp.ones((block, block), dtype=bool))

    def advance(carry, piece):
        state, previous = carry
        value_block, step_block, keys_block, query_block, seg_block = piece
        decays = jnp.cumsum(step_block * rates[None, :], axis=0)
        within = lower_mask & (seg_block[:, None] == seg_block[None, :])
        spread = decays[:, None, :] - decays[None, :, :]
        weights = jnp.exp(jnp.where(within[:, :, None], spread, -1e+30))
        scores = jnp.dot(query_block, keys_block.T, precision=HIGHEST)
        driven = value_block * step_block[:, :, None]
        inside = jnp.einsum('tsh,shp->thp', scores[:, :, None] * weights, driven, precision=HIGHEST)
        carried = (seg_block == previous).astype(jnp.float32)
        reach = jnp.exp(decays) * carried[:, None]
        outside = jnp.einsum('tn,hpn->thp', query_block, state, precision=HIGHEST) * reach[:, :, None]
        final = seg_block[-1]
        kept = (final == previous).astype(jnp.float32)
        tail = jnp.exp(decays[-1][None, :] - decays) * (seg_block == final).astype(jnp.float32)[:, None]
        fresh = jnp.einsum('sh,shp,sn->hpn', tail, driven, keys_block, precision=HIGHEST)
        state = state * (jnp.exp(decays[-1]) * kept)[:, None, None] + fresh
        return ((state, final), inside + outside)
    start = (jnp.zeros((heads, width, keys_in.shape[1]), jnp.float32), jnp.array(-1, dtype=jnp.int32))
    _, result = lax.scan(jax.checkpoint(advance), start, pieces)
    return result.reshape(values.shape)

def mixer(values, states, gate_pre, steps_pre, step_bias, decay_log, skip_gain, segment):
    heads = step_bias.shape[0]
    state_width = states.shape[1] // 2
    steps = jax.nn.softplus(steps_pre + step_bias[None, :])
    rates = -jnp.exp(decay_log)
    shaped = values.reshape(values.shape[0], heads, -1)
    result = state_space(shaped, steps, rates, states[:, :state_width], states[:, state_width:], segment, SPAN)
    result = result + skip_gain[None, :, None] * shaped
    return result.reshape(values.shape) * jax.nn.silu(gate_pre)

def forward(rows, norm_gain, in_gate, in_value, in_states, in_steps, conv_value, conv_value_bias, conv_states, conv_states_bias, step_bias, decay_log, skip_gain, gate_gain, out_proj, segment):
    inverse = lax.rsqrt(lax.optimization_barrier(jnp.mean(rows * rows, axis=1, keepdims=True)) + EPSILON)
    normed = low(rows * inverse * norm_gain[None, :])
    gate_pre = low_back(jnp.dot(normed, in_gate, precision=HIGHEST))
    value_pre = low_back(jnp.dot(normed, in_value, precision=HIGHEST))
    states_pre = low_back(jnp.dot(normed, in_states, precision=HIGHEST))
    steps_pre = low_back(jnp.dot(normed, in_steps, precision=HIGHEST))
    values = low(causal_conv(value_pre, conv_value, conv_value_bias, segment))
    states = low(causal_conv(states_pre, conv_states, conv_states_bias, segment))
    mixed = mixer(values, states, gate_pre, steps_pre, step_bias, decay_log, skip_gain, segment)
    inverse_gate = lax.rsqrt(lax.optimization_barrier(jnp.mean(mixed * mixed, axis=1, keepdims=True)) + EPSILON)
    gated = low(mixed * gate_gain[None, :])
    branch = low_back(jnp.dot(gated, out_proj.T, precision=HIGHEST))
    return rows + inverse_gate * branch

def reference(block_input, lengths, norm_gain, in_gate, in_value, in_states, in_steps, conv_value, conv_value_bias, conv_states, conv_states_bias, step_bias, decay_log, skip_gain, gate_gain, out_proj, cotangent):
    starts = jnp.arange(lengths.shape[0], dtype=jnp.int32)[:, None] * (lengths.shape[1] + 1)
    segment = (segment_numbers(lengths, TOK_DEV) + starts).reshape(-1).astype(jnp.int32)
    arrays = (block_input, norm_gain, in_gate, in_value, in_states, in_steps, conv_value, conv_value_bias, conv_states, conv_states_bias, step_bias, decay_log, skip_gain, gate_gain, out_proj)
    floats = tuple((item.astype(jnp.float32) for item in arrays))
    result, pullback = jax.vjp(partial(forward, segment=segment), *floats)
    grads = pullback(cotangent.astype(jnp.float32))
    return (result.astype(jnp.bfloat16), grads[0].astype(jnp.bfloat16), grads[1], grads[2], grads[3], grads[4], grads[5], grads[6], grads[7], grads[8], grads[9], grads[10], grads[11], grads[12], grads[13], grads[14])
```

```python
import functools

import jax
import jax.numpy as jnp
from jax import lax
from jax.experimental import pallas as pl
from jax.experimental.pallas import tpu as pltpu
from jax.sharding import PartitionSpec as P

EPSILON = 1e-05
HALO = 16
LH = 128
QB = 128
LOG2E = 1.4426950408889634
TINY = 1e-30
F32 = jnp.float32
BF16 = jnp.bfloat16
MESH = pl.DeviceIdType.MESH
MIB = 1024 * 1024


def mm(a, b, ca, cb):
    return lax.dot_general(a, b, (((ca,), (cb,)), ((), ())), preferred_element_type=F32)


def shape(dims, dtype):
    return jax.ShapeDtypeStruct(dims, dtype)


def params(limit=48):
    return pltpu.CompilerParams(vmem_limit_bytes=limit * MIB)


def cost(flops, nbytes):
    return pl.CostEstimate(flops=int(flops), transcendentals=0, bytes_accessed=int(nbytes))


def chunk_of(count, most, unit):
    best = unit
    for size in range(unit, most + 1, unit):
        if count % size == 0:
            best = size
    return best


def sigmoid(v):
    return 0.5 * jnp.tanh(0.5 * v) + 0.5


def lane_chunks(count, most=256):
    return [pl.ds(base, most) for base in range(0, count, most)]


def folded(v):
    out = v[:, 0:128]
    for base in range(128, v.shape[1], 128):
        out = out + v[:, base : base + 128]
    return out


def lane_cumsum(v, reverse=False):
    size = v.shape[1]
    lane = lax.broadcasted_iota(jnp.int32, v.shape, 1)
    step = 1
    while step < size:
        if reverse:
            moved = pltpu.roll(v, size - step, 1)
            v = v + jnp.where(lane < size - step, moved, 0.0)
        else:
            moved = pltpu.roll(v, step, 1)
            v = v + jnp.where(lane >= step, moved, 0.0)
        step *= 2
    return v


def block_terms(dt, a2, seg_ref, b):
    cum = lane_cumsum(a2)
    logdt = jnp.log2(jnp.maximum(dt, TINY))
    source = cum - logdt
    q = dt.shape[1]
    prev = seg_ref[0:1, pl.ds(pl.multiple_of(b * q, q), q)][:, q - 1 :]
    segr = seg_ref[0:1, pl.ds(pl.multiple_of(LH + b * q, q), q)]
    segc = jnp.broadcast_to(segr, (q, q)).T
    last = cum[:, q - 1 : q]
    final = segr[:, q - 1 : q]
    reach = jnp.where(segr == prev, jnp.exp2(cum), 0.0)
    tail = jnp.where(segr == final, jnp.exp2(last - source), 0.0)
    kept = jnp.where(final == prev, jnp.exp2(last), 0.0)
    pad = (-dt.shape[0]) % 128
    padded = jnp.concatenate([source, jnp.zeros((pad, q), F32)], axis=0) if pad else source
    columns = padded.T
    row_s = lax.broadcasted_iota(jnp.int32, (q, q), 0)
    col_t = lax.broadcasted_iota(jnp.int32, (q, q), 1)
    bias = jnp.where((row_s <= col_t) & (segc == segr), 0.0, -1e30)
    return cum, columns, reach, tail, kept, bias


def scan_fwd_kernel(
    places, width,
    x_ref, dt_ref, a_ref, seg_ref, b_ref, c_ref, sin_ref, skip_ref,
    y_ref, st_ref, state,
):
    @pl.when(pl.program_id(0) == 0)
    def _():
        state[...] = sin_ref[...].astype(F32)

    cum, columns, reach, tail, kept, bias = block_terms(dt_ref[...], a_ref[...], seg_ref, pl.program_id(0))
    gt = mm(b_ref[...], c_ref[...], 1, 1)
    low = state[...].astype(BF16)
    st_ref[0] = low
    y_ref[...] = mm(low, c_ref[...], 1, 1)
    for i, h in enumerate(places):
        rows = slice(i * width, (i + 1) * width)
        weights = jnp.exp2(cum[h : h + 1] - columns[:, h : h + 1] + bias)
        mix = (gt * weights).astype(BF16)
        xh = x_ref[rows]
        xf = xh.astype(F32)
        y_ref[rows] = mm(xh, mix, 1, 0) + y_ref[rows] * reach[h : h + 1] + skip_ref[h, 0] * xf
        xs = (xf * tail[h : h + 1]).astype(BF16)
        state[rows] = state[rows] * kept[h : h + 1] + mm(xs, b_ref[...], 1, 0)


def scan_bwd_kernel(
    places, width,
    x_ref, dy_ref, y_ref, dt_ref, a_ref, seg_ref, b_ref, c_ref,
    st_ref, rin_ref, skip_ref,
    dx_ref, db_ref, dc_ref, xdx_ref, da_ref,
    adjoint, xs_all, ds_all, rows_v, rows_c, rows_r, rows_e,
):
    @pl.when(pl.program_id(0) == 0)
    def _():
        adjoint[...] = rin_ref[...].astype(F32)

    cum, columns, reach, tail, kept, bias = block_terms(
        dt_ref[...], a_ref[...], seg_ref, pl.num_programs(0) - 1 - pl.program_id(0)
    )
    bk, ck = b_ref[...], c_ref[...]
    gt = mm(bk, ck, 1, 1)
    r_low = adjoint[...].astype(BF16)
    s_low = st_ref[0]
    dx_ref[...] = mm(r_low, bk, 1, 1)
    dg = jnp.zeros(gt.shape, F32)
    for i, h in enumerate(places):
        rows = slice(i * width, (i + 1) * width)
        weights = jnp.exp2(cum[h : h + 1] - columns[:, h : h + 1] + bias)
        mix = (gt * weights).astype(BF16)
        xh, dyh = x_ref[rows], dy_ref[rows]
        xf, dyf = xh.astype(F32), dyh.astype(F32)
        pairs = mm(xh, dyh, 0, 0)
        dg = dg + weights * pairs
        inner = mm(dyh, mix, 1, 1)
        outer = dx_ref[rows] * tail[h : h + 1]
        skip = skip_ref[h, 0]
        rows_v[h : h + 1] = jnp.sum(xf * outer, axis=0, keepdims=True)
        rows_c[h : h + 1] = jnp.sum(xf * inner, axis=0, keepdims=True)
        rows_r[h : h + 1] = jnp.sum(dyf * (y_ref[rows] - skip * xf), axis=0, keepdims=True)
        dx_ref[rows] = inner + outer + skip * dyf
        xs_all[rows] = (xf * tail[h : h + 1]).astype(BF16)
        ds = (dyf * reach[h : h + 1]).astype(BF16)
        ds_all[rows] = ds
        carried = adjoint[rows] * kept[h : h + 1]
        rows_e[h : h + 1] = jnp.sum(carried * s_low[rows].astype(F32), axis=0, keepdims=True)
        adjoint[rows] = carried + mm(ds, ck, 1, 0)
    dgl = dg.astype(BF16)
    db_ref[...] = mm(xs_all[...], r_low, 0, 0) + mm(dgl, ck, 1, 0)
    dc_ref[...] = mm(ds_all[...], s_low, 0, 0) + mm(dgl, bk, 0, 0)
    v, c = rows_v[...], rows_c[...]
    xdx_ref[...] = v + c
    ends = jnp.sum(rows_e[...], axis=1, keepdims=True)
    da_ref[...] = lane_cumsum(rows_r[...] - c, True) + (lane_cumsum(v) - v) + ends


def scan_specs(inner, heads, state, nb, flip):
    def at(b):
        return nb - 1 - b if flip else b

    lanes = pl.BlockSpec((inner, QB), lambda b: (0, at(b)))
    per_head = pl.BlockSpec((heads, QB), lambda b: (0, at(b)))
    seg = pl.BlockSpec((8, LH + nb * QB), lambda b: (0, 0))
    nat = pl.BlockSpec((QB, state), lambda b: (at(b), 0))
    full = pl.BlockSpec((inner, state), lambda b: (0, 0))
    skip = pl.BlockSpec(memory_space=pltpu.SMEM)
    st = pl.BlockSpec((1, inner, state), lambda b: (at(b), 0, 0))
    return lanes, per_head, seg, nat, full, skip, st


def scan_forward(places, x, dt, a2, seg, bm, cm, sin, skip):
    heads, tokens = dt.shape
    inner, state = x.shape[0], bm.shape[1]
    nb = tokens // QB
    lanes, per_head, sg, nat, full, sk, st = scan_specs(inner, heads, state, nb, False)
    return pl.pallas_call(
        functools.partial(scan_fwd_kernel, places, inner // len(places)),
        grid=(nb,),
        in_specs=[lanes, per_head, per_head, sg, nat, nat, full, sk],
        out_specs=[lanes, st],
        out_shape=[
            jax.ShapeDtypeStruct((inner, tokens), F32),
            jax.ShapeDtypeStruct((nb, inner, state), BF16),
        ],
        scratch_shapes=[pltpu.VMEM((inner, state), F32)],
        compiler_params=params(),
        cost_estimate=pl.CostEstimate(
            flops=20 * inner * tokens * state, transcendentals=0, bytes_accessed=10 * x.size
        ),
    )(x, dt, a2, seg, bm, cm, sin, skip)


def scan_backward(places, x, dy, y, dt, a2, seg, bm, cm, st_in, rin, skip):
    heads, tokens = dt.shape
    inner, state = x.shape[0], bm.shape[1]
    nb = tokens // QB
    lanes, per_head, sg, nat, full, sk, st = scan_specs(inner, heads, state, nb, True)
    return pl.pallas_call(
        functools.partial(scan_bwd_kernel, places, inner // len(places)),
        grid=(nb,),
        in_specs=[lanes, lanes, lanes, per_head, per_head, sg, nat, nat, st, full, sk],
        out_specs=[lanes, nat, nat, per_head, per_head],
        out_shape=[
            jax.ShapeDtypeStruct((inner, tokens), F32),
            jax.ShapeDtypeStruct((tokens, state), F32),
            jax.ShapeDtypeStruct((tokens, state), F32),
            jax.ShapeDtypeStruct((heads, tokens), F32),
            jax.ShapeDtypeStruct((heads, tokens), F32),
        ],
        scratch_shapes=[
            pltpu.VMEM((inner, state), F32),
            pltpu.VMEM((inner, QB), BF16),
            pltpu.VMEM((inner, QB), BF16),
            pltpu.VMEM((heads, QB), F32),
            pltpu.VMEM((heads, QB), F32),
            pltpu.VMEM((heads, QB), F32),
            pltpu.VMEM((heads, state), F32),
        ],
        compiler_params=params(),
        cost_estimate=pl.CostEstimate(
            flops=60 * inner * tokens * state, transcendentals=0, bytes_accessed=16 * x.size
        ),
    )(x, dy, y, dt, a2, seg, bm, cm, st_in, rin, skip)

def gather_kernel(
    ndp, nz, sc, hs, hw,
    x_ref, cot_ref, wv_in, wg_in, wo_in,
    states_ref, stepw_ref, cv_ref, cvb_ref, gg1_ref, heads_ref, cs_ref, csb_ref, gain_ref, len_ref,
    gv_ref, gs_ref, gg_ref, go_ref, pars_ref, nt_ref, ct_ref, vpre_ref, gpre_ref, vt_ref, st_ref, bc_ref,
    seg_ref, match_ref, ahead_ref, v_ref, dt_ref, a_ref, scale_ref, rates_ref, whole_ref, sin_ref,
    xbuf, nt, cbuf, ct, wv_ref, wg_ref, wo_ref, ws_ref, small_own, small_sib, par_ref, wvm, wsm, pvm, cols,
    scols, shifts, spre, st_low, vpre, gpre, vt,
    scaled, tails, fresh, hop_out, hop_in,
    z_send, full_recv, near_send, far_send, far_recv, misc_send, misc_recv, par_send, par_recv, local, load, out_sem,
    hop_send, hop_recv,
):
    nh, lo = 2 * nz, ndp // 2
    n, width = x_ref.shape
    tokens = 2 * n
    r, c = wv_in.shape
    dp, head = lax.axis_index("dp"), lax.axis_index("head")
    core, zed = lax.rem(head, 2), lax.div(head, 2)
    dhi, dlo = lax.div(dp, lo), lax.rem(dp, lo)
    sib = zed * 2 + 1 - core
    hi_peer = (1 - dhi) * lo + dlo
    lo_slots = [lax.rem(dlo + k, lo) for k in range(1, lo)]
    lo_peers = [dhi * lo + s for s in lo_slots]

    def half(rows, i):
        return pl.ds(0, rows // 32 * 16) if i == 0 else pl.ds(rows // 32 * 16, rows - rows // 32 * 16)

    order = [1] + [nz - 1] * (nz > 2) + list(range(2, nz - 1))

    barrier = pltpu.get_barrier_semaphore()
    partners = [(dp, lax.rem(head + k, nh)) for k in range(1, nh)]
    partners += [(p, head) for p in lo_peers + [hi_peer]]
    for partner in partners:
        pl.semaphore_signal(barrier, inc=1, device_id=partner, device_id_type=MESH)
    pl.semaphore_wait(barrier, len(partners))

    def remote(src, dst, send, recv, device):
        pltpu.make_async_remote_copy(
            src_ref=src, dst_ref=dst, send_sem=send, recv_sem=recv, device_id=device, device_id_type=MESH
        ).start()

    def wait_for(ref, sem):
        pltpu.make_async_copy(ref, ref, sem).wait()

    def along_z(m, own, slot):
        for k in range(1, nz):
            remote(
                own, slot, z_send.at[m, k], full_recv.at[m, dp, zed], (dp, lax.rem(zed + k, nz) * 2 + core)
            )

    def near(m, slots, zi, own=None):
        z = lax.rem(zed + zi, nz)
        if own is None:
            wait_for(slots.at[dp, z], full_recv.at[m, dp, z])
        src = slots.at[dp, z] if own is None else own
        for i, p in enumerate(lo_peers + [hi_peer]):
            remote(src, slots.at[dp, z], near_send.at[m, zi, i], full_recv.at[m, dp, z], (p, head))

    def far(m, slots, zi):
        z = lax.rem(zed + zi, nz)
        wait_for(slots.at[hi_peer, z], full_recv.at[m, hi_peer, z])
        for i, p in enumerate(lo_peers):
            part = slots.at[hi_peer, z, half(slots.shape[2], 0)]
            remote(part, part, far_send.at[m, zi, i], far_recv.at[m, hi_peer, z, 0], (p, head))
        for i, d in enumerate(lo_peers):
            wait_for(slots.at[d, z], full_recv.at[m, d, z])
            part = slots.at[d, z, half(slots.shape[2], 1)]
            remote(part, part, far_send.at[m, zi, lo - 1 + i], far_recv.at[m, d, z, 1], (hi_peer, head))

    def fetch(m, slots, vm, z):
        for s in lo_slots:
            d = (1 - dhi) * lo + s
            for i in range(2):
                wait_for(slots.at[d, z, half(slots.shape[2], i)], far_recv.at[m, d, z, i])
        for d in range(ndp):
            pltpu.make_async_copy(slots.at[d, z], vm.at[z, d], load.at[m, z, d]).start()

    def fetched(m, slots, vm, z):
        for d in range(ndp):
            pltpu.make_async_copy(slots.at[d, z], vm.at[z, d], load.at[m, z, d]).wait()

    def lanes(v, before):
        parts = [jnp.zeros((v.shape[0], before), F32)] * (before > 0) + [v.astype(F32)]
        return jnp.concatenate(parts + [jnp.zeros((v.shape[0], 128 - before - v.shape[1]), F32)], axis=1)

    wv_ref[...] = wv_in[...].T
    along_z(0, wv_ref, gv_ref.at[dp, zed])
    near(0, gv_ref, 0, wv_ref)
    small_t = pltpu.roll(lanes(states_ref[...], 0), core * sc, 1) + lanes(stepw_ref[...], 2 * sc)
    ws_ref[...] = small_t.T[0 : ws_ref.shape[0]].astype(BF16)
    remote(ws_ref, small_sib, misc_send.at[0], misc_recv.at[0], (dp, sib))
    own_rows = pl.ds(HALO + core * n, n)
    remote(x_ref, xbuf.at[own_rows], misc_send.at[1], misc_recv.at[1], (dp, sib))

    @pl.when((core == 1) & (zed < nz - 1))
    def _():
        for i in range(2):
            remote(
                x_ref.at[pl.ds(n - HALO, HALO)], xbuf.at[pl.ds(0, HALO)], misc_send.at[3 + i], misc_recv.at[3],
                (dp, (zed + 1) * 2 + i),
            )

    wg_ref[...] = wg_in[...].T
    wo_ref[...] = wo_in[...].T
    mine = [
        pltpu.make_async_copy(x_ref, xbuf.at[own_rows], local.at[0]),
        pltpu.make_async_copy(wv_ref, gv_ref.at[dp, zed], local.at[1]),
        pltpu.make_async_copy(wg_ref, gg_ref.at[dp, zed], local.at[2]),
        pltpu.make_async_copy(cot_ref, cbuf.at[pl.ds(core * n, n)], local.at[3]),
        pltpu.make_async_copy(wo_ref, go_ref.at[dp, zed], local.at[4]),
    ]
    for copy in mine:
        copy.start()

    wait_for(small_sib, misc_recv.at[0])
    line = lax.broadcasted_iota(jnp.int32, small_own.shape, 0)
    low_line = (1 - core) * sc
    theirs = (line >= low_line) & (line < low_line + sc)
    small_own[...] = jnp.where(
        theirs, small_sib[...].astype(F32), ws_ref[...].astype(F32)
    ).astype(BF16)
    along_z(1, small_own, gs_ref.at[dp, zed])
    near(1, gs_ref, 0, small_own)
    own_small = pltpu.make_async_copy(small_own, gs_ref.at[dp, zed], local.at[7])
    own_small.start()
    par_ref[...] = jnp.zeros(par_ref.shape, F32)
    par_ref[0:4] = cv_ref[...]
    par_ref[4:5] = cvb_ref[...]
    par_ref[5:6] = gg1_ref[...]
    par_ref[6:9, 0:128] = lanes(heads_ref[...], 0)
    par_ref[9:13, 0:128] = pltpu.roll(lanes(cs_ref[...], 0), core * sc, 1)
    par_ref[13:14, 0:128] = pltpu.roll(lanes(csb_ref[...], 0), core * sc, 1)
    own_par = pltpu.make_async_copy(par_ref, pars_ref.at[head], local.at[5])
    own_par.start()
    for k in range(1, nh):
        remote(par_ref, pars_ref.at[head], par_send.at[k], par_recv.at[head], (dp, lax.rem(head + k, nh)))
    remote(cot_ref, cbuf.at[pl.ds(core * n, n)], misc_send.at[2], misc_recv.at[2], (dp, sib))

    span = LH + tokens
    ends = [len_ref[0, 0]]
    for k in range(1, len_ref.shape[1]):
        ends.append(ends[-1] + len_ref[0, k])

    def segment(at):
        number = sum([(at >= end).astype(F32) for end in ends[1:]], (at >= ends[0]).astype(F32))
        return jnp.where((at < 0) | (at >= nz * tokens), -1.0, number)

    at = zed * tokens - LH + lax.broadcasted_iota(jnp.int32, (8, span), 1)
    tap = lax.broadcasted_iota(jnp.int32, (8, span), 0)
    number = segment(at)
    seg_ref[...] = number
    valid = (tap < 4) & (at >= zed * tokens)
    match_ref[...] = jnp.where(valid & (segment(at - 3 + tap) == number), 1.0, 0.0)
    ahead_ref[...] = jnp.where((tap < 4) & (segment(at + 3 - tap) == number), 1.0, 0.0)[:, LH:]

    def normalise(start, count):
        rows = xbuf[pl.ds(start, count), :].astype(F32)
        inverse = lax.rsqrt(jnp.mean(rows * rows, axis=1, keepdims=True) + EPSILON)
        return (rows * inverse * gain_ref[...]).astype(BF16)

    def normalise_half(which):
        @pl.loop(0, n // 128)
        def _(i):
            at = pl.multiple_of(which * n + i * 128, 128)
            nt[:, pl.ds(pl.multiple_of(LH + at, 128), 128)] = normalise(pl.multiple_of(HALO + at, 16), 128).T

    def turn(which):
        @pl.loop(0, n // 128)
        def _(i):
            at = pl.multiple_of(which * n + i * 128, 128)
            ct[:, pl.ds(at, 128)] = cbuf[pl.ds(at, 128), :].T

    mine[0].wait()
    normalise_half(core)
    near(0, gv_ref, order[0])
    wait_for(x_ref, misc_recv.at[1])
    normalise_half(1 - core)
    for zi in order[1:]:
        near(0, gv_ref, zi)
    along_z(2, wg_ref, gg_ref.at[dp, zed])
    for zi in order:
        near(1, gs_ref, zi)

    @pl.when(zed > 0)
    def _():
        wait_for(xbuf.at[pl.ds(0, HALO)], misc_recv.at[3])

    @pl.when(zed == 0)
    def _():
        xbuf[0:HALO, :] = jnp.zeros((HALO, width), BF16)

    before = normalise(0, HALO).astype(F32)
    nt[:, 0:LH] = jnp.concatenate([jnp.zeros((LH - HALO, width), F32), before], axis=0).astype(BF16).T
    out_nt = pltpu.make_async_copy(nt.at[:, pl.ds(LH, tokens)], nt_ref, out_sem.at[3 * nz])
    out_nt.start()
    far(0, gv_ref, 0)
    far(1, gs_ref, 0)
    mine[3].wait()
    turn(core)
    for zi in order:
        far(0, gv_ref, zi)
        far(1, gs_ref, zi)
    near(2, gg_ref, 0, wg_ref)

    for k in range(1, nh):
        other = lax.rem(head + k, nh)
        wait_for(pars_ref.at[other], par_recv.at[other])
    own_par.wait()
    get_pars = pltpu.make_async_copy(pars_ref, pvm, local.at[5])
    get_pars.start()
    wait_for(cot_ref, misc_recv.at[2])
    turn(1 - core)
    get_pars.wait()
    out_ct = pltpu.make_async_copy(ct, ct_ref, out_sem.at[3 * nz + 1])
    out_ct.start()

    own_small.wait()
    mine[1].wait()
    for z in range(nz):
        fetch(1, gs_ref, wsm, z)
    for z in range(nz):
        fetch(0, gv_ref, wvm, z)
    place = lax.broadcasted_iota(jnp.int32, (256, 128), 0) - lax.broadcasted_iota(jnp.int32, (256, 128), 1)

    @pl.loop(0, tokens // 128)
    def _(b):
        at = pl.ds(pl.multiple_of(LH + b * 128, 128), 128)
        for k in range(3):
            shifts[b, :, k * 128 : k * 128 + 128] = jnp.where(
                place == 125 + k, match_ref[k : k + 1, at], 0.0
            ).astype(BF16)

    lanes_chunk = chunk_of(span, 384, 128)

    def by_width(weights, z):
        return jnp.concatenate([weights[z, d] for d in range(ndp)], axis=1)

    def shift(source, count, rest=None):
        @pl.loop(0, tokens // 128)
        def _(b):
            wide = pl.ds(pl.multiple_of(b * 128, 128), 256)
            moved = mm(source[:, wide], shifts[b], 1, 0)
            if rest is not None:
                moved = moved + mm(rest[:, wide], shifts[b], 1, 0)
            for k in range(3):
                gpre[k, 0:count, pl.ds(pl.multiple_of(b * 128, 128), 128)] = moved[:, k * 128 : k * 128 + 128]

    def convolved(source, taps, rows, base, rest=None):
        at = pl.ds(base, 256)
        here = source[rows, pl.ds(LH + base, 256)].astype(F32)
        if rest is not None:
            here = here + rest[rows, pl.ds(LH + base, 256)].astype(F32)
        pre = taps[:, 3:4] * here + taps[:, 4:5]
        for k in range(3):
            pre = pre + taps[:, k : k + 1] * gpre[k, rows, at]
        return pre * sigmoid(pre)

    for z in range(nz):
        fetched(1, gs_ref, wsm, z)

    @pl.loop(0, span // lanes_chunk)
    def _(i):
        at = pl.ds(pl.multiple_of(i * lanes_chunk, 128), lanes_chunk)
        left = jnp.concatenate([by_width(wsm, z) for z in range(nz)], axis=0)
        spre[:, at] = mm(left, nt[:, at], 1, 0)

    sr = wsm.shape[2]
    for z in range(nz):
        part = slice(z * 2 * sc, (z + 1) * 2 * sc)
        here = spre[z * sr : z * sr + 2 * sc, :]
        high = here.astype(BF16)
        st_ref[part, :] = high
        st_low[part, :] = (here - high.astype(F32)).astype(BF16)
        v_ref[z * 8 : z * 8 + 8, :] = spre[z * sr + 2 * sc : z * sr + 2 * sc + 8, LH:]
        both = pvm[2 * z, 8:16, 0:128] + pvm[2 * z + 1, 8:16, 0:128]
        scols[part, :] = both.T[0 : 2 * sc, 1:6]
    bc_rows = 2 * sc * nz
    shift(st_ref, bc_rows, st_low)

    @pl.loop(0, bc_rows // 32, unroll=2)
    def _(g):
        rows = pl.ds(pl.multiple_of(g * 32, 32), 32)
        taps = scols[rows, :]
        for base in range(0, tokens, 256):
            scaled[rows, pl.ds(base, 256)] = convolved(st_ref, taps, rows, base, st_low).astype(BF16)

    @pl.loop(0, tokens // 128)
    def _(b):
        at = pl.ds(pl.multiple_of(b * 128, 128), 128)
        for i in range(2):
            bc_ref[i, at, :] = scaled[i * 128 : i * 128 + 128, at].T

    columns = [pvm[2 * z + core, 0:16, 0:128].T[0:8] for z in range(nz)]

    def column(k):
        return jnp.concatenate([v[:, k : k + 1] for v in columns], axis=0)

    v = v_ref[...] + column(6)
    v_ref[...] = v
    dt = jnp.maximum(v, 0.0) + jnp.log1p(jnp.exp(-jnp.abs(v)))
    dt_ref[...] = dt
    rates = -jnp.exp(column(7))
    rates_ref[...] = jnp.broadcast_to(rates, rates_ref.shape)
    a2 = dt * (rates * LOG2E)
    a_ref[...] = a2
    segr = seg_ref[0:1, LH:]
    last, first = segr[:, tokens - 1 :], seg_ref[0:1, LH - 1 : LH]
    before = lane_cumsum(a2)
    through = before[:, tokens - 1 :]
    scale_ref[...] = jnp.where(segr == first, jnp.exp2(before), 0.0)
    whole_ref[...] = jnp.broadcast_to(jnp.where(last == first, jnp.exp2(through), 0.0), whole_ref.shape)
    tail = jnp.where(segr == last, jnp.exp2(lane_cumsum(a2, True) - a2) * dt, 0.0)
    tails[...] = tail

    for z in range(nz):
        fetched(0, gv_ref, wvm, z)

    @pl.loop(0, nz)
    def _(z):
        cols[...] = pvm[2 * z + core, 0:8, :].T

        @pl.loop(0, span // lanes_chunk)
        def _(i):
            at = pl.ds(pl.multiple_of(i * lanes_chunk, 128), lanes_chunk)
            vpre[z, :, at] = mm(by_width(wvm, z), nt[:, at], 1, 0).astype(BF16)

        pltpu.make_async_copy(vpre.at[z], vpre_ref.at[z], out_sem.at[z]).start()
        shift(vpre.at[z], c)

        @pl.loop(0, c // 32, unroll=2)
        def _(g):
            rows = pl.ds(pl.multiple_of(g * 32, 32), 32)
            taps = cols[rows, :]
            decay = pl.ds(z * 8 + g // (hw // 32), 1)
            for base in range(0, tokens, 256):
                at = pl.ds(base, 256)
                low = convolved(vpre.at[z], taps, rows, base).astype(BF16)
                vt[z, rows, at] = low
                scaled[rows, at] = (low.astype(F32) * tails[decay, at]).astype(BF16)

        pltpu.make_async_copy(vt.at[z], vt_ref.at[z], out_sem.at[nz + z]).start()
        fresh[z] = mm(scaled[0:c, :], bc_ref[0], 1, 0)

        @pl.when(z < nz - 1)
        def _():
            near(2, gg_ref, z + 1)

        @pl.when(z > 0)
        def _():
            far(2, gg_ref, z - 1)

        @pl.when(z == 1)
        def _():
            along_z(3, wo_ref, go_ref.at[dp, zed])

    far(2, gg_ref, nz - 1)

    mine[2].wait()
    near(3, go_ref, 0, wo_ref)
    for z in range(nz):
        fetch(2, gg_ref, wvm, z)
    gate_chunk = chunk_of(tokens, 512, 128)

    def hop(i):
        if i:
            hop_arrived(i - 1)
            for z in range(nz):
                for h in range(hs):
                    at = slice(h * hw, (h + 1) * hw)
                    state = whole_ref[z * 8 + h : z * 8 + h + 1, :] * hop_in[i - 1, z, at, :].astype(F32)
                    hop_out[i, z, at, :] = (fresh[z, at, :] + state).astype(BF16)
        else:
            hop_out[0] = fresh[...].astype(BF16)

        @pl.when(zed < nz - 1)
        def _():
            remote(hop_out.at[i], hop_in.at[i], hop_send.at[i], hop_recv.at[i], (dp, (zed + 1) * 2 + core))

    def hop_arrived(i):
        @pl.when(zed > 0)
        def _():
            wait_for(hop_in.at[i], hop_recv.at[i])

        @pl.when(zed == 0)
        def _():
            hop_in[i] = jnp.zeros(hop_in.shape[1:], BF16)

    hops = nz // 2
    for i in range(hops):
        hop(i)
        if i == 0:
            for zi in order:
                near(3, go_ref, zi)
        for z in (2 * i, 2 * i + 1):
            fetched(2, gg_ref, wvm, z)

        @pl.loop(2 * i, 2 * i + 2)
        def _(z):
            @pl.loop(0, tokens // gate_chunk)
            def _(i):
                at = pl.multiple_of(i * gate_chunk, 128)
                right = nt[:, pl.ds(pl.multiple_of(LH + at, 128), gate_chunk)]
                gpre[z, 0:c, pl.ds(at, gate_chunk)] = mm(by_width(wvm, z), right, 1, 0)

            pltpu.make_async_copy(gpre.at[z, pl.ds(0, c)], gpre_ref.at[z], out_sem.at[2 * nz + z]).start()

    for zi in [0] + order:
        far(3, go_ref, zi)
    hop_arrived(hops - 1)
    sin_ref[...] = hop_in[hops - 1]

    @pl.when(zed < nz - 1)
    def _():
        for i in range(hops):
            wait_for(hop_out.at[i], hop_send.at[i])

    mine[4].wait()
    for z in range(nz):
        for s in lo_slots:
            d = (1 - dhi) * lo + s
            for i in range(2):
                wait_for(go_ref.at[d, z, half(c, i)], far_recv.at[3, d, z, i])
    sent = [wv_ref, small_own, wg_ref, wo_ref]
    for m in range(4):
        for k in range(1, nz):
            wait_for(sent[m], z_send.at[m, k])
    for m in range(4):
        for zi in range(nz):
            for i in range(lo):
                wait_for(sent[m], near_send.at[m, zi, i])
            for i in range(2 * (lo - 1)):
                wait_for(sent[m].at[half(sent[m].shape[0], i // (lo - 1))], far_send.at[m, zi, i])
    wait_for(ws_ref, misc_send.at[0])
    wait_for(x_ref, misc_send.at[1])
    wait_for(cot_ref, misc_send.at[2])
    for k in range(1, nh):
        wait_for(par_ref, par_send.at[k])

    @pl.when((core == 1) & (zed < nz - 1))
    def _():
        for i in range(2):
            wait_for(x_ref.at[pl.ds(n - HALO, HALO)], misc_send.at[3 + i])

    for z in range(nz):
        pltpu.make_async_copy(vpre.at[z], vpre_ref.at[z], out_sem.at[z]).wait()
        pltpu.make_async_copy(vt.at[z], vt_ref.at[z], out_sem.at[nz + z]).wait()
        pltpu.make_async_copy(gpre.at[z, pl.ds(0, c)], gpre_ref.at[z], out_sem.at[2 * nz + z]).wait()
    out_nt.wait()
    out_ct.wait()


def gather_project(
    ndp, nz, sc, hs, hw, x, cot, wv, wg, wo, states, stepw, cv, cvb, gg, heads, cs, csb, gain, lengths
):
    n, width = x.shape
    tokens = 2 * n
    r, c = wv.shape
    nh, lo, hops = 2 * nz, ndp // 2, nz // 2
    sr, most = 2 * sc + 16, max(c, 2 * sc * nz)
    anywhere = pl.BlockSpec(memory_space=pl.ANY)
    vmem = pl.BlockSpec(memory_space=pltpu.VMEM)
    dma = pltpu.SemaphoreType.DMA
    return pl.pallas_call(
        functools.partial(gather_kernel, ndp, nz, sc, hs, hw),
        in_specs=[anywhere] * 2 + [vmem] * 12 + [pl.BlockSpec(memory_space=pltpu.SMEM)],
        out_specs=[anywhere] * 10 + [vmem] * 12,
        out_shape=[
            shape((ndp, nz, c, r), BF16),
            shape((ndp, nz, sr, r), BF16),
            shape((ndp, nz, c, r), BF16),
            shape((ndp, nz, c, r), BF16),
            shape((nh, 16, c), F32),
            shape((width, tokens), BF16),
            shape((width, tokens), BF16),
            shape((nz, c, LH + tokens), BF16),
            shape((nz, c, tokens), F32),
            shape((nz, c, tokens), BF16),
            shape((2 * sc * nz, LH + tokens), BF16),
            shape((2, tokens, 128), BF16),
            shape((8, LH + tokens), F32),
            shape((8, LH + tokens), F32),
            shape((8, tokens), F32),
            shape((nz * 8, tokens), F32),
            shape((nz * 8, tokens), F32),
            shape((nz * 8, tokens), F32),
            shape((nz * 8, tokens), F32),
            shape((nz * 8, 128), F32),
            shape((nz * 8, 128), F32),
            shape((nz, c, 128), BF16),
        ],
        scratch_shapes=[
            pltpu.VMEM((HALO + tokens, width), BF16),
            pltpu.VMEM((width, LH + tokens), BF16),
            pltpu.VMEM((tokens, width), BF16),
            pltpu.VMEM((width, tokens), BF16),
            pltpu.VMEM((c, r), BF16),
            pltpu.VMEM((c, r), BF16),
            pltpu.VMEM((c, r), BF16),
            pltpu.VMEM((sr, r), BF16),
            pltpu.VMEM((sr, r), BF16),
            pltpu.VMEM((sr, r), BF16),
            pltpu.VMEM((16, c), F32),
            pltpu.VMEM((nz, ndp, c, r), BF16),
            pltpu.VMEM((nz, ndp, sr, r), BF16),
            pltpu.VMEM((nh, 16, c), F32),
            pltpu.VMEM((c, 8), F32),
            pltpu.VMEM((2 * sc * nz, 5), F32),
            pltpu.VMEM((tokens // 128, 256, 384), BF16),
            pltpu.VMEM((nz * sr, LH + tokens), F32),
            pltpu.VMEM((2 * sc * nz, LH + tokens), BF16),
            pltpu.VMEM((nz, c, LH + tokens), BF16),
            pltpu.VMEM((nz, most, tokens), F32),
            pltpu.VMEM((nz, c, tokens), BF16),
            pltpu.VMEM((most, tokens), BF16),
            pltpu.VMEM((nz * 8, tokens), F32),
            pltpu.VMEM((nz, c, 128), F32),
            pltpu.VMEM((hops, nz, c, 128), BF16),
            pltpu.VMEM((hops, nz, c, 128), BF16),
            dma((4, nz)),
            dma((4, ndp, nz)),
            dma((4, nz, lo)),
            dma((4, nz, 2 * (lo - 1))),
            dma((4, ndp, nz, 2)),
            dma((5,)),
            dma((4,)),
            dma((nh,)),
            dma((nh,)),
            dma((8,)),
            dma((3, nz, ndp)),
            dma((3 * nz + 2,)),
            dma((hops,)),
            dma((hops,)),
        ],
        compiler_params=pltpu.CompilerParams(
            collective_id=1, has_side_effects=True, vmem_limit_bytes=60 * MIB
        ),
        cost_estimate=cost(2 * tokens * width * nz * (2 * c + 128), 60 * MIB),
    )(x, cot, wv, wg, wo, states, stepw, cv, cvb, gg, heads, cs, csb, gain, lengths)

def mix_kernel(ndp, wo_ref, ct_ref, y_ref, g_ref, gain_ref, gated_ref, h1_ref, sums_ref, acc, low):
    c, tokens = y_ref.shape
    z = pl.program_id(0)
    chunk = chunk_of(tokens, 512, 128)

    @pl.loop(0, tokens // chunk)
    def _(i):
        at = pl.ds(pl.multiple_of(i * chunk, 128), chunk)
        left = jnp.concatenate([wo_ref[d, 0] for d in range(ndp)], axis=1)
        h1_ref[:, at] = mm(left, ct_ref[:, at], 1, 0)

    @pl.when(z == 0)
    def _():
        acc[...] = jnp.zeros(acc.shape, F32)

    @pl.loop(0, c // 16, unroll=2)
    def _(i):
        rows = pl.ds(pl.multiple_of(i * 16, 16), 16)
        scale = gain_ref[rows, :]
        for at in lane_chunks(tokens):
            g = g_ref[rows, at]
            mixed = y_ref[rows, at] * (g * sigmoid(g))
            gated = (mixed * scale).astype(BF16)
            low[rows, at] = gated
            square = mixed * mixed
            dots = gated.astype(F32) * h1_ref[rows, at]
            acc[0:8, at] += square[0:8] + square[8:16]
            acc[8:16, at] += dots[0:8] + dots[8:16]

    gated_ref[0] = low[...].T

    @pl.when(z == pl.num_programs(0) - 1)
    def _():
        sums_ref[0:1] = jnp.sum(acc[0:8], axis=0, keepdims=True)
        sums_ref[1:2] = jnp.sum(acc[8:16], axis=0, keepdims=True)
        sums_ref[2:8] = jnp.zeros((6, tokens), F32)


def mix(wo, ct, y, g, gain):
    ndp, nz, c, r = wo.shape
    width, tokens = ct.shape
    inner = nz * c
    block = pl.BlockSpec((c, tokens), lambda z: (z, 0))
    return pl.pallas_call(
        functools.partial(mix_kernel, ndp),
        grid=(nz,),
        in_specs=[
            pl.BlockSpec((ndp, 1, c, r), lambda z: (0, z, 0, 0)),
            pl.BlockSpec((width, tokens), lambda z: (0, 0)),
            block, block,
            pl.BlockSpec((c, 1), lambda z: (z, 0)),
        ],
        out_specs=[
            pl.BlockSpec((1, tokens, c), lambda z: (z, 0, 0)), block, pl.BlockSpec((8, tokens), lambda z: (0, 0)),
        ],
        out_shape=[shape((nz, tokens, c), BF16), shape((inner, tokens), F32), shape((8, tokens), F32)],
        scratch_shapes=[pltpu.VMEM((16, tokens), F32), pltpu.VMEM((c, tokens), BF16)],
        compiler_params=params(),
        cost_estimate=cost(2 * inner * tokens * width, 22 * inner * tokens),
    )(wo, ct, y, g, gain)


def unmix_kernel(
    ndp, nz, hs, hw, total,
    y_ref, g_ref, h1_ref, x_ref, gain_ref, sums_ref, scale_ref, cm_ref, whole_ref, nt_ref,
    dy_ref, gl_ref, cols_ref, grad_ref, rin_ref,
    scaled, acc, low, turned, back, hop_out, hop_in, hop_send, hop_recv,
):
    c = y_ref.shape[0]
    hops = nz // 2
    step = pl.program_id(0)
    dp, head = lax.axis_index("dp"), lax.axis_index("head")
    core, zed = lax.rem(head, 2), lax.div(head, 2)

    @pl.when(step == 0)
    def _():
        barrier = pltpu.get_barrier_semaphore()
        for k in range(1, nz):
            pl.semaphore_signal(
                barrier, inc=1, device_id=(dp, lax.rem(zed + k, nz) * 2 + core), device_id_type=MESH
            )
        pl.semaphore_wait(barrier, nz - 1)

    @pl.when(step < nz)
    def _():
        inverse = lax.rsqrt(sums_ref[0:1] / total + EPSILON)
        weight = sums_ref[1:2] * (inverse * inverse * inverse) / total

        @pl.loop(0, c // 16, unroll=2)
        def _(i):
            rows = pl.ds(pl.multiple_of(i * 16, 16), 16)
            gain = gain_ref[rows, :]
            head_row = pl.ds(i // (hw // 16), 1)
            gains, skips = [], []
            for at in lane_chunks(y_ref.shape[1]):
                y, g = y_ref[rows, at], g_ref[rows, at]
                sig = sigmoid(g)
                silu = g * sig
                mixed = y * silu
                gated_grad = h1_ref[rows, at] * inverse[:, at]
                mixed_grad = gated_grad * gain - weight[:, at] * mixed
                dy = (mixed_grad * silu).astype(BF16)
                dy_ref[rows, at] = dy
                low[rows, at] = (mixed_grad * y * (sig + silu * (1.0 - sig))).astype(BF16)
                dyf = dy.astype(F32)
                scaled[rows, at] = (dyf * scale_ref[head_row, at]).astype(BF16)
                gains.append(folded(gated_grad * mixed))
                skips.append(folded(dyf * x_ref[rows, at].astype(F32)))
            acc[0, rows, :] = sum(gains[1:], gains[0])
            acc[1, rows, :] = sum(skips[1:], skips[0])

        for k in range(2):
            cols_ref[0, k : k + 1] = jnp.sum(acc[k].T, axis=0, keepdims=True)
        cols_ref[0, 2:8] = jnp.zeros((6, c), F32)
        flipped = low[...].T
        gl_ref[0] = flipped
        turned[step] = flipped
        back[step] = mm(scaled[...], cm_ref[...], 1, 0)

    def hop_arrived(i, z):
        @pl.when(zed < nz - 1)
        def _():
            pltpu.make_async_copy(hop_in.at[i, z], hop_in.at[i, z], hop_recv.at[i, z]).wait()

        @pl.when(zed == nz - 1)
        def _():
            hop_in[i, z] = jnp.zeros(hop_in.shape[2:], BF16)

    def hop(i, z):
        if i:
            hop_arrived(i - 1, z)
            for h in range(hs):
                at = slice(h * hw, (h + 1) * hw)
                state = whole_ref[pl.ds(z * 8 + h, 1), :] * hop_in[i - 1, z, at, :].astype(F32)
                hop_out[i, z, at, :] = (back[z, at, :] + state).astype(BF16)
        else:
            hop_out[0, z] = back[z].astype(BF16)

        @pl.when(zed > 0)
        def _():
            pltpu.make_async_remote_copy(
                src_ref=hop_out.at[i, z], dst_ref=hop_in.at[i, z],
                send_sem=hop_send.at[i, z], recv_sem=hop_recv.at[i, z],
                device_id=(dp, (zed - 1) * 2 + core), device_id_type=MESH,
            ).start()

    @pl.when(step >= nz)
    def _():
        r = nt_ref.shape[0] // ndp
        right = turned[step - nz]
        for d in range(ndp):
            grad_ref[d, 0] = mm(nt_ref[d * r : (d + 1) * r, :], right, 1, 0).astype(BF16)

    for i in range(hops):
        @pl.when((step >= 2 * i) & (step < nz + 2 * i))
        def _(i=i):
            hop(i, step - 2 * i)

    @pl.when(step == 2 * nz - 1)
    def _():
        for z in range(nz):
            hop_arrived(hops - 1, z)
        rin_ref[...] = hop_in[hops - 1]

        @pl.when(zed > 0)
        def _():
            for i in range(hops):
                for z in range(nz):
                    pltpu.make_async_copy(hop_out.at[i, z], hop_out.at[i, z], hop_send.at[i, z]).wait()


def unmix(ndp, nz, hs, hw, y, g, h1, x, gain, sums, scale, cm, whole, nt):
    inner, tokens = y.shape
    c = inner // nz
    state = cm.shape[1]
    width = nt.shape[0]
    hops = nz // 2

    def first(s):
        return jnp.minimum(s, nz - 1)

    def second(s):
        return jnp.maximum(s - nz, 0)

    block = pl.BlockSpec((c, tokens), lambda s: (first(s), 0))
    dma = pltpu.SemaphoreType.DMA

    def fixed(v):
        return pl.BlockSpec(v.shape, lambda s: (0,) * v.ndim)

    return pl.pallas_call(
        functools.partial(unmix_kernel, ndp, nz, hs, hw, inner * 2),
        grid=(2 * nz,),
        in_specs=[
            block, block, block, block,
            pl.BlockSpec((c, 1), lambda s: (first(s), 0)),
            fixed(sums),
            pl.BlockSpec((8, tokens), lambda s: (first(s), 0)),
            fixed(cm), fixed(whole), fixed(nt),
        ],
        out_specs=[
            block,
            pl.BlockSpec((1, tokens, c), lambda s: (first(s), 0, 0)),
            pl.BlockSpec((1, 8, c), lambda s: (first(s), 0, 0)),
            pl.BlockSpec((ndp, 1, width // ndp, c), lambda s: (0, second(s), 0, 0)),
            pl.BlockSpec((nz, c, state), lambda s: (0, 0, 0)),
        ],
        out_shape=[
            shape((inner, tokens), BF16), shape((nz, tokens, c), BF16), shape((nz, 8, c), F32),
            shape((ndp, nz, width // ndp, c), BF16), shape((nz, c, state), BF16),
        ],
        scratch_shapes=[
            pltpu.VMEM((c, tokens), BF16), pltpu.VMEM((2, c, 128), F32), pltpu.VMEM((c, tokens), BF16),
            pltpu.VMEM((nz, tokens, c), BF16), pltpu.VMEM((nz, c, state), F32),
            pltpu.VMEM((hops, nz, c, state), BF16), pltpu.VMEM((hops, nz, c, state), BF16),
            dma((hops, nz)), dma((hops, nz)),
        ],
        compiler_params=pltpu.CompilerParams(
            collective_id=4, has_side_effects=True, vmem_limit_bytes=56 * MIB
        ),
        cost_estimate=cost(2 * inner * tokens * (state + width), 28 * inner * tokens),
    )(y, g, h1, x, gain, sums, scale, cm, whole, nt)


def weight_grad_kernel(ndp, total, *refs):
    left_ref, right_ref = refs[0], refs[1]
    r = left_ref.shape[0] // ndp
    if total:
        sums_ref, out_ref, left = refs[2:]

        @pl.when(pl.program_id(0) == 0)
        def _():
            inverse = lax.rsqrt(sums_ref[0:1] / total + EPSILON)

            @pl.loop(0, left.shape[0] // 64)
            def _(i):
                rows = pl.ds(pl.multiple_of(i * 64, 64), 64)
                left[rows, :] = (left_ref[rows, :].astype(F32) * inverse).astype(BF16)
    else:
        out_ref, left = refs[2], left_ref
    for d in range(ndp):
        out_ref[d, 0] = mm(left[d * r : (d + 1) * r, :], right_ref[0], 1, 0).astype(BF16)


def weight_grad(ndp, left, right, sums=None):
    width, tokens = left.shape
    nz, _, c = right.shape
    r, inner = width // ndp, nz * c
    operands = [left, right]
    specs = [pl.BlockSpec((width, tokens), lambda z: (0, 0)), pl.BlockSpec((1, tokens, c), lambda z: (z, 0, 0))]
    scratch = []
    if sums is not None:
        operands.append(sums)
        specs.append(pl.BlockSpec((8, tokens), lambda z: (0, 0)))
        scratch = [pltpu.VMEM((width, tokens), BF16)]
    return pl.pallas_call(
        functools.partial(weight_grad_kernel, ndp, 0 if sums is None else inner * 2),
        grid=(nz,),
        in_specs=specs,
        out_specs=pl.BlockSpec((ndp, 1, r, c), lambda z: (0, z, 0, 0)),
        out_shape=shape((ndp, nz, r, c), BF16),
        scratch_shapes=scratch,
        compiler_params=params(),
        cost_estimate=cost(2 * inner * tokens * width, 8 * inner * tokens),
    )(*operands)


def back_project_kernel(nz, n, weight_ref, right_ref, keep_ref, send_ref):
    core = lax.rem(lax.axis_index("head"), 2)
    weight = jnp.concatenate([weight_ref[0, z] for z in range(nz)], axis=0)

    def product(which):
        at = pl.ds(pl.multiple_of(which * n, 128), n)
        return mm(jnp.concatenate([right_ref[z, at, :] for z in range(nz)], axis=1), weight, 1, 0)

    send_ref[0] = product(1 - core).astype(BF16)
    keep_ref[0] = product(core)


def back_project(weight, right):
    ndp, nz, c, r = weight.shape
    tokens = right.shape[1]
    n = tokens // 2
    return pl.pallas_call(
        functools.partial(back_project_kernel, nz, n),
        grid=(ndp,),
        in_specs=[
            pl.BlockSpec((1, nz, c, r), lambda d: (d, 0, 0, 0)),
            pl.BlockSpec(right.shape, lambda d: (0, 0, 0)),
        ],
        out_specs=[pl.BlockSpec((1, n, r), lambda d: (d, 0, 0))] * 2,
        out_shape=[shape((ndp, n, r), F32), shape((ndp, n, r), BF16)],
        compiler_params=params(),
        cost_estimate=cost(2 * weight.size * tokens, 2 * right.size),
    )(weight, right)


def result_kernel(total, keep_ref, got_ref, sums_ref, x_ref, out_ref):
    inverse = lax.rsqrt(sums_ref[...].T[:, 0:1] / total + EPSILON)
    blocks = [keep_ref[d] + got_ref[d].astype(F32) for d in range(keep_ref.shape[0])]
    branch = jnp.concatenate(blocks, axis=1)
    out_ref[...] = (x_ref[...].astype(F32) + branch * inverse).astype(BF16)


def result(total, keep, got, sums, x):
    n, width = x.shape
    ndp, _, r = keep.shape
    blocks = pl.BlockSpec((ndp, 128, r), lambda i: (0, i, 0))
    rows = pl.BlockSpec((128, width), lambda i: (i, 0))
    return pl.pallas_call(
        functools.partial(result_kernel, total),
        grid=(n // 128,),
        in_specs=[blocks, blocks, pl.BlockSpec((8, 128), lambda i: (0, i)), rows],
        out_specs=rows,
        out_shape=shape((n, width), BF16),
        compiler_params=params(),
        cost_estimate=cost(0, 12 * n * width),
    )(keep, got, sums, x)


def conv_back_kernel(
    nz, sc,
    dx_hbm, p_hbm, db_hbm, dc_hbm, st_hbm,
    pars, match, ahead, v_ref, dt_ref, xdx_ref, da_ref, rates_ref, mix_ref,
    vl, small_t, table_ref,
    st, dstates, e, p, cols, scols, shifts, moved, acc, queue, squeue, heads, halo, sheads, shalo, turn, slanes,
    load, e_load, ds_send, ds_recv, halo_send, halo_recv,
):
    nh = 2 * nz
    _, c, wide = queue.shape
    tokens = wide - 128
    sr = 2 * sc + 16
    dp, head = lax.axis_index("dp"), lax.axis_index("head")
    core, zed = lax.rem(head, 2), lax.div(head, 2)

    def column_loads(z):
        at = pl.ds(pl.multiple_of(z * c, 16), c)
        return [
            pltpu.make_async_copy(dx_hbm.at[at], e.at[pl.ds(0, c)], e_load.at[0]),
            pltpu.make_async_copy(p_hbm.at[at], p, e_load.at[1]),
        ]

    for copy in column_loads(0):
        copy.start()
    loads = [
        pltpu.make_async_copy(a, b, load.at[i])
        for i, (a, b) in enumerate([(st_hbm, st), (db_hbm, dstates.at[0]), (dc_hbm, dstates.at[1])])
    ]
    for copy in loads:
        copy.start()

    barrier = pltpu.get_barrier_semaphore()
    for k in range(1, nh):
        pl.semaphore_signal(barrier, inc=1, device_id=(dp, lax.rem(head + k, nh)), device_id_type=MESH)
    pl.semaphore_wait(barrier, nh - 1)

    def remote(src, dst, send_sem, recv_sem, device):
        pltpu.make_async_remote_copy(
            src_ref=src, dst_ref=dst, send_sem=send_sem, recv_sem=recv_sem, device_id=device, device_id_type=MESH
        ).start()

    def wait_for(ref, sem):
        pltpu.make_async_copy(ref, ref, sem).wait()

    for i, ref in enumerate((db_hbm, dc_hbm)):
        remote(ref, dstates.at[2 + i], ds_send.at[i], ds_recv.at[i], (dp, zed * 2 + 1 - core))

    place = lax.broadcasted_iota(jnp.int32, (256, 128), 0) - lax.broadcasted_iota(jnp.int32, (256, 128), 1)

    def build_shifts(mask, first, before):
        @pl.loop(0, tokens // 128)
        def _(b):
            at = pl.ds(pl.multiple_of(before + b * 128, 128), 128)
            for k in range(3):
                shifts[b, :, k * 128 : k * 128 + 128] = jnp.where(
                    place == first(k), mask[k : k + 1, at], 0.0
                ).astype(BF16)

    def shift(source, count):
        @pl.loop(0, tokens // 128)
        def _(b):
            at = pl.multiple_of(b * 128, 128)
            out = mm(source[:, pl.ds(at, 256)], shifts[b], 1, 0).astype(BF16)
            for k in range(3):
                moved[k, 0:count, pl.ds(at, 128)] = out[:, k * 128 : k * 128 + 128]

    def slopes(source, taps, rows, base, grad):
        at = pl.ds(base, 256)
        terms = [moved[k, rows, at].astype(F32) for k in range(3)]
        terms.append(source[rows, pl.ds(LH + base, 256)].astype(F32))
        pre = taps[:, 4:5]
        for k in range(4):
            pre = pre + taps[:, k : k + 1] * terms[k]
        sig = sigmoid(pre)
        q = grad * (sig * (1.0 + pre * (1.0 - sig)))
        return q, [folded(q * term) for term in terms] + [folded(q)]

    def line_sums(count, to):
        for k in range(5):
            to(k)[...] = jnp.sum(acc[k, 0:count].T, axis=0, keepdims=True)

    build_shifts(match, lambda k: 125 + k, LH)

    @pl.loop(0, nz)
    def _(z):
        for copy in column_loads(z):
            copy.wait()
        cols[...] = pars[2 * z + core, 0:8, :].T
        shift(p, c)

        @pl.loop(0, c // 16, unroll=2)
        def _(i):
            rows_at = pl.ds(pl.multiple_of(i * 16, 16), 16)
            taps = cols[rows_at, :]
            totals = None
            for base in range(0, tokens, 256):
                q, terms = slopes(p, taps, rows_at, base, e[rows_at, pl.ds(base, 256)])
                queue[z, rows_at, pl.ds(base, 256)] = q.astype(BF16)
                totals = terms if totals is None else [a + b for a, b in zip(totals, terms)]
            for k in range(5):
                acc[k, rows_at, :] = totals[k]

        @pl.when(z < nz - 1)
        def _():
            for copy in column_loads(z + 1):
                copy.start()

        heads[z] = queue[z, :, 0:128].astype(F32).T[0:8]

        @pl.when(zed > 0)
        def _():
            remote(
                heads.at[z], halo.at[z], halo_send.at[z], halo_recv.at[z], (dp, (zed - 1) * 2 + core)
            )

        line_sums(c, lambda k: table_ref.at[z, k : k + 1])
        table_ref[z, 5:6] = mix_ref[z, 0:1]
        table_ref[z, 6:16] = jnp.zeros((10, c), F32)
        table_ref[z, 8:9] = mix_ref[z, 1:2]

    count = nz * 8
    da, dt, rates = da_ref[...], dt_ref[...], rates_ref[:, 0:1]
    step_grad = jnp.where(dt > TINY, xdx_ref[...] / jnp.maximum(dt, TINY), 0.0) + rates * da
    steps_grad = step_grad * sigmoid(v_ref[...])
    for k, v in ((6, steps_grad), (7, rates * (dt * da))):
        padded = folded(v)
        if count < 128:
            padded = jnp.concatenate([padded, jnp.zeros((128 - count, 128), F32)], axis=0)
        line = jnp.sum(padded.T, axis=0, keepdims=True)
        for z in range(nz):
            table_ref[z, k : k + 1, 0:128] = line[:, 0:128]
    steps_low = steps_grad.astype(BF16)

    for i in range(3):
        loads[i].wait()
    for i in range(2):
        wait_for(dstates.at[2 + i], ds_recv.at[i])
    for z in range(nz):
        both = pars[2 * z, 8:16, 0:128] + pars[2 * z + 1, 8:16, 0:128]
        scols[z * 2 * sc : (z + 1) * 2 * sc, :] = both.T[0 : 2 * sc, 1:6]

    @pl.loop(0, tokens // 128)
    def _(b):
        at = pl.ds(pl.multiple_of(b * 128, 128), 128)
        for i in range(2):
            e[i * 128 : i * 128 + 128, at] = (dstates[i, at, :] + dstates[2 + i, at, :]).T

    bc_rows = 2 * sc * nz
    shift(st, bc_rows)

    @pl.loop(0, bc_rows // 16, unroll=2)
    def _(i):
        rows_at = pl.ds(pl.multiple_of(i * 16, 16), 16)
        taps = scols[rows_at, :]
        totals = None
        for base in range(0, tokens, 256):
            q, terms = slopes(st, taps, rows_at, base, e[rows_at, pl.ds(base, 256)])
            squeue[rows_at, pl.ds(base, 256)] = q.astype(BF16)
            totals = terms if totals is None else [a + b for a, b in zip(totals, terms)]
        for k in range(5):
            acc[k, rows_at, :] = totals[k]

    sheads[...] = squeue[:, 0:128].astype(F32).T[0:8]

    @pl.when(zed > 0)
    def _():
        remote(sheads, shalo, halo_send.at[nz], halo_recv.at[nz], (dp, (zed - 1) * 2 + core))

    for k in range(5):
        line = jnp.sum(acc[k, 0:bc_rows].T, axis=0, keepdims=True)
        for z in range(nz):
            table_ref[z, 9 + k : 10 + k, 0 : 2 * sc] = line[:, z * 2 * sc : (z + 1) * 2 * sc]

    build_shifts(ahead, lambda k: 3 - k, 0)

    @pl.when(zed == nz - 1)
    def _():
        halo[...] = jnp.zeros(halo.shape, F32)
        shalo[...] = jnp.zeros(shalo.shape, F32)

    @pl.when(zed < nz - 1)
    def _():
        wait_for(shalo, halo_recv.at[nz])

    def back_taps(source, taps, rows_at, base):
        at = pl.ds(base, 256)
        grad = taps[:, 3:4] * source[rows_at, at].astype(F32)
        for k in range(3):
            grad = grad + taps[:, k : k + 1] * moved[k, rows_at, at].astype(F32)
        return grad

    squeue[:, tokens:] = jnp.concatenate([shalo[...], jnp.zeros((120, bc_rows), F32)], axis=0).T.astype(BF16)
    shift(squeue, bc_rows)
    for z in range(nz):
        for i in range(2 * sc // 16):
            rows_at = slice(z * 2 * sc + i * 16, z * 2 * sc + i * 16 + 16)
            mine = ((i * 16) // sc == core).astype(F32)
            taps = scols[rows_at, :] * mine
            for base in range(0, tokens, 256):
                slanes[z, i * 16 : i * 16 + 16, pl.ds(base, 256)] = back_taps(
                    squeue, taps, rows_at, base
                ).astype(BF16)
        slanes[z, 2 * sc : 2 * sc + 16, :] = jnp.concatenate(
            [steps_low[z * 8 : z * 8 + 8].astype(F32), jnp.zeros((8, tokens), F32)], axis=0
        ).astype(BF16)

    def values_back(z):
        @pl.when(zed < nz - 1)
        def _():
            wait_for(halo.at[z], halo_recv.at[z])

        queue[z, :, tokens:] = jnp.concatenate([halo[z], jnp.zeros((120, c), F32)], axis=0).T.astype(BF16)
        cols[...] = pars[2 * z + core, 0:8, :].T
        shift(queue.at[z], c)

        @pl.loop(0, c // 16, unroll=2)
        def _(i):
            rows_at = pl.ds(pl.multiple_of(i * 16, 16), 16)
            taps = cols[rows_at, :]
            for base in range(0, tokens, 256):
                turn[rows_at, pl.ds(base, 256)] = back_taps(queue.at[z], taps, rows_at, base).astype(BF16)

        vl[z] = turn[...].T

    @pl.loop(0, nz)
    def _(z):
        values_back(z)

    small_t[...] = slanes[...].reshape(nz * sr, tokens).T
    for i in range(2):
        wait_for(dstates.at[2 + i], ds_send.at[i])

    @pl.when(zed > 0)
    def _():
        for z in range(nz):
            wait_for(heads.at[z], halo_send.at[z])
        wait_for(sheads, halo_send.at[nz])


def conv_back(nz, sc, dx, p, db, dc, st, pars, match, ahead, v, dt, xdx, da, rates, mixed):
    inner, tokens = dx.shape
    c = inner // nz
    sr, most = 2 * sc + 16, max(c, st.shape[0])
    anywhere = pl.BlockSpec(memory_space=pl.ANY)
    vmem = pl.BlockSpec(memory_space=pltpu.VMEM)
    dma = pltpu.SemaphoreType.DMA

    def buffer(*dims, dtype=F32):
        return pltpu.VMEM(dims, dtype)

    low = functools.partial(buffer, dtype=BF16)
    return pl.pallas_call(
        functools.partial(conv_back_kernel, nz, sc),
        in_specs=[anywhere] * 5 + [vmem] * 9,
        out_specs=[vmem] * 3,
        out_shape=[shape((nz, tokens, c), BF16), shape((tokens, nz * sr), BF16), shape((nz, 16, c), F32)],
        scratch_shapes=[
            low(*st.shape), buffer(4, tokens, 128), buffer(most, tokens), low(c, LH + tokens), buffer(c, 8),
            buffer(st.shape[0], 5), low(tokens // 128, 256, 384), low(3, most, tokens), buffer(5, most, 128),
            low(nz, c, tokens + 128), low(st.shape[0], tokens + 128), buffer(nz, 8, c), buffer(nz, 8, c),
            buffer(8, st.shape[0]), buffer(8, st.shape[0]), low(c, tokens), low(nz, sr, tokens),
            dma((3,)), dma((2,)), dma((2,)), dma((2,)), dma((nz + 1,)), dma((nz + 1,)),
        ],
        compiler_params=pltpu.CompilerParams(
            collective_id=3, has_side_effects=True, vmem_limit_bytes=56 * MIB
        ),
        cost_estimate=cost(8 * inner * tokens * 384, 40 * MIB),
    )(dx, p, db, dc, st, pars, match, ahead, v, dt, xdx, da, rates, mixed)


def last_kernel(
    ndp, nz, sc,
    nt_hbm, vl_hbm, small_hbm, gl_hbm, wg_hbm, wv_hbm, ws_hbm, x_hbm, cot_hbm, planes, table_ref, gain_ref,
    sum_ref, grad_ref, norm_ref, row_ref, early_ref,
    nt, vl, small_t, gl, wg, wv, ws, x, cot, small_g, blocks, own, keep, send, got,
    got_first, got_second, got_hi, got_lo, z_out, z_got, tables, trows, norm_own, norms, norm_sum, norm_sums,
    load, w_load, first_send, first_recv, second_send, second_recv, hi_send, hi_recv, lo_send, lo_recv,
    z_send, z_recv, table_send, table_recv, trow_send, trow_recv, sib_send, sib_recv,
    norm_send, norm_recv, plane_send, plane_recv, early_send, early_recv, early_own,
):
    nh, lo = 2 * nz, ndp // 2
    width, tokens = nt.shape
    n = tokens // 2
    rows, c = own.shape[1:]
    sr = 2 * sc + 16
    r = width // ndp
    half = rows // 32 * 16
    dp, head = lax.axis_index("dp"), lax.axis_index("head")
    core, zed = lax.rem(head, 2), lax.div(head, 2)
    dhi, dlo = lax.div(dp, lo), lax.rem(dp, lo)
    hi_peer = (1 - dhi) * lo + dlo
    lo_peers = [dhi * lo + lax.rem(dlo + k, lo) for k in range(1, lo)]
    diagonal = [(1 - dhi) * lo + lax.rem(dlo + k, lo) for k in range(1, lo)]
    top, low = pl.ds(0, half), pl.ds(half, rows - half)
    order = [1] + [nz - 1] * (nz > 2) + list(range(2, nz - 1)) + [0]
    slots = [lax.rem(zed + zi, nz) for zi in order]

    loads = [
        pltpu.make_async_copy(a, b, load.at[i])
        for i, (a, b) in enumerate([
            (nt_hbm, nt), (small_hbm, small_t), (vl_hbm, vl), (gl_hbm, gl), (ws_hbm, ws), (x_hbm, x), (cot_hbm, cot),
        ])
    ]
    for copy in loads:
        copy.start()

    barrier = pltpu.get_barrier_semaphore()
    partners = [(dp, lax.rem(head + k, nh)) for k in range(1, nh)]
    partners += [(lax.rem(dp + k, ndp), head) for k in range(1, ndp)]
    for partner in partners:
        pl.semaphore_signal(barrier, inc=1, device_id=partner, device_id_type=MESH)
    pl.semaphore_wait(barrier, len(partners))

    def remote(src, dst, send_sem, recv_sem, device):
        pltpu.make_async_remote_copy(
            src_ref=src, dst_ref=dst, send_sem=send_sem, recv_sem=recv_sem, device_id=device, device_id_type=MESH
        ).start()

    def wait_for(ref, sem):
        pltpu.make_async_copy(ref, ref, sem).wait()

    for m in range(2):
        for k in range(1, nz):
            z = lax.rem(zed + k, nz)
            remote(
                planes.at[m, z], early_ref.at[m, zed], early_send.at[m, k], early_recv.at[m, zed], (dp, z * 2 + core)
            )
        pltpu.make_async_copy(planes.at[m, zed], early_ref.at[m, zed], early_own.at[m]).start()

    for k in range(1, ndp):
        remote(
            table_ref, tables.at[k - 1], table_send.at[k - 1], table_recv.at[k - 1], (lax.rem(dp + k, ndp), head)
        )

    def product(d, z, to):
        left = nt[pl.ds(pl.multiple_of(d * r, 16), r), :]
        to[0:r] = mm(left, vl[z], 1, 0).astype(to.dtype)
        at = pl.multiple_of(z * sr + core * sc, 16)
        to[r : r + sc] = small_g[d, pl.ds(at, sc), :].astype(to.dtype)
        to[r + sc : rows] = small_g[d, pl.ds(pl.multiple_of(z * sr + 2 * sc, 16), 16), :].astype(to.dtype)

    loads[0].wait()
    loads[1].wait()

    @pl.loop(0, ndp)
    def _(d):
        small_g[d] = mm(nt[pl.ds(pl.multiple_of(d * r, 16), r), :], small_t[...], 1, 0).T

    loads[2].wait()
    for j, z in enumerate(slots):
        for i, d in enumerate(diagonal):
            product(d, z, blocks.at[i, j])
            remote(
                blocks.at[i, j, top], got_first.at[i, z], first_send.at[i, j], first_recv.at[i, z],
                (lo_peers[i], head),
            )
            remote(
                blocks.at[i, j, low], got_second.at[i, z], second_send.at[i, j], second_recv.at[i, z],
                (hi_peer, head),
            )

    across = lo - 1
    for j, z in enumerate(slots):
        product(hi_peer, z, blocks.at[across, j])
        for i, d in enumerate(lo_peers):
            product(d, z, blocks.at[lo + i, j])
        product(dp, z, own.at[j])
        total = blocks[across, j, top].astype(F32)
        for i in range(lo - 1):
            wait_for(got_first.at[i, z], first_recv.at[i, z])
            total = total + got_first[i, z].astype(F32)
        blocks[across, j, top] = total.astype(BF16)
        remote(blocks.at[across, j], got_hi.at[z], hi_send.at[j], hi_recv.at[z], (hi_peer, head))
        for i, d in enumerate(lo_peers):
            wait_for(got_second.at[i, z], second_recv.at[i, z])
            blocks[lo + i, j, low] = (
                blocks[lo + i, j, low].astype(F32) + got_second[i, z].astype(F32)
            ).astype(BF16)
            remote(blocks.at[lo + i, j], got_lo.at[i, z], lo_send.at[i, j], lo_recv.at[i, z], (d, head))

    for copy in loads[3:5]:
        copy.wait()

    def weight_loads(d, slot):
        return [
            pltpu.make_async_copy(wg_hbm.at[d], wg.at[slot], w_load.at[0, slot]),
            pltpu.make_async_copy(wv_hbm.at[d], wv.at[slot], w_load.at[1, slot]),
        ]

    for copy in weight_loads(0, 0):
        copy.start()

    @pl.loop(0, ndp)
    def _(d):
        slot = lax.rem(d, 2)

        @pl.when(d < ndp - 1)
        def _():
            for copy in weight_loads(d + 1, 1 - slot):
                copy.start()

        for copy in weight_loads(d, slot):
            copy.wait()
        weights = [weight[slot].reshape(nz * c, r) for weight in (wg, wv)] + [ws[d].reshape(nz * sr, r)]
        for which, buffer in ((1 - core, send), (core, keep)):
            at = pl.ds(pl.multiple_of(which * n, 128), n)
            out = mm(small_t[at, :], weights[2], 1, 0)
            for left, weight in ((gl, weights[0]), (vl, weights[1])):
                out = out + mm(jnp.concatenate([left[z, at, :] for z in range(nz)], axis=1), weight, 1, 0)
            buffer[d] = out.astype(buffer.dtype)

    remote(send, got, sib_send.at[0], sib_recv.at[0], (dp, zed * 2 + 1 - core))

    def pass_on(j):
        z = slots[j]
        wait_for(got_hi.at[z], hi_recv.at[z])
        total = own[j] + got_hi[z].astype(F32)
        for i in range(lo - 1):
            wait_for(got_lo.at[i, z], lo_recv.at[i, z])
            total = total + got_lo[i, z].astype(F32)
        own[j] = total
        if order[j]:
            z_out[j] = total.astype(BF16)
            remote(z_out.at[j], z_got.at[zed], z_send.at[j], z_recv.at[zed], (dp, z * 2 + core))

    pass_on(0)

    total = table_ref[...]
    for k in range(1, ndp):
        wait_for(tables.at[k - 1], table_recv.at[k - 1])
        total = total + tables[k - 1]
    tables[ndp - 1] = total
    for j, z in enumerate(slots[:-1]):
        remote(tables.at[ndp - 1, z], trows.at[zed], trow_send.at[j], trow_recv.at[zed], (dp, z * 2 + core))

    for copy in loads[5:]:
        copy.wait()
    wait_for(got, sib_recv.at[0])
    norm_own[...] = jnp.zeros(norm_own.shape, F32)

    @pl.loop(0, n // 128)
    def _(i):
        at = pl.ds(pl.multiple_of(i * 128, 128), 128)
        full = jnp.concatenate([keep[d, at, :] + got[d, at, :].astype(F32) for d in range(ndp)], axis=1)
        tokens_x = x[at, :].astype(F32)
        inverse = lax.rsqrt(jnp.mean(tokens_x * tokens_x, axis=1, keepdims=True) + EPSILON)
        gained = full * gain_ref[...]
        dots = jnp.sum(gained * tokens_x, axis=1, keepdims=True)
        grad = inverse * gained - tokens_x * (inverse * inverse * inverse / width) * dots
        grad_ref[at, :] = (cot[at, :].astype(F32) + grad).astype(BF16)
        norm_own[0:1] += jnp.sum(full * (tokens_x * inverse), axis=0, keepdims=True)

    for k in range(1, nh):
        remote(
            norm_own, norms.at[k - 1], norm_send.at[k - 1], norm_recv.at[k - 1], (dp, lax.rem(head + k, nh))
        )
    for j in range(1, nz - 1):
        pass_on(j)
    total = norm_own[...]
    for k in range(1, nh):
        wait_for(norms.at[k - 1], norm_recv.at[k - 1])
        total = total + norms[k - 1]
    norm_sum[...] = total
    for k in range(1, ndp):
        remote(
            norm_sum, norm_sums.at[k - 1], plane_send.at[k - 1], plane_recv.at[k - 1],
            (lax.rem(dp + k, ndp), head),
        )
    pass_on(nz - 1)
    total = tables[ndp - 1, zed]
    for k in range(1, nz):
        z = lax.rem(zed + k, nz)
        wait_for(trows.at[z], trow_recv.at[z])
        total = total + trows[z]
    row_ref[...] = total
    total = norm_sum[...]
    for k in range(1, ndp):
        wait_for(norm_sums.at[k - 1], plane_recv.at[k - 1])
        total = total + norm_sums[k - 1]
    norm_ref[...] = total
    total = own[nz - 1]
    for k in range(1, nz):
        z = lax.rem(zed + k, nz)
        wait_for(z_got.at[z], z_recv.at[z])
        total = total + z_got[z].astype(F32)
    sum_ref[...] = total

    for m in range(2):
        pltpu.make_async_copy(planes.at[m, zed], early_ref.at[m, zed], early_own.at[m]).wait()
        for k in range(1, nz):
            z = lax.rem(zed + k, nz)
            wait_for(early_ref.at[m, z], early_recv.at[m, z])
            wait_for(planes.at[m, z], early_send.at[m, k])
    for j in range(nz):
        for i in range(lo - 1):
            wait_for(got_first.at[i, j], first_send.at[i, j])
            wait_for(got_second.at[i, j], second_send.at[i, j])
            wait_for(got_lo.at[i, j], lo_send.at[i, j])
        wait_for(got_hi.at[j], hi_send.at[j])
    for j in range(nz - 1):
        wait_for(z_out.at[j], z_send.at[j])
        wait_for(trows.at[j], trow_send.at[j])
    for k in range(ndp - 1):
        wait_for(table_ref, table_send.at[k])
        wait_for(norm_sum, plane_send.at[k])
    for k in range(nh - 1):
        wait_for(norm_own, norm_send.at[k])
    wait_for(send, sib_send.at[0])


def last_steps(ndp, nz, sc, nt, vl, small, gl, wg, wv, ws, x, cot, planes, table, gain):
    nh, lo = 2 * nz, ndp // 2
    width, tokens = nt.shape
    n = tokens // 2
    c = vl.shape[2]
    r = width // ndp
    rows = r + sc + 16
    half = rows // 32 * 16
    anywhere = pl.BlockSpec(memory_space=pl.ANY)
    vmem = pl.BlockSpec(memory_space=pltpu.VMEM)
    dma = pltpu.SemaphoreType.DMA

    def buffer(*dims, dtype=F32):
        return pltpu.VMEM(dims, dtype)

    low = functools.partial(buffer, dtype=BF16)
    return pl.pallas_call(
        functools.partial(last_kernel, ndp, nz, sc),
        in_specs=[anywhere] * 10 + [vmem] * 2,
        out_specs=[vmem] * 4 + [anywhere],
        out_shape=[
            shape((rows, c), F32),
            shape((n, width), BF16),
            shape((8, width), F32),
            shape((16, c), F32),
            shape(planes.shape, BF16),
        ],
        scratch_shapes=[
            low(width, tokens), low(*vl.shape), low(*small.shape), low(*gl.shape), low(2, nz, c, r), low(2, nz, c, r),
            low(*ws.shape), low(n, width), low(n, width), buffer(ndp, nz * ws.shape[2], r),
            low(ndp - 1, nz, rows, c), buffer(nz, rows, c), buffer(ndp, n, r), low(ndp, n, r), low(ndp, n, r),
            low(lo - 1, nz, half, c), low(lo - 1, nz, rows - half, c), low(nz, rows, c), low(lo - 1, nz, rows, c),
            low(nz - 1, rows, c), low(nz, rows, c), buffer(ndp, nz, 16, c), buffer(nz, 16, c),
            buffer(8, width), buffer(nh - 1, 8, width), buffer(8, width), buffer(ndp - 1, 8, width),
            dma((7,)), dma((2, 2)),
            dma((lo - 1, nz)), dma((lo - 1, nz)), dma((lo - 1, nz)), dma((lo - 1, nz)),
            dma((nz,)), dma((nz,)), dma((lo - 1, nz)), dma((lo - 1, nz)),
            dma((nz,)), dma((nz,)), dma((ndp - 1,)), dma((ndp - 1,)), dma((nz,)), dma((nz,)),
            dma((1,)), dma((1,)), dma((nh - 1,)), dma((nh - 1,)), dma((ndp - 1,)), dma((ndp - 1,)),
            dma((2, nz)), dma((2, nz)), dma((2,)),
        ],
        compiler_params=pltpu.CompilerParams(
            collective_id=2, has_side_effects=True, vmem_limit_bytes=63 * MIB
        ),
        cost_estimate=cost(4 * nz * c * tokens * width, 40 * MIB),
    )(nt, vl, small, gl, wg, wv, ws, x, cot, planes, table, gain)

def shards(
    block_input, lengths, norm_gain, in_gate, in_value, in_states, in_steps,
    conv_value, conv_value_bias, conv_states, conv_states_bias,
    step_bias, decay_log, skip_gain, gate_gain, out_proj, cotangent,
):
    ndp, nh = lax.axis_size("dp"), lax.axis_size("head")
    nz, lo = nh // 2, ndp // 2
    own, width = block_input.shape
    tokens = 2 * own
    dp, head = lax.axis_index("dp"), lax.axis_index("head")
    core, zed = head % 2, head // 2
    dhi, dlo = dp // lo, dp % lo
    r, cols = in_gate.shape
    hs, sc, taps = step_bias.shape[0], in_states.shape[1], conv_value.shape[0]
    heads, inner, state, hw = hs * nz, cols * nz, sc * nz, cols // hs
    total = 2 * inner

    def sibling(v):
        return lax.ppermute(v, "head", [(i, i ^ 1) for i in range(nh)])

    def zshift(v, k):
        return lax.ppermute(v, "head", [(i, (i + 2 * k) % nh) for i in range(nh)])

    def zstep(v, k):
        return lax.ppermute(
            v, "head", [(i, i + 2 * k) for i in range(nh) if 0 <= i + 2 * k < nh]
        )

    def lo_shift(v, k):
        return lax.ppermute(
            v, "dp", [(h * lo + i, h * lo + (i + k) % lo) for h in range(2) for i in range(lo)]
        )

    def hi_swap(v):
        return lax.ppermute(v, "dp", [(i, (i + lo) % ndp) for i in range(ndp)])

    def block(g, d, start, count):
        return lax.dynamic_slice(g, (d, 0, start, 0), (1, nz, count, g.shape[3]))[0]

    def slot(k):
        return (dlo + k) % lo

    def scatter_sends(g):
        rows = g.shape[2]
        half = rows // 32 * 16
        diagonal = [(1 - dhi) * lo + slot(k) for k in range(1, lo)]
        return [(block(g, d, 0, half), block(g, d, half, rows - half)) for d in diagonal]

    def scatter_first(sends):
        return [lo_shift(a, k + 1) for k, (a, _) in enumerate(sends)], [hi_swap(b) for _, b in sends]

    def scatter(g, first, second):
        rows = g.shape[2]
        half = rows // 32 * 16
        peer = (1 - dhi) * lo + dlo
        top = block(g, peer, 0, half).astype(F32)
        for v in first:
            top = top + v.astype(F32)
        sent = jnp.concatenate([top.astype(BF16), block(g, peer, half, rows - half)], axis=1)
        total_here = block(g, dp, 0, rows).astype(F32) + hi_swap(sent).astype(F32)
        for k in range(1, lo):
            d = dhi * lo + slot(k)
            low = block(g, d, half, rows - half).astype(F32) + second[k - 1].astype(F32)
            sent = jnp.concatenate([block(g, d, 0, half), low.astype(BF16)], axis=1)
            total_here = total_here + lo_shift(sent, k).astype(F32)
        return total_here.astype(BF16)

    heads_par = jnp.stack([step_bias, decay_log, skip_gain])
    (
        g_value, g_small, g_gate, g_out, everyone, normed_t, cot_t, value_pre, gate_pre, x_t, states_pre, bc,
        seg, match, ahead, v_steps, dt, a2, scale_back, rates, whole, sin,
    ) = gather_project(
        ndp, nz, sc, hs, hw, block_input, cotangent, in_value, in_gate, out_proj, in_states, in_steps,
        conv_value, conv_value_bias[None], gate_gain[None], heads_par, conv_states, conv_states_bias[None],
        norm_gain[None, :], lengths,
    )
    sin = sin.reshape(inner, state)
    x_t = x_t.reshape(inner, tokens)
    value_pre = value_pre.reshape(inner, LH + tokens)
    gate_pre = gate_pre.reshape(inner, tokens)
    bm, cm = bc[0], bc[1]
    places = [(i // hs) * 8 + i % hs for i in range(heads)]
    pars = lax.dynamic_index_in_dim(everyone.reshape(nz, 2, 16, cols), core, 1, keepdims=False)
    taps_t = pars[:, :8].transpose(0, 2, 1).reshape(inner, 8)
    gain = taps_t[:, 5:6]
    skip = pars[:, 8, :8].reshape(nz * 8)
    y_t, st = scan_forward(places, x_t, dt, a2, seg, bm, cm, sin, skip[:, None])

    gated, h1, sums = mix(g_out, cot_t, y_t, gate_pre, gain)
    sums = sums + sibling(sums)
    own_sums = lax.dynamic_slice_in_dim(sums, core * own, own, 1)
    out_blocks = weight_grad(ndp, cot_t, gated, sums=sums)
    out_sends = scatter_sends(out_blocks)
    y_late, out_sends = lax.optimization_barrier((y_t, out_sends))
    dy_t, gate_low, mix_cols, gate_blocks, rin = unmix(
        ndp, nz, hs, hw, y_late, gate_pre, h1, x_t, gain, sums, scale_back, cm, whole, normed_t
    )
    rin = rin.reshape(inner, state)
    plane_out = scatter(out_blocks, *scatter_first(out_sends))
    gate_first = scatter_first(scatter_sends(gate_blocks))
    dx_t, db, dc, xdx, da = scan_backward(
        places, x_t, dy_t, y_t, dt, a2, seg, bm, cm, st, rin, skip[:, None]
    )

    gate_first, dx_t = lax.optimization_barrier((gate_first, dx_t))
    plane_gate = scatter(gate_blocks, *gate_first)
    value_low, small_low, table = conv_back(
        nz, sc, dx_t, value_pre, db, dc, states_pre, everyone, match, ahead, v_steps, dt, xdx, da, rates, mix_cols
    )
    gated, table = lax.optimization_barrier((gated, table))
    keep, send = back_project(g_out, gated)
    out = result(total, keep, sibling(send), own_sums, block_input)
    sum_value, input_grad, norm_rows, row, early = last_steps(
        ndp, nz, sc, normed_t, value_low, small_low, gate_low, g_gate, g_value, g_small, block_input, cotangent,
        jnp.stack([plane_out, plane_gate]), table, norm_gain[None, :],
    )
    sum_out, sum_gate = early.astype(F32).sum(axis=1)
    own_lanes = lax.dynamic_slice_in_dim(row[6:14], zed * 8, hs, 1)
    states_row = lax.dynamic_slice_in_dim(row[9:14], core * sc, sc, 1)
    return (
        out,
        input_grad,
        norm_rows[0],
        sum_gate,
        sum_value[:r],
        sum_value[r : r + sc].T,
        sum_value[r + sc : r + sc + hs].T,
        row[:taps],
        row[4],
        states_row[:taps],
        states_row[taps],
        own_lanes[0],
        own_lanes[1],
        row[8].reshape(hs, hw).sum(axis=1),
        row[5],
        sum_out,
    )


def solution(mesh):
    both = P(("dp", "head"), None)
    grid = P("dp", "head")
    return jax.shard_map(
        shards,
        mesh=mesh,
        in_specs=(
            both, P("dp", None), P(), grid, grid, grid, grid,
            P(None, "head"), P("head"), P(None, "head"), P("head"),
            P("head"), P("head"), P("head"), P("head"), grid, both,
        ),
        out_specs=(
            both, both, P(), grid, grid, grid, grid,
            P(None, "head"), P("head"), P(None, "head"), P("head"),
            P("head"), P("head"), P("head"), P("head"), grid,
        ),
        check_vma=False,
    )
```

```python
import functools

import jax
import jax.numpy as jnp
from jax import lax
from jax.experimental import pallas as pl
from jax.experimental.pallas import tpu as pltpu
from jax.sharding import PartitionSpec as P

EPSILON = 1e-05
HALO = 16
LH = 128
QB = 128
LOG2E = 1.4426950408889634
TINY = 1e-30
F32 = jnp.float32
BF16 = jnp.bfloat16
MESH = pl.DeviceIdType.MESH
MIB = 1024 * 1024


def mm(a, b, ca, cb):
    return lax.dot_general(a, b, (((ca,), (cb,)), ((), ())), preferred_element_type=F32)


def shape(dims, dtype):
    return jax.ShapeDtypeStruct(dims, dtype)


def params(limit=48):
    return pltpu.CompilerParams(vmem_limit_bytes=limit * MIB)


def cost(flops, nbytes):
    return pl.CostEstimate(flops=int(flops), transcendentals=0, bytes_accessed=int(nbytes))


def chunk_of(count, most, unit):
    best = unit
    for size in range(unit, most + 1, unit):
        if count % size == 0:
            best = size
    return best


def sigmoid(v):
    return 0.5 * jnp.tanh(0.5 * v) + 0.5


def lane_chunks(count, most=256):
    return [pl.ds(base, most) for base in range(0, count, most)]


def folded(v):
    out = v[:, 0:128]
    for base in range(128, v.shape[1], 128):
        out = out + v[:, base : base + 128]
    return out


def lane_cumsum(v, reverse=False):
    size = v.shape[1]
    lane = lax.broadcasted_iota(jnp.int32, v.shape, 1)
    step = 1
    while step < size:
        if reverse:
            moved = pltpu.roll(v, size - step, 1)
            v = v + jnp.where(lane < size - step, moved, 0.0)
        else:
            moved = pltpu.roll(v, step, 1)
            v = v + jnp.where(lane >= step, moved, 0.0)
        step *= 2
    return v


def block_terms(dt, a2, seg_ref, b):
    cum = lane_cumsum(a2)
    logdt = jnp.log2(jnp.maximum(dt, TINY))
    source = cum - logdt
    q = dt.shape[1]
    prev = seg_ref[0:1, pl.ds(pl.multiple_of(b * q, q), q)][:, q - 1 :]
    segr = seg_ref[0:1, pl.ds(pl.multiple_of(LH + b * q, q), q)]
    segc = jnp.broadcast_to(segr, (q, q)).T
    last = cum[:, q - 1 : q]
    final = segr[:, q - 1 : q]
    reach = jnp.where(segr == prev, jnp.exp2(cum), 0.0)
    tail = jnp.where(segr == final, jnp.exp2(last - source), 0.0)
    kept = jnp.where(final == prev, jnp.exp2(last), 0.0)
    pad = (-dt.shape[0]) % 128
    padded = jnp.concatenate([source, jnp.zeros((pad, q), F32)], axis=0) if pad else source
    columns = padded.T
    row_s = lax.broadcasted_iota(jnp.int32, (q, q), 0)
    col_t = lax.broadcasted_iota(jnp.int32, (q, q), 1)
    bias = jnp.where((row_s <= col_t) & (segc == segr), 0.0, -1e30)
    return cum, columns, reach, tail, kept, bias


def scan_fwd_kernel(
    places, width,
    x_ref, dt_ref, a_ref, seg_ref, b_ref, c_ref, sin_ref, skip_ref,
    y_ref, st_ref, state,
):
    @pl.when(pl.program_id(0) == 0)
    def _():
        state[...] = sin_ref[...].astype(F32)

    cum, columns, reach, tail, kept, bias = block_terms(dt_ref[...], a_ref[...], seg_ref, pl.program_id(0))
    gt = mm(b_ref[...], c_ref[...], 1, 1)
    low = state[...].astype(BF16)
    st_ref[0] = low
    y_ref[...] = mm(low, c_ref[...], 1, 1)
    for i, h in enumerate(places):
        rows = slice(i * width, (i + 1) * width)
        weights = jnp.exp2(cum[h : h + 1] - columns[:, h : h + 1] + bias)
        mix = (gt * weights).astype(BF16)
        xh = x_ref[rows]
        xf = xh.astype(F32)
        y_ref[rows] = mm(xh, mix, 1, 0) + y_ref[rows] * reach[h : h + 1] + skip_ref[h, 0] * xf
        xs = (xf * tail[h : h + 1]).astype(BF16)
        state[rows] = state[rows] * kept[h : h + 1] + mm(xs, b_ref[...], 1, 0)


def scan_bwd_kernel(
    places, width,
    x_ref, dy_ref, y_ref, dt_ref, a_ref, seg_ref, b_ref, c_ref,
    st_ref, rin_ref, skip_ref,
    dx_ref, db_ref, dc_ref, xdx_ref, da_ref,
    adjoint, xs_all, ds_all, rows_v, rows_c, rows_r, rows_e,
):
    @pl.when(pl.program_id(0) == 0)
    def _():
        adjoint[...] = rin_ref[...].astype(F32)

    cum, columns, reach, tail, kept, bias = block_terms(
        dt_ref[...], a_ref[...], seg_ref, pl.num_programs(0) - 1 - pl.program_id(0)
    )
    bk, ck = b_ref[...], c_ref[...]
    gt = mm(bk, ck, 1, 1)
    r_low = adjoint[...].astype(BF16)
    s_low = st_ref[0]
    dx_ref[...] = mm(r_low, bk, 1, 1)
    dg = jnp.zeros(gt.shape, F32)
    for i, h in enumerate(places):
        rows = slice(i * width, (i + 1) * width)
        weights = jnp.exp2(cum[h : h + 1] - columns[:, h : h + 1] + bias)
        mix = (gt * weights).astype(BF16)
        xh, dyh = x_ref[rows], dy_ref[rows]
        xf, dyf = xh.astype(F32), dyh.astype(F32)
        pairs = mm(xh, dyh, 0, 0)
        dg = dg + weights * pairs
        inner = mm(dyh, mix, 1, 1)
        outer = dx_ref[rows] * tail[h : h + 1]
        skip = skip_ref[h, 0]
        rows_v[h : h + 1] = jnp.sum(xf * outer, axis=0, keepdims=True)
        rows_c[h : h + 1] = jnp.sum(xf * inner, axis=0, keepdims=True)
        rows_r[h : h + 1] = jnp.sum(dyf * (y_ref[rows] - skip * xf), axis=0, keepdims=True)
        dx_ref[rows] = inner + outer + skip * dyf
        xs_all[rows] = (xf * tail[h : h + 1]).astype(BF16)
        ds = (dyf * reach[h : h + 1]).astype(BF16)
        ds_all[rows] = ds
        carried = adjoint[rows] * kept[h : h + 1]
        rows_e[h : h + 1] = jnp.sum(carried * s_low[rows].astype(F32), axis=0, keepdims=True)
        adjoint[rows] = carried + mm(ds, ck, 1, 0)
    dgl = dg.astype(BF16)
    db_ref[...] = mm(xs_all[...], r_low, 0, 0) + mm(dgl, ck, 1, 0)
    dc_ref[...] = mm(ds_all[...], s_low, 0, 0) + mm(dgl, bk, 0, 0)
    v, c = rows_v[...], rows_c[...]
    xdx_ref[...] = v + c
    ends = jnp.sum(rows_e[...], axis=1, keepdims=True)
    da_ref[...] = lane_cumsum(rows_r[...] - c, True) + (lane_cumsum(v) - v) + ends


def scan_specs(inner, heads, state, nb, flip):
    def at(b):
        return nb - 1 - b if flip else b

    lanes = pl.BlockSpec((inner, QB), lambda b: (0, at(b)))
    per_head = pl.BlockSpec((heads, QB), lambda b: (0, at(b)))
    seg = pl.BlockSpec((8, LH + nb * QB), lambda b: (0, 0))
    nat = pl.BlockSpec((QB, state), lambda b: (at(b), 0))
    full = pl.BlockSpec((inner, state), lambda b: (0, 0))
    skip = pl.BlockSpec(memory_space=pltpu.SMEM)
    st = pl.BlockSpec((1, inner, state), lambda b: (at(b), 0, 0))
    return lanes, per_head, seg, nat, full, skip, st


def scan_forward(places, x, dt, a2, seg, bm, cm, sin, skip):
    heads, tokens = dt.shape
    inner, state = x.shape[0], bm.shape[1]
    nb = tokens // QB
    lanes, per_head, sg, nat, full, sk, st = scan_specs(inner, heads, state, nb, False)
    return pl.pallas_call(
        functools.partial(scan_fwd_kernel, places, inner // len(places)),
        grid=(nb,),
        in_specs=[lanes, per_head, per_head, sg, nat, nat, full, sk],
        out_specs=[lanes, st],
        out_shape=[
            jax.ShapeDtypeStruct((inner, tokens), F32),
            jax.ShapeDtypeStruct((nb, inner, state), BF16),
        ],
        scratch_shapes=[pltpu.VMEM((inner, state), F32)],
        compiler_params=params(),
        cost_estimate=pl.CostEstimate(
            flops=20 * inner * tokens * state, transcendentals=0, bytes_accessed=10 * x.size
        ),
    )(x, dt, a2, seg, bm, cm, sin, skip)


def scan_backward(places, x, dy, y, dt, a2, seg, bm, cm, st_in, rin, skip):
    heads, tokens = dt.shape
    inner, state = x.shape[0], bm.shape[1]
    nb = tokens // QB
    lanes, per_head, sg, nat, full, sk, st = scan_specs(inner, heads, state, nb, True)
    return pl.pallas_call(
        functools.partial(scan_bwd_kernel, places, inner // len(places)),
        grid=(nb,),
        in_specs=[lanes, lanes, lanes, per_head, per_head, sg, nat, nat, st, full, sk],
        out_specs=[lanes, nat, nat, per_head, per_head],
        out_shape=[
            jax.ShapeDtypeStruct((inner, tokens), F32),
            jax.ShapeDtypeStruct((tokens, state), F32),
            jax.ShapeDtypeStruct((tokens, state), F32),
            jax.ShapeDtypeStruct((heads, tokens), F32),
            jax.ShapeDtypeStruct((heads, tokens), F32),
        ],
        scratch_shapes=[
            pltpu.VMEM((inner, state), F32),
            pltpu.VMEM((inner, QB), BF16),
            pltpu.VMEM((inner, QB), BF16),
            pltpu.VMEM((heads, QB), F32),
            pltpu.VMEM((heads, QB), F32),
            pltpu.VMEM((heads, QB), F32),
            pltpu.VMEM((heads, state), F32),
        ],
        compiler_params=params(),
        cost_estimate=pl.CostEstimate(
            flops=60 * inner * tokens * state, transcendentals=0, bytes_accessed=16 * x.size
        ),
    )(x, dy, y, dt, a2, seg, bm, cm, st_in, rin, skip)

def gather_kernel(
    ndp, nz, sc, hs, hw,
    x_ref, cot_ref, wv_in, wg_in, wo_in,
    states_ref, stepw_ref, cv_ref, cvb_ref, gg1_ref, heads_ref, cs_ref, csb_ref, gain_ref, len_ref,
    gv_ref, gs_ref, gg_ref, go_ref, pars_ref, nt_ref, ct_ref, vpre_ref, gpre_ref, vt_ref, st_ref, bc_ref,
    seg_ref, match_ref, ahead_ref, v_ref, dt_ref, a_ref, scale_ref, rates_ref, whole_ref, sin_ref,
    xbuf, nt, cbuf, ct, wv_ref, wg_ref, wo_ref, ws_ref, small_own, small_sib, par_ref, wvm, wsm, pvm, cols,
    scols, shifts, spre, st_low, vpre, gpre, vt,
    scaled, tails, fresh, hop_out, hop_in,
    z_send, full_recv, near_send, far_send, far_recv, misc_send, misc_recv, par_send, par_recv, local, load, out_sem,
    hop_send, hop_recv,
):
    nh, lo = 2 * nz, ndp // 2
    n, width = x_ref.shape
    tokens = 2 * n
    r, c = wv_in.shape
    dp, head = lax.axis_index("dp"), lax.axis_index("head")
    core, zed = lax.rem(head, 2), lax.div(head, 2)
    dhi, dlo = lax.div(dp, lo), lax.rem(dp, lo)
    sib = zed * 2 + 1 - core
    hi_peer = (1 - dhi) * lo + dlo
    lo_slots = [lax.rem(dlo + k, lo) for k in range(1, lo)]
    lo_peers = [dhi * lo + s for s in lo_slots]

    def half(rows, i):
        return pl.ds(0, rows // 32 * 16) if i == 0 else pl.ds(rows // 32 * 16, rows - rows // 32 * 16)

    order = [1] + [nz - 1] * (nz > 2) + list(range(2, nz - 1))

    barrier = pltpu.get_barrier_semaphore()
    partners = [(dp, lax.rem(head + k, nh)) for k in range(1, nh)]
    partners += [(p, head) for p in lo_peers + [hi_peer]]
    for partner in partners:
        pl.semaphore_signal(barrier, inc=1, device_id=partner, device_id_type=MESH)
    pl.semaphore_wait(barrier, len(partners))

    def remote(src, dst, send, recv, device):
        pltpu.make_async_remote_copy(
            src_ref=src, dst_ref=dst, send_sem=send, recv_sem=recv, device_id=device, device_id_type=MESH
        ).start()

    def wait_for(ref, sem):
        pltpu.make_async_copy(ref, ref, sem).wait()

    def along_z(m, own, slot):
        for k in range(1, nz):
            remote(
                own, slot, z_send.at[m, k], full_recv.at[m, dp, zed], (dp, lax.rem(zed + k, nz) * 2 + core)
            )

    def near(m, slots, zi, own=None):
        z = lax.rem(zed + zi, nz)
        if own is None:
            wait_for(slots.at[dp, z], full_recv.at[m, dp, z])
        src = slots.at[dp, z] if own is None else own
        for i, p in enumerate(lo_peers + [hi_peer]):
            remote(src, slots.at[dp, z], near_send.at[m, zi, i], full_recv.at[m, dp, z], (p, head))

    def far(m, slots, zi):
        z = lax.rem(zed + zi, nz)
        wait_for(slots.at[hi_peer, z], full_recv.at[m, hi_peer, z])
        for i, p in enumerate(lo_peers):
            part = slots.at[hi_peer, z, half(slots.shape[2], 0)]
            remote(part, part, far_send.at[m, zi, i], far_recv.at[m, hi_peer, z, 0], (p, head))
        for i, d in enumerate(lo_peers):
            wait_for(slots.at[d, z], full_recv.at[m, d, z])
            part = slots.at[d, z, half(slots.shape[2], 1)]
            remote(part, part, far_send.at[m, zi, lo - 1 + i], far_recv.at[m, d, z, 1], (hi_peer, head))

    def fetch(m, slots, vm, z):
        for s in lo_slots:
            d = (1 - dhi) * lo + s
            for i in range(2):
                wait_for(slots.at[d, z, half(slots.shape[2], i)], far_recv.at[m, d, z, i])
        for d in range(ndp):
            pltpu.make_async_copy(slots.at[d, z], vm.at[z, d], load.at[m, z, d]).start()

    def fetched(m, slots, vm, z):
        for d in range(ndp):
            pltpu.make_async_copy(slots.at[d, z], vm.at[z, d], load.at[m, z, d]).wait()

    def lanes(v, before):
        parts = [jnp.zeros((v.shape[0], before), F32)] * (before > 0) + [v.astype(F32)]
        return jnp.concatenate(parts + [jnp.zeros((v.shape[0], 128 - before - v.shape[1]), F32)], axis=1)

    wv_ref[...] = wv_in[...].T
    along_z(0, wv_ref, gv_ref.at[dp, zed])
    near(0, gv_ref, 0, wv_ref)
    small_t = pltpu.roll(lanes(states_ref[...], 0), core * sc, 1) + lanes(stepw_ref[...], 2 * sc)
    ws_ref[...] = small_t.T[0 : ws_ref.shape[0]].astype(BF16)
    remote(ws_ref, small_sib, misc_send.at[0], misc_recv.at[0], (dp, sib))
    own_rows = pl.ds(HALO + core * n, n)
    remote(x_ref, xbuf.at[own_rows], misc_send.at[1], misc_recv.at[1], (dp, sib))

    @pl.when((core == 1) & (zed < nz - 1))
    def _():
        for i in range(2):
            remote(
                x_ref.at[pl.ds(n - HALO, HALO)], xbuf.at[pl.ds(0, HALO)], misc_send.at[3 + i], misc_recv.at[3],
                (dp, (zed + 1) * 2 + i),
            )

    wg_ref[...] = wg_in[...].T
    wo_ref[...] = wo_in[...].T
    mine = [
        pltpu.make_async_copy(x_ref, xbuf.at[own_rows], local.at[0]),
        pltpu.make_async_copy(wv_ref, gv_ref.at[dp, zed], local.at[1]),
        pltpu.make_async_copy(wg_ref, gg_ref.at[dp, zed], local.at[2]),
        pltpu.make_async_copy(cot_ref, cbuf.at[pl.ds(core * n, n)], local.at[3]),
        pltpu.make_async_copy(wo_ref, go_ref.at[dp, zed], local.at[4]),
    ]
    for copy in mine:
        copy.start()

    wait_for(small_sib, misc_recv.at[0])
    line = lax.broadcasted_iota(jnp.int32, small_own.shape, 0)
    low_line = (1 - core) * sc
    theirs = (line >= low_line) & (line < low_line + sc)
    small_own[...] = jnp.where(
        theirs, small_sib[...].astype(F32), ws_ref[...].astype(F32)
    ).astype(BF16)
    along_z(1, small_own, gs_ref.at[dp, zed])
    near(1, gs_ref, 0, small_own)
    own_small = pltpu.make_async_copy(small_own, gs_ref.at[dp, zed], local.at[7])
    own_small.start()
    par_ref[...] = jnp.zeros(par_ref.shape, F32)
    par_ref[0:4] = cv_ref[...]
    par_ref[4:5] = cvb_ref[...]
    par_ref[5:6] = gg1_ref[...]
    par_ref[6:9, 0:128] = lanes(heads_ref[...], 0)
    par_ref[9:13, 0:128] = pltpu.roll(lanes(cs_ref[...], 0), core * sc, 1)
    par_ref[13:14, 0:128] = pltpu.roll(lanes(csb_ref[...], 0), core * sc, 1)
    own_par = pltpu.make_async_copy(par_ref, pars_ref.at[head], local.at[5])
    own_par.start()
    for k in range(1, nh):
        remote(par_ref, pars_ref.at[head], par_send.at[k], par_recv.at[head], (dp, lax.rem(head + k, nh)))
    remote(cot_ref, cbuf.at[pl.ds(core * n, n)], misc_send.at[2], misc_recv.at[2], (dp, sib))

    span = LH + tokens
    ends = [len_ref[0, 0]]
    for k in range(1, len_ref.shape[1]):
        ends.append(ends[-1] + len_ref[0, k])

    def segment(at):
        number = sum([(at >= end).astype(F32) for end in ends[1:]], (at >= ends[0]).astype(F32))
        return jnp.where((at < 0) | (at >= nz * tokens), -1.0, number)

    at = zed * tokens - LH + lax.broadcasted_iota(jnp.int32, (8, span), 1)
    tap = lax.broadcasted_iota(jnp.int32, (8, span), 0)
    number = segment(at)
    seg_ref[...] = number
    valid = (tap < 4) & (at >= zed * tokens)
    match_ref[...] = jnp.where(valid & (segment(at - 3 + tap) == number), 1.0, 0.0)
    ahead_ref[...] = jnp.where((tap < 4) & (segment(at + 3 - tap) == number), 1.0, 0.0)[:, LH:]

    def normalise(start, count):
        rows = xbuf[pl.ds(start, count), :].astype(F32)
        inverse = lax.rsqrt(jnp.mean(rows * rows, axis=1, keepdims=True) + EPSILON)
        return (rows * inverse * gain_ref[...]).astype(BF16)

    def normalise_half(which):
        @pl.loop(0, n // 128)
        def _(i):
            at = pl.multiple_of(which * n + i * 128, 128)
            nt[:, pl.ds(pl.multiple_of(LH + at, 128), 128)] = normalise(pl.multiple_of(HALO + at, 16), 128).T

    def turn(which):
        @pl.loop(0, n // 128)
        def _(i):
            at = pl.multiple_of(which * n + i * 128, 128)
            ct[:, pl.ds(at, 128)] = cbuf[pl.ds(at, 128), :].T

    mine[0].wait()
    normalise_half(core)
    near(0, gv_ref, order[0])
    wait_for(x_ref, misc_recv.at[1])
    normalise_half(1 - core)
    for zi in order[1:]:
        near(0, gv_ref, zi)
    along_z(2, wg_ref, gg_ref.at[dp, zed])
    for zi in order:
        near(1, gs_ref, zi)

    @pl.when(zed > 0)
    def _():
        wait_for(xbuf.at[pl.ds(0, HALO)], misc_recv.at[3])

    @pl.when(zed == 0)
    def _():
        xbuf[0:HALO, :] = jnp.zeros((HALO, width), BF16)

    before = normalise(0, HALO).astype(F32)
    nt[:, 0:LH] = jnp.concatenate([jnp.zeros((LH - HALO, width), F32), before], axis=0).astype(BF16).T
    out_nt = pltpu.make_async_copy(nt.at[:, pl.ds(LH, tokens)], nt_ref, out_sem.at[3 * nz])
    out_nt.start()
    far(0, gv_ref, 0)
    far(1, gs_ref, 0)
    mine[3].wait()
    turn(core)
    for zi in order:
        far(0, gv_ref, zi)
        far(1, gs_ref, zi)
    near(2, gg_ref, 0, wg_ref)

    for k in range(1, nh):
        other = lax.rem(head + k, nh)
        wait_for(pars_ref.at[other], par_recv.at[other])
    own_par.wait()
    get_pars = pltpu.make_async_copy(pars_ref, pvm, local.at[5])
    get_pars.start()
    wait_for(cot_ref, misc_recv.at[2])
    turn(1 - core)
    get_pars.wait()
    out_ct = pltpu.make_async_copy(ct, ct_ref, out_sem.at[3 * nz + 1])
    out_ct.start()

    own_small.wait()
    mine[1].wait()
    for z in range(nz):
        fetch(1, gs_ref, wsm, z)
    for z in range(nz):
        fetch(0, gv_ref, wvm, z)
    place = lax.broadcasted_iota(jnp.int32, (256, 128), 0) - lax.broadcasted_iota(jnp.int32, (256, 128), 1)

    @pl.loop(0, tokens // 128)
    def _(b):
        at = pl.ds(pl.multiple_of(LH + b * 128, 128), 128)
        for k in range(3):
            shifts[b, :, k * 128 : k * 128 + 128] = jnp.where(
                place == 125 + k, match_ref[k : k + 1, at], 0.0
            ).astype(BF16)

    lanes_chunk = chunk_of(span, 384, 128)

    def by_width(weights, z):
        return jnp.concatenate([weights[z, d] for d in range(ndp)], axis=1)

    def shift(source, count, rest=None):
        @pl.loop(0, tokens // 128)
        def _(b):
            wide = pl.ds(pl.multiple_of(b * 128, 128), 256)
            moved = mm(source[:, wide], shifts[b], 1, 0)
            if rest is not None:
                moved = moved + mm(rest[:, wide], shifts[b], 1, 0)
            for k in range(3):
                gpre[k, 0:count, pl.ds(pl.multiple_of(b * 128, 128), 128)] = moved[:, k * 128 : k * 128 + 128]

    def convolved(source, taps, rows, base, rest=None):
        at = pl.ds(base, 256)
        here = source[rows, pl.ds(LH + base, 256)].astype(F32)
        if rest is not None:
            here = here + rest[rows, pl.ds(LH + base, 256)].astype(F32)
        pre = taps[:, 3:4] * here + taps[:, 4:5]
        for k in range(3):
            pre = pre + taps[:, k : k + 1] * gpre[k, rows, at]
        return pre * sigmoid(pre)

    for z in range(nz):
        fetched(1, gs_ref, wsm, z)

    @pl.loop(0, span // lanes_chunk)
    def _(i):
        at = pl.ds(pl.multiple_of(i * lanes_chunk, 128), lanes_chunk)
        left = jnp.concatenate([by_width(wsm, z) for z in range(nz)], axis=0)
        spre[:, at] = mm(left, nt[:, at], 1, 0)

    sr = wsm.shape[2]
    for z in range(nz):
        part = slice(z * 2 * sc, (z + 1) * 2 * sc)
        here = spre[z * sr : z * sr + 2 * sc, :]
        high = here.astype(BF16)
        st_ref[part, :] = high
        st_low[part, :] = (here - high.astype(F32)).astype(BF16)
        v_ref[z * 8 : z * 8 + 8, :] = spre[z * sr + 2 * sc : z * sr + 2 * sc + 8, LH:]
        both = pvm[2 * z, 8:16, 0:128] + pvm[2 * z + 1, 8:16, 0:128]
        scols[part, :] = both.T[0 : 2 * sc, 1:6]
    bc_rows = 2 * sc * nz
    shift(st_ref, bc_rows, st_low)

    @pl.loop(0, bc_rows // 32, unroll=2)
    def _(g):
        rows = pl.ds(pl.multiple_of(g * 32, 32), 32)
        taps = scols[rows, :]
        for base in range(0, tokens, 256):
            scaled[rows, pl.ds(base, 256)] = convolved(st_ref, taps, rows, base, st_low).astype(BF16)

    @pl.loop(0, tokens // 128)
    def _(b):
        at = pl.ds(pl.multiple_of(b * 128, 128), 128)
        for i in range(2):
            bc_ref[i, at, :] = scaled[i * 128 : i * 128 + 128, at].T

    columns = [pvm[2 * z + core, 0:16, 0:128].T[0:8] for z in range(nz)]

    def column(k):
        return jnp.concatenate([v[:, k : k + 1] for v in columns], axis=0)

    v = v_ref[...] + column(6)
    v_ref[...] = v
    dt = jnp.maximum(v, 0.0) + jnp.log1p(jnp.exp(-jnp.abs(v)))
    dt_ref[...] = dt
    rates = -jnp.exp(column(7))
    rates_ref[...] = jnp.broadcast_to(rates, rates_ref.shape)
    a2 = dt * (rates * LOG2E)
    a_ref[...] = a2
    segr = seg_ref[0:1, LH:]
    last, first = segr[:, tokens - 1 :], seg_ref[0:1, LH - 1 : LH]
    before = lane_cumsum(a2)
    through = before[:, tokens - 1 :]
    scale_ref[...] = jnp.where(segr == first, jnp.exp2(before), 0.0)
    whole_ref[...] = jnp.broadcast_to(jnp.where(last == first, jnp.exp2(through), 0.0), whole_ref.shape)
    tail = jnp.where(segr == last, jnp.exp2(lane_cumsum(a2, True) - a2) * dt, 0.0)
    tails[...] = tail

    for z in range(nz):
        fetched(0, gv_ref, wvm, z)

    @pl.loop(0, nz)
    def _(z):
        cols[...] = pvm[2 * z + core, 0:8, :].T

        @pl.loop(0, span // lanes_chunk)
        def _(i):
            at = pl.ds(pl.multiple_of(i * lanes_chunk, 128), lanes_chunk)
            vpre[z, :, at] = mm(by_width(wvm, z), nt[:, at], 1, 0).astype(BF16)

        pltpu.make_async_copy(vpre.at[z], vpre_ref.at[z], out_sem.at[z]).start()
        shift(vpre.at[z], c)

        @pl.loop(0, c // 32, unroll=2)
        def _(g):
            rows = pl.ds(pl.multiple_of(g * 32, 32), 32)
            taps = cols[rows, :]
            decay = pl.ds(z * 8 + g // (hw // 32), 1)
            for base in range(0, tokens, 256):
                at = pl.ds(base, 256)
                low = convolved(vpre.at[z], taps, rows, base).astype(BF16)
                vt[z, rows, at] = low
                scaled[rows, at] = (low.astype(F32) * tails[decay, at]).astype(BF16)

        pltpu.make_async_copy(vt.at[z], vt_ref.at[z], out_sem.at[nz + z]).start()
        fresh[z] = mm(scaled[0:c, :], bc_ref[0], 1, 0)

        @pl.when(z < nz - 1)
        def _():
            near(2, gg_ref, z + 1)

        @pl.when(z > 0)
        def _():
            far(2, gg_ref, z - 1)

        @pl.when(z == 1)
        def _():
            along_z(3, wo_ref, go_ref.at[dp, zed])

    far(2, gg_ref, nz - 1)

    mine[2].wait()
    near(3, go_ref, 0, wo_ref)
    for z in range(nz):
        fetch(2, gg_ref, wvm, z)
    gate_chunk = chunk_of(tokens, 512, 128)

    def hop(i):
        if i:
            hop_arrived(i - 1)
            for z in range(nz):
                for h in range(hs):
                    at = slice(h * hw, (h + 1) * hw)
                    state = whole_ref[z * 8 + h : z * 8 + h + 1, :] * hop_in[i - 1, z, at, :].astype(F32)
                    hop_out[i, z, at, :] = (fresh[z, at, :] + state).astype(BF16)
        else:
            hop_out[0] = fresh[...].astype(BF16)

        @pl.when(zed < nz - 1)
        def _():
            remote(hop_out.at[i], hop_in.at[i], hop_send.at[i], hop_recv.at[i], (dp, (zed + 1) * 2 + core))

    def hop_arrived(i):
        @pl.when(zed > 0)
        def _():
            wait_for(hop_in.at[i], hop_recv.at[i])

        @pl.when(zed == 0)
        def _():
            hop_in[i] = jnp.zeros(hop_in.shape[1:], BF16)

    hops = nz // 2
    for i in range(hops):
        hop(i)
        if i == 0:
            for zi in order:
                near(3, go_ref, zi)
        for z in (2 * i, 2 * i + 1):
            fetched(2, gg_ref, wvm, z)

        @pl.loop(2 * i, 2 * i + 2)
        def _(z):
            @pl.loop(0, tokens // gate_chunk)
            def _(i):
                at = pl.multiple_of(i * gate_chunk, 128)
                right = nt[:, pl.ds(pl.multiple_of(LH + at, 128), gate_chunk)]
                gpre[z, 0:c, pl.ds(at, gate_chunk)] = mm(by_width(wvm, z), right, 1, 0)

            pltpu.make_async_copy(gpre.at[z, pl.ds(0, c)], gpre_ref.at[z], out_sem.at[2 * nz + z]).start()

    for zi in [0] + order:
        far(3, go_ref, zi)
    hop_arrived(hops - 1)
    sin_ref[...] = hop_in[hops - 1]

    @pl.when(zed < nz - 1)
    def _():
        for i in range(hops):
            wait_for(hop_out.at[i], hop_send.at[i])

    mine[4].wait()
    for z in range(nz):
        for s in lo_slots:
            d = (1 - dhi) * lo + s
            for i in range(2):
                wait_for(go_ref.at[d, z, half(c, i)], far_recv.at[3, d, z, i])
    sent = [wv_ref, small_own, wg_ref, wo_ref]
    for m in range(4):
        for k in range(1, nz):
            wait_for(sent[m], z_send.at[m, k])
    for m in range(4):
        for zi in range(nz):
            for i in range(lo):
                wait_for(sent[m], near_send.at[m, zi, i])
            for i in range(2 * (lo - 1)):
                wait_for(sent[m].at[half(sent[m].shape[0], i // (lo - 1))], far_send.at[m, zi, i])
    wait_for(ws_ref, misc_send.at[0])
    wait_for(x_ref, misc_send.at[1])
    wait_for(cot_ref, misc_send.at[2])
    for k in range(1, nh):
        wait_for(par_ref, par_send.at[k])

    @pl.when((core == 1) & (zed < nz - 1))
    def _():
        for i in range(2):
            wait_for(x_ref.at[pl.ds(n - HALO, HALO)], misc_send.at[3 + i])

    for z in range(nz):
        pltpu.make_async_copy(vpre.at[z], vpre_ref.at[z], out_sem.at[z]).wait()
        pltpu.make_async_copy(vt.at[z], vt_ref.at[z], out_sem.at[nz + z]).wait()
        pltpu.make_async_copy(gpre.at[z, pl.ds(0, c)], gpre_ref.at[z], out_sem.at[2 * nz + z]).wait()
    out_nt.wait()
    out_ct.wait()


def gather_project(
    ndp, nz, sc, hs, hw, x, cot, wv, wg, wo, states, stepw, cv, cvb, gg, heads, cs, csb, gain, lengths
):
    n, width = x.shape
    tokens = 2 * n
    r, c = wv.shape
    nh, lo, hops = 2 * nz, ndp // 2, nz // 2
    sr, most = 2 * sc + 16, max(c, 2 * sc * nz)
    anywhere = pl.BlockSpec(memory_space=pl.ANY)
    vmem = pl.BlockSpec(memory_space=pltpu.VMEM)
    dma = pltpu.SemaphoreType.DMA
    return pl.pallas_call(
        functools.partial(gather_kernel, ndp, nz, sc, hs, hw),
        in_specs=[anywhere] * 2 + [vmem] * 12 + [pl.BlockSpec(memory_space=pltpu.SMEM)],
        out_specs=[anywhere] * 10 + [vmem] * 12,
        out_shape=[
            shape((ndp, nz, c, r), BF16),
            shape((ndp, nz, sr, r), BF16),
            shape((ndp, nz, c, r), BF16),
            shape((ndp, nz, c, r), BF16),
            shape((nh, 16, c), F32),
            shape((width, tokens), BF16),
            shape((width, tokens), BF16),
            shape((nz, c, LH + tokens), BF16),
            shape((nz, c, tokens), F32),
            shape((nz, c, tokens), BF16),
            shape((2 * sc * nz, LH + tokens), BF16),
            shape((2, tokens, 128), BF16),
            shape((8, LH + tokens), F32),
            shape((8, LH + tokens), F32),
            shape((8, tokens), F32),
            shape((nz * 8, tokens), F32),
            shape((nz * 8, tokens), F32),
            shape((nz * 8, tokens), F32),
            shape((nz * 8, tokens), F32),
            shape((nz * 8, 128), F32),
            shape((nz * 8, 128), F32),
            shape((nz, c, 128), BF16),
        ],
        scratch_shapes=[
            pltpu.VMEM((HALO + tokens, width), BF16),
            pltpu.VMEM((width, LH + tokens), BF16),
            pltpu.VMEM((tokens, width), BF16),
            pltpu.VMEM((width, tokens), BF16),
            pltpu.VMEM((c, r), BF16),
            pltpu.VMEM((c, r), BF16),
            pltpu.VMEM((c, r), BF16),
            pltpu.VMEM((sr, r), BF16),
            pltpu.VMEM((sr, r), BF16),
            pltpu.VMEM((sr, r), BF16),
            pltpu.VMEM((16, c), F32),
            pltpu.VMEM((nz, ndp, c, r), BF16),
            pltpu.VMEM((nz, ndp, sr, r), BF16),
            pltpu.VMEM((nh, 16, c), F32),
            pltpu.VMEM((c, 8), F32),
            pltpu.VMEM((2 * sc * nz, 5), F32),
            pltpu.VMEM((tokens // 128, 256, 384), BF16),
            pltpu.VMEM((nz * sr, LH + tokens), F32),
            pltpu.VMEM((2 * sc * nz, LH + tokens), BF16),
            pltpu.VMEM((nz, c, LH + tokens), BF16),
            pltpu.VMEM((nz, most, tokens), F32),
            pltpu.VMEM((nz, c, tokens), BF16),
            pltpu.VMEM((most, tokens), BF16),
            pltpu.VMEM((nz * 8, tokens), F32),
            pltpu.VMEM((nz, c, 128), F32),
            pltpu.VMEM((hops, nz, c, 128), BF16),
            pltpu.VMEM((hops, nz, c, 128), BF16),
            dma((4, nz)),
            dma((4, ndp, nz)),
            dma((4, nz, lo)),
            dma((4, nz, 2 * (lo - 1))),
            dma((4, ndp, nz, 2)),
            dma((5,)),
            dma((4,)),
            dma((nh,)),
            dma((nh,)),
            dma((8,)),
            dma((3, nz, ndp)),
            dma((3 * nz + 2,)),
            dma((hops,)),
            dma((hops,)),
        ],
        compiler_params=pltpu.CompilerParams(
            collective_id=1, has_side_effects=True, vmem_limit_bytes=60 * MIB
        ),
        cost_estimate=cost(2 * tokens * width * nz * (2 * c + 128), 60 * MIB),
    )(x, cot, wv, wg, wo, states, stepw, cv, cvb, gg, heads, cs, csb, gain, lengths)

def mix_kernel(ndp, wo_ref, ct_ref, y_ref, g_ref, gain_ref, gated_ref, h1_ref, sums_ref, acc, low):
    c, tokens = y_ref.shape
    z = pl.program_id(0)
    chunk = chunk_of(tokens, 512, 128)

    @pl.loop(0, tokens // chunk)
    def _(i):
        at = pl.ds(pl.multiple_of(i * chunk, 128), chunk)
        left = jnp.concatenate([wo_ref[d, 0] for d in range(ndp)], axis=1)
        h1_ref[:, at] = mm(left, ct_ref[:, at], 1, 0)

    @pl.when(z == 0)
    def _():
        acc[...] = jnp.zeros(acc.shape, F32)

    @pl.loop(0, c // 16, unroll=2)
    def _(i):
        rows = pl.ds(pl.multiple_of(i * 16, 16), 16)
        scale = gain_ref[rows, :]
        for at in lane_chunks(tokens):
            g = g_ref[rows, at]
            mixed = y_ref[rows, at] * (g * sigmoid(g))
            gated = (mixed * scale).astype(BF16)
            low[rows, at] = gated
            square = mixed * mixed
            dots = gated.astype(F32) * h1_ref[rows, at]
            acc[0:8, at] += square[0:8] + square[8:16]
            acc[8:16, at] += dots[0:8] + dots[8:16]

    gated_ref[0] = low[...].T

    @pl.when(z == pl.num_programs(0) - 1)
    def _():
        sums_ref[0:1] = jnp.sum(acc[0:8], axis=0, keepdims=True)
        sums_ref[1:2] = jnp.sum(acc[8:16], axis=0, keepdims=True)
        sums_ref[2:8] = jnp.zeros((6, tokens), F32)


def mix(wo, ct, y, g, gain):
    ndp, nz, c, r = wo.shape
    width, tokens = ct.shape
    inner = nz * c
    block = pl.BlockSpec((c, tokens), lambda z: (z, 0))
    return pl.pallas_call(
        functools.partial(mix_kernel, ndp),
        grid=(nz,),
        in_specs=[
            pl.BlockSpec((ndp, 1, c, r), lambda z: (0, z, 0, 0)),
            pl.BlockSpec((width, tokens), lambda z: (0, 0)),
            block, block,
            pl.BlockSpec((c, 1), lambda z: (z, 0)),
        ],
        out_specs=[
            pl.BlockSpec((1, tokens, c), lambda z: (z, 0, 0)), block, pl.BlockSpec((8, tokens), lambda z: (0, 0)),
        ],
        out_shape=[shape((nz, tokens, c), BF16), shape((inner, tokens), F32), shape((8, tokens), F32)],
        scratch_shapes=[pltpu.VMEM((16, tokens), F32), pltpu.VMEM((c, tokens), BF16)],
        compiler_params=params(),
        cost_estimate=cost(2 * inner * tokens * width, 22 * inner * tokens),
    )(wo, ct, y, g, gain)


def unmix_kernel(
    ndp, nz, hs, hw, total,
    y_ref, g_ref, h1_ref, x_ref, gain_ref, sums_ref, scale_ref, cm_ref, whole_ref, nt_ref,
    dy_ref, gl_ref, cols_ref, grad_ref, rin_ref,
    scaled, acc, low, turned, back, hop_out, hop_in, hop_send, hop_recv,
):
    c = y_ref.shape[0]
    hops = nz // 2
    step = pl.program_id(0)
    dp, head = lax.axis_index("dp"), lax.axis_index("head")
    core, zed = lax.rem(head, 2), lax.div(head, 2)

    @pl.when(step == 0)
    def _():
        barrier = pltpu.get_barrier_semaphore()
        for k in range(1, nz):
            pl.semaphore_signal(
                barrier, inc=1, device_id=(dp, lax.rem(zed + k, nz) * 2 + core), device_id_type=MESH
            )
        pl.semaphore_wait(barrier, nz - 1)

    @pl.when(step < nz)
    def _():
        inverse = lax.rsqrt(sums_ref[0:1] / total + EPSILON)
        weight = sums_ref[1:2] * (inverse * inverse * inverse) / total

        @pl.loop(0, c // 16, unroll=2)
        def _(i):
            rows = pl.ds(pl.multiple_of(i * 16, 16), 16)
            gain = gain_ref[rows, :]
            head_row = pl.ds(i // (hw // 16), 1)
            gains, skips = [], []
            for at in lane_chunks(y_ref.shape[1]):
                y, g = y_ref[rows, at], g_ref[rows, at]
                sig = sigmoid(g)
                silu = g * sig
                mixed = y * silu
                gated_grad = h1_ref[rows, at] * inverse[:, at]
                mixed_grad = gated_grad * gain - weight[:, at] * mixed
                dy = (mixed_grad * silu).astype(BF16)
                dy_ref[rows, at] = dy
                low[rows, at] = (mixed_grad * y * (sig + silu * (1.0 - sig))).astype(BF16)
                dyf = dy.astype(F32)
                scaled[rows, at] = (dyf * scale_ref[head_row, at]).astype(BF16)
                gains.append(folded(gated_grad * mixed))
                skips.append(folded(dyf * x_ref[rows, at].astype(F32)))
            acc[0, rows, :] = sum(gains[1:], gains[0])
            acc[1, rows, :] = sum(skips[1:], skips[0])

        for k in range(2):
            cols_ref[0, k : k + 1] = jnp.sum(acc[k].T, axis=0, keepdims=True)
        cols_ref[0, 2:8] = jnp.zeros((6, c), F32)
        flipped = low[...].T
        gl_ref[0] = flipped
        turned[step] = flipped
        back[step] = mm(scaled[...], cm_ref[...], 1, 0)

    def hop_arrived(i, z):
        @pl.when(zed < nz - 1)
        def _():
            pltpu.make_async_copy(hop_in.at[i, z], hop_in.at[i, z], hop_recv.at[i, z]).wait()

        @pl.when(zed == nz - 1)
        def _():
            hop_in[i, z] = jnp.zeros(hop_in.shape[2:], BF16)

    def hop(i, z):
        if i:
            hop_arrived(i - 1, z)
            for h in range(hs):
                at = slice(h * hw, (h + 1) * hw)
                state = whole_ref[pl.ds(z * 8 + h, 1), :] * hop_in[i - 1, z, at, :].astype(F32)
                hop_out[i, z, at, :] = (back[z, at, :] + state).astype(BF16)
        else:
            hop_out[0, z] = back[z].astype(BF16)

        @pl.when(zed > 0)
        def _():
            pltpu.make_async_remote_copy(
                src_ref=hop_out.at[i, z], dst_ref=hop_in.at[i, z],
                send_sem=hop_send.at[i, z], recv_sem=hop_recv.at[i, z],
                device_id=(dp, (zed - 1) * 2 + core), device_id_type=MESH,
            ).start()

    @pl.when(step >= nz)
    def _():
        r = nt_ref.shape[0] // ndp
        right = turned[step - nz]
        for d in range(ndp):
            grad_ref[d, 0] = mm(nt_ref[d * r : (d + 1) * r, :], right, 1, 0).astype(BF16)

    for i in range(hops):
        @pl.when((step >= 2 * i) & (step < nz + 2 * i))
        def _(i=i):
            hop(i, step - 2 * i)

    @pl.when(step == 2 * nz - 1)
    def _():
        for z in range(nz):
            hop_arrived(hops - 1, z)
        rin_ref[...] = hop_in[hops - 1]

        @pl.when(zed > 0)
        def _():
            for i in range(hops):
                for z in range(nz):
                    pltpu.make_async_copy(hop_out.at[i, z], hop_out.at[i, z], hop_send.at[i, z]).wait()


def unmix(ndp, nz, hs, hw, y, g, h1, x, gain, sums, scale, cm, whole, nt):
    inner, tokens = y.shape
    c = inner // nz
    state = cm.shape[1]
    width = nt.shape[0]
    hops = nz // 2

    def first(s):
        return jnp.minimum(s, nz - 1)

    def second(s):
        return jnp.maximum(s - nz, 0)

    block = pl.BlockSpec((c, tokens), lambda s: (first(s), 0))
    dma = pltpu.SemaphoreType.DMA

    def fixed(v):
        return pl.BlockSpec(v.shape, lambda s: (0,) * v.ndim)

    return pl.pallas_call(
        functools.partial(unmix_kernel, ndp, nz, hs, hw, inner * 2),
        grid=(2 * nz,),
        in_specs=[
            block, block, block, block,
            pl.BlockSpec((c, 1), lambda s: (first(s), 0)),
            fixed(sums),
            pl.BlockSpec((8, tokens), lambda s: (first(s), 0)),
            fixed(cm), fixed(whole), fixed(nt),
        ],
        out_specs=[
            block,
            pl.BlockSpec((1, tokens, c), lambda s: (first(s), 0, 0)),
            pl.BlockSpec((1, 8, c), lambda s: (first(s), 0, 0)),
            pl.BlockSpec((ndp, 1, width // ndp, c), lambda s: (0, second(s), 0, 0)),
            pl.BlockSpec((nz, c, state), lambda s: (0, 0, 0)),
        ],
        out_shape=[
            shape((inner, tokens), BF16), shape((nz, tokens, c), BF16), shape((nz, 8, c), F32),
            shape((ndp, nz, width // ndp, c), BF16), shape((nz, c, state), BF16),
        ],
        scratch_shapes=[
            pltpu.VMEM((c, tokens), BF16), pltpu.VMEM((2, c, 128), F32), pltpu.VMEM((c, tokens), BF16),
            pltpu.VMEM((nz, tokens, c), BF16), pltpu.VMEM((nz, c, state), F32),
            pltpu.VMEM((hops, nz, c, state), BF16), pltpu.VMEM((hops, nz, c, state), BF16),
            dma((hops, nz)), dma((hops, nz)),
        ],
        compiler_params=pltpu.CompilerParams(
            collective_id=4, has_side_effects=True, vmem_limit_bytes=56 * MIB
        ),
        cost_estimate=cost(2 * inner * tokens * (state + width), 28 * inner * tokens),
    )(y, g, h1, x, gain, sums, scale, cm, whole, nt)


def weight_grad_kernel(ndp, total, *refs):
    left_ref, right_ref = refs[0], refs[1]
    r = left_ref.shape[0] // ndp
    if total:
        sums_ref, out_ref, left = refs[2:]

        @pl.when(pl.program_id(0) == 0)
        def _():
            inverse = lax.rsqrt(sums_ref[0:1] / total + EPSILON)

            @pl.loop(0, left.shape[0] // 64)
            def _(i):
                rows = pl.ds(pl.multiple_of(i * 64, 64), 64)
                left[rows, :] = (left_ref[rows, :].astype(F32) * inverse).astype(BF16)
    else:
        out_ref, left = refs[2], left_ref
    for d in range(ndp):
        out_ref[d, 0] = mm(left[d * r : (d + 1) * r, :], right_ref[0], 1, 0).astype(BF16)


def weight_grad(ndp, left, right, sums=None):
    width, tokens = left.shape
    nz, _, c = right.shape
    r, inner = width // ndp, nz * c
    operands = [left, right]
    specs = [pl.BlockSpec((width, tokens), lambda z: (0, 0)), pl.BlockSpec((1, tokens, c), lambda z: (z, 0, 0))]
    scratch = []
    if sums is not None:
        operands.append(sums)
        specs.append(pl.BlockSpec((8, tokens), lambda z: (0, 0)))
        scratch = [pltpu.VMEM((width, tokens), BF16)]
    return pl.pallas_call(
        functools.partial(weight_grad_kernel, ndp, 0 if sums is None else inner * 2),
        grid=(nz,),
        in_specs=specs,
        out_specs=pl.BlockSpec((ndp, 1, r, c), lambda z: (0, z, 0, 0)),
        out_shape=shape((ndp, nz, r, c), BF16),
        scratch_shapes=scratch,
        compiler_params=params(),
        cost_estimate=cost(2 * inner * tokens * width, 8 * inner * tokens),
    )(*operands)


def conv_back_kernel(
    nz, sc,
    dx_hbm, p_hbm, db_hbm, dc_hbm, st_hbm, plane,
    pars, match, ahead, v_ref, dt_ref, xdx_ref, da_ref, rates_ref, mix_ref,
    vl, small_t, table_ref, early_ref,
    st, dstates, e, p, cols, scols, shifts, moved, acc, queue, squeue, heads, halo, sheads, shalo, turn, slanes,
    load, e_load, ds_send, ds_recv, halo_send, halo_recv, early_send, early_recv, early_own,
):
    nh = 2 * nz
    _, c, wide = queue.shape
    tokens = wide - 128
    sr = 2 * sc + 16
    dp, head = lax.axis_index("dp"), lax.axis_index("head")
    core, zed = lax.rem(head, 2), lax.div(head, 2)

    def column_loads(z):
        at = pl.ds(pl.multiple_of(z * c, 16), c)
        return [
            pltpu.make_async_copy(dx_hbm.at[at], e.at[pl.ds(0, c)], e_load.at[0]),
            pltpu.make_async_copy(p_hbm.at[at], p, e_load.at[1]),
        ]

    for copy in column_loads(0):
        copy.start()
    loads = [
        pltpu.make_async_copy(a, b, load.at[i])
        for i, (a, b) in enumerate([(st_hbm, st), (db_hbm, dstates.at[0]), (dc_hbm, dstates.at[1])])
    ]
    for copy in loads:
        copy.start()

    barrier = pltpu.get_barrier_semaphore()
    for k in range(1, nh):
        pl.semaphore_signal(barrier, inc=1, device_id=(dp, lax.rem(head + k, nh)), device_id_type=MESH)
    pl.semaphore_wait(barrier, nh - 1)

    def remote(src, dst, send_sem, recv_sem, device):
        pltpu.make_async_remote_copy(
            src_ref=src, dst_ref=dst, send_sem=send_sem, recv_sem=recv_sem, device_id=device, device_id_type=MESH
        ).start()

    def wait_for(ref, sem):
        pltpu.make_async_copy(ref, ref, sem).wait()

    for i, ref in enumerate((db_hbm, dc_hbm)):
        remote(ref, dstates.at[2 + i], ds_send.at[i], ds_recv.at[i], (dp, zed * 2 + 1 - core))

    for k in range(1, nz):
        z = lax.rem(zed + k, nz)
        remote(plane.at[z], early_ref.at[zed], early_send.at[k], early_recv.at[zed], (dp, z * 2 + core))
    keep_own = pltpu.make_async_copy(plane.at[zed], early_ref.at[zed], early_own.at[0])
    keep_own.start()

    place = lax.broadcasted_iota(jnp.int32, (256, 128), 0) - lax.broadcasted_iota(jnp.int32, (256, 128), 1)

    def build_shifts(mask, first, before):
        @pl.loop(0, tokens // 128)
        def _(b):
            at = pl.ds(pl.multiple_of(before + b * 128, 128), 128)
            for k in range(3):
                shifts[b, :, k * 128 : k * 128 + 128] = jnp.where(
                    place == first(k), mask[k : k + 1, at], 0.0
                ).astype(BF16)

    def shift(source, count):
        @pl.loop(0, tokens // 128)
        def _(b):
            at = pl.multiple_of(b * 128, 128)
            out = mm(source[:, pl.ds(at, 256)], shifts[b], 1, 0).astype(BF16)
            for k in range(3):
                moved[k, 0:count, pl.ds(at, 128)] = out[:, k * 128 : k * 128 + 128]

    def slopes(source, taps, rows, base, grad):
        at = pl.ds(base, 256)
        terms = [moved[k, rows, at].astype(F32) for k in range(3)]
        terms.append(source[rows, pl.ds(LH + base, 256)].astype(F32))
        pre = taps[:, 4:5]
        for k in range(4):
            pre = pre + taps[:, k : k + 1] * terms[k]
        sig = sigmoid(pre)
        q = grad * (sig * (1.0 + pre * (1.0 - sig)))
        return q, [folded(q * term) for term in terms] + [folded(q)]

    def line_sums(count, to):
        for k in range(5):
            to(k)[...] = jnp.sum(acc[k, 0:count].T, axis=0, keepdims=True)

    build_shifts(match, lambda k: 125 + k, LH)

    @pl.loop(0, nz)
    def _(z):
        for copy in column_loads(z):
            copy.wait()
        cols[...] = pars[2 * z + core, 0:8, :].T
        shift(p, c)

        @pl.loop(0, c // 16, unroll=2)
        def _(i):
            rows_at = pl.ds(pl.multiple_of(i * 16, 16), 16)
            taps = cols[rows_at, :]
            totals = None
            for base in range(0, tokens, 256):
                q, terms = slopes(p, taps, rows_at, base, e[rows_at, pl.ds(base, 256)])
                queue[z, rows_at, pl.ds(base, 256)] = q.astype(BF16)
                totals = terms if totals is None else [a + b for a, b in zip(totals, terms)]
            for k in range(5):
                acc[k, rows_at, :] = totals[k]

        @pl.when(z < nz - 1)
        def _():
            for copy in column_loads(z + 1):
                copy.start()

        heads[z] = queue[z, :, 0:128].astype(F32).T[0:8]

        @pl.when(zed > 0)
        def _():
            remote(
                heads.at[z], halo.at[z], halo_send.at[z], halo_recv.at[z], (dp, (zed - 1) * 2 + core)
            )

        line_sums(c, lambda k: table_ref.at[z, k : k + 1])
        table_ref[z, 5:6] = mix_ref[z, 0:1]
        table_ref[z, 6:16] = jnp.zeros((10, c), F32)
        table_ref[z, 8:9] = mix_ref[z, 1:2]

    count = nz * 8
    da, dt, rates = da_ref[...], dt_ref[...], rates_ref[:, 0:1]
    step_grad = jnp.where(dt > TINY, xdx_ref[...] / jnp.maximum(dt, TINY), 0.0) + rates * da
    steps_grad = step_grad * sigmoid(v_ref[...])
    for k, v in ((6, steps_grad), (7, rates * (dt * da))):
        padded = folded(v)
        if count < 128:
            padded = jnp.concatenate([padded, jnp.zeros((128 - count, 128), F32)], axis=0)
        line = jnp.sum(padded.T, axis=0, keepdims=True)
        for z in range(nz):
            table_ref[z, k : k + 1, 0:128] = line[:, 0:128]
    steps_low = steps_grad.astype(BF16)

    for i in range(3):
        loads[i].wait()
    for i in range(2):
        wait_for(dstates.at[2 + i], ds_recv.at[i])
    for z in range(nz):
        both = pars[2 * z, 8:16, 0:128] + pars[2 * z + 1, 8:16, 0:128]
        scols[z * 2 * sc : (z + 1) * 2 * sc, :] = both.T[0 : 2 * sc, 1:6]

    @pl.loop(0, tokens // 128)
    def _(b):
        at = pl.ds(pl.multiple_of(b * 128, 128), 128)
        for i in range(2):
            e[i * 128 : i * 128 + 128, at] = (dstates[i, at, :] + dstates[2 + i, at, :]).T

    bc_rows = 2 * sc * nz
    shift(st, bc_rows)

    @pl.loop(0, bc_rows // 16, unroll=2)
    def _(i):
        rows_at = pl.ds(pl.multiple_of(i * 16, 16), 16)
        taps = scols[rows_at, :]
        totals = None
        for base in range(0, tokens, 256):
            q, terms = slopes(st, taps, rows_at, base, e[rows_at, pl.ds(base, 256)])
            squeue[rows_at, pl.ds(base, 256)] = q.astype(BF16)
            totals = terms if totals is None else [a + b for a, b in zip(totals, terms)]
        for k in range(5):
            acc[k, rows_at, :] = totals[k]

    sheads[...] = squeue[:, 0:128].astype(F32).T[0:8]

    @pl.when(zed > 0)
    def _():
        remote(sheads, shalo, halo_send.at[nz], halo_recv.at[nz], (dp, (zed - 1) * 2 + core))

    for k in range(5):
        line = jnp.sum(acc[k, 0:bc_rows].T, axis=0, keepdims=True)
        for z in range(nz):
            table_ref[z, 9 + k : 10 + k, 0 : 2 * sc] = line[:, z * 2 * sc : (z + 1) * 2 * sc]

    build_shifts(ahead, lambda k: 3 - k, 0)

    @pl.when(zed == nz - 1)
    def _():
        halo[...] = jnp.zeros(halo.shape, F32)
        shalo[...] = jnp.zeros(shalo.shape, F32)

    @pl.when(zed < nz - 1)
    def _():
        wait_for(shalo, halo_recv.at[nz])

    def back_taps(source, taps, rows_at, base):
        at = pl.ds(base, 256)
        grad = taps[:, 3:4] * source[rows_at, at].astype(F32)
        for k in range(3):
            grad = grad + taps[:, k : k + 1] * moved[k, rows_at, at].astype(F32)
        return grad

    squeue[:, tokens:] = jnp.concatenate([shalo[...], jnp.zeros((120, bc_rows), F32)], axis=0).T.astype(BF16)
    shift(squeue, bc_rows)
    for z in range(nz):
        for i in range(2 * sc // 16):
            rows_at = slice(z * 2 * sc + i * 16, z * 2 * sc + i * 16 + 16)
            mine = ((i * 16) // sc == core).astype(F32)
            taps = scols[rows_at, :] * mine
            for base in range(0, tokens, 256):
                slanes[z, i * 16 : i * 16 + 16, pl.ds(base, 256)] = back_taps(
                    squeue, taps, rows_at, base
                ).astype(BF16)
        slanes[z, 2 * sc : 2 * sc + 16, :] = jnp.concatenate(
            [steps_low[z * 8 : z * 8 + 8].astype(F32), jnp.zeros((8, tokens), F32)], axis=0
        ).astype(BF16)

    def values_back(z):
        @pl.when(zed < nz - 1)
        def _():
            wait_for(halo.at[z], halo_recv.at[z])

        queue[z, :, tokens:] = jnp.concatenate([halo[z], jnp.zeros((120, c), F32)], axis=0).T.astype(BF16)
        cols[...] = pars[2 * z + core, 0:8, :].T
        shift(queue.at[z], c)

        @pl.loop(0, c // 16, unroll=2)
        def _(i):
            rows_at = pl.ds(pl.multiple_of(i * 16, 16), 16)
            taps = cols[rows_at, :]
            for base in range(0, tokens, 256):
                turn[rows_at, pl.ds(base, 256)] = back_taps(queue.at[z], taps, rows_at, base).astype(BF16)

        vl[z] = turn[...].T

    @pl.loop(0, nz)
    def _(z):
        values_back(z)

    small_t[...] = slanes[...].reshape(nz * sr, tokens).T
    keep_own.wait()
    for k in range(1, nz):
        z = lax.rem(zed + k, nz)
        wait_for(early_ref.at[z], early_recv.at[z])
        wait_for(plane.at[z], early_send.at[k])
    for i in range(2):
        wait_for(dstates.at[2 + i], ds_send.at[i])

    @pl.when(zed > 0)
    def _():
        for z in range(nz):
            wait_for(heads.at[z], halo_send.at[z])
        wait_for(sheads, halo_send.at[nz])


def conv_back(nz, sc, dx, p, db, dc, st, plane, pars, match, ahead, v, dt, xdx, da, rates, mixed):
    inner, tokens = dx.shape
    c = inner // nz
    sr, most = 2 * sc + 16, max(c, st.shape[0])
    anywhere = pl.BlockSpec(memory_space=pl.ANY)
    vmem = pl.BlockSpec(memory_space=pltpu.VMEM)
    dma = pltpu.SemaphoreType.DMA

    def buffer(*dims, dtype=F32):
        return pltpu.VMEM(dims, dtype)

    low = functools.partial(buffer, dtype=BF16)
    return pl.pallas_call(
        functools.partial(conv_back_kernel, nz, sc),
        in_specs=[anywhere] * 6 + [vmem] * 9,
        out_specs=[vmem] * 3 + [anywhere],
        out_shape=[shape((nz, tokens, c), BF16), shape((tokens, nz * sr), BF16), shape((nz, 16, c), F32), shape(plane.shape, BF16)],
        scratch_shapes=[
            low(*st.shape), buffer(4, tokens, 128), buffer(most, tokens), low(c, LH + tokens), buffer(c, 8),
            buffer(st.shape[0], 5), low(tokens // 128, 256, 384), low(3, most, tokens), buffer(5, most, 128),
            low(nz, c, tokens + 128), low(st.shape[0], tokens + 128), buffer(nz, 8, c), buffer(nz, 8, c),
            buffer(8, st.shape[0]), buffer(8, st.shape[0]), low(c, tokens), low(nz, sr, tokens),
            dma((3,)), dma((2,)), dma((2,)), dma((2,)), dma((nz + 1,)), dma((nz + 1,)), dma((nz,)), dma((nz,)), dma((1,)),
        ],
        compiler_params=pltpu.CompilerParams(
            collective_id=3, has_side_effects=True, vmem_limit_bytes=56 * MIB
        ),
        cost_estimate=cost(8 * inner * tokens * 384, 40 * MIB),
    )(dx, p, db, dc, st, plane, pars, match, ahead, v, dt, xdx, da, rates, mixed)


def last_kernel(
    ndp, nz, sc,
    nt_hbm, vl_hbm, small_hbm, gl_hbm, wg_hbm, wv_hbm, ws_hbm, x_hbm, cot_hbm, plane, gated_hbm, wo_hbm,
    table_ref, gain_ref, sums_ref,
    sum_ref, grad_ref, norm_ref, row_ref, out_ref, early_ref,
    nt, vl, small_t, gl, wg, wv, ws, x, cot, small_g, blocks, own, keep, send, got,
    keep_out, send_out, got_out,
    got_first, got_second, got_hi, got_lo, z_out, z_got, tables, trows, norm_own, norms, norm_sum, norm_sums,
    load, w_load, first_send, first_recv, second_send, second_recv, hi_send, hi_recv, lo_send, lo_recv,
    z_send, z_recv, table_send, table_recv, trow_send, trow_recv, sib_send, sib_recv,
    out_send, out_recv, gated_load,
    norm_send, norm_recv, plane_send, plane_recv, early_send, early_recv, early_own,
):
    nh, lo = 2 * nz, ndp // 2
    width, tokens = nt.shape
    n = tokens // 2
    rows, c = own.shape[1:]
    sr = 2 * sc + 16
    r = width // ndp
    half = rows // 32 * 16
    dp, head = lax.axis_index("dp"), lax.axis_index("head")
    core, zed = lax.rem(head, 2), lax.div(head, 2)
    dhi, dlo = lax.div(dp, lo), lax.rem(dp, lo)
    hi_peer = (1 - dhi) * lo + dlo
    lo_peers = [dhi * lo + lax.rem(dlo + k, lo) for k in range(1, lo)]
    diagonal = [(1 - dhi) * lo + lax.rem(dlo + k, lo) for k in range(1, lo)]
    top, low = pl.ds(0, half), pl.ds(half, rows - half)
    order = [1] + [nz - 1] * (nz > 2) + list(range(2, nz - 1)) + [0]
    slots = [lax.rem(zed + zi, nz) for zi in order]

    loads = [
        pltpu.make_async_copy(a, b, load.at[i])
        for i, (a, b) in enumerate([
            (nt_hbm, nt), (small_hbm, small_t), (vl_hbm, vl), (gl_hbm, gl), (ws_hbm, ws), (x_hbm, x), (cot_hbm, cot),
        ])
    ]
    for copy in loads:
        copy.start()

    barrier = pltpu.get_barrier_semaphore()
    partners = [(dp, lax.rem(head + k, nh)) for k in range(1, nh)]
    partners += [(lax.rem(dp + k, ndp), head) for k in range(1, ndp)]
    for partner in partners:
        pl.semaphore_signal(barrier, inc=1, device_id=partner, device_id_type=MESH)
    pl.semaphore_wait(barrier, len(partners))

    def remote(src, dst, send_sem, recv_sem, device):
        pltpu.make_async_remote_copy(
            src_ref=src, dst_ref=dst, send_sem=send_sem, recv_sem=recv_sem, device_id=device, device_id_type=MESH
        ).start()

    def wait_for(ref, sem):
        pltpu.make_async_copy(ref, ref, sem).wait()

    for k in range(1, nz):
        z = lax.rem(zed + k, nz)
        remote(plane.at[z], early_ref.at[zed], early_send.at[k], early_recv.at[zed], (dp, z * 2 + core))
    keep_own = pltpu.make_async_copy(plane.at[zed], early_ref.at[zed], early_own.at[0])
    keep_own.start()

    for k in range(1, ndp):
        remote(
            table_ref, tables.at[k - 1], table_send.at[k - 1], table_recv.at[k - 1], (lax.rem(dp + k, ndp), head)
        )

    def product(d, z, to):
        left = nt[pl.ds(pl.multiple_of(d * r, 16), r), :]
        to[0:r] = mm(left, vl[z], 1, 0).astype(to.dtype)
        at = pl.multiple_of(z * sr + core * sc, 16)
        to[r : r + sc] = small_g[d, pl.ds(at, sc), :].astype(to.dtype)
        to[r + sc : rows] = small_g[d, pl.ds(pl.multiple_of(z * sr + 2 * sc, 16), 16), :].astype(to.dtype)

    loads[0].wait()
    loads[1].wait()

    @pl.loop(0, ndp)
    def _(d):
        small_g[d] = mm(nt[pl.ds(pl.multiple_of(d * r, 16), r), :], small_t[...], 1, 0).T

    loads[2].wait()
    for j, z in enumerate(slots):
        for i, d in enumerate(diagonal):
            product(d, z, blocks.at[i, j])
            remote(
                blocks.at[i, j, top], got_first.at[i, z], first_send.at[i, j], first_recv.at[i, z],
                (lo_peers[i], head),
            )
            remote(
                blocks.at[i, j, low], got_second.at[i, z], second_send.at[i, j], second_recv.at[i, z],
                (hi_peer, head),
            )

    across = lo - 1
    for j, z in enumerate(slots):
        product(hi_peer, z, blocks.at[across, j])
        for i, d in enumerate(lo_peers):
            product(d, z, blocks.at[lo + i, j])
        product(dp, z, own.at[j])
        total = blocks[across, j, top].astype(F32)
        for i in range(lo - 1):
            wait_for(got_first.at[i, z], first_recv.at[i, z])
            total = total + got_first[i, z].astype(F32)
        blocks[across, j, top] = total.astype(BF16)
        remote(blocks.at[across, j], got_hi.at[z], hi_send.at[j], hi_recv.at[z], (hi_peer, head))
        for i, d in enumerate(lo_peers):
            wait_for(got_second.at[i, z], second_recv.at[i, z])
            blocks[lo + i, j, low] = (
                blocks[lo + i, j, low].astype(F32) + got_second[i, z].astype(F32)
            ).astype(BF16)
            remote(blocks.at[lo + i, j], got_lo.at[i, z], lo_send.at[i, j], lo_recv.at[i, z], (d, head))

    for copy in loads[3:5]:
        copy.wait()

    def weight_loads(d, slot):
        return [
            pltpu.make_async_copy(wg_hbm.at[d], wg.at[slot], w_load.at[0, slot]),
            pltpu.make_async_copy(wv_hbm.at[d], wv.at[slot], w_load.at[1, slot]),
        ]

    for copy in weight_loads(0, 0):
        copy.start()

    @pl.loop(0, ndp)
    def _(d):
        slot = lax.rem(d, 2)

        @pl.when(d < ndp - 1)
        def _():
            for copy in weight_loads(d + 1, 1 - slot):
                copy.start()

        for copy in weight_loads(d, slot):
            copy.wait()
        weights = [weight[slot].reshape(nz * c, r) for weight in (wg, wv)] + [ws[d].reshape(nz * sr, r)]
        for which, buffer in ((1 - core, send), (core, keep)):
            at = pl.ds(pl.multiple_of(which * n, 128), n)
            out = mm(small_t[at, :], weights[2], 1, 0)
            for left, weight in ((gl, weights[0]), (vl, weights[1])):
                out = out + mm(jnp.concatenate([left[z, at, :] for z in range(nz)], axis=1), weight, 1, 0)
            buffer[d] = out.astype(buffer.dtype)

    remote(send, got, sib_send.at[0], sib_recv.at[0], (dp, zed * 2 + 1 - core))

    def pass_on(j):
        z = slots[j]
        wait_for(got_hi.at[z], hi_recv.at[z])
        total = own[j] + got_hi[z].astype(F32)
        for i in range(lo - 1):
            wait_for(got_lo.at[i, z], lo_recv.at[i, z])
            total = total + got_lo[i, z].astype(F32)
        own[j] = total
        if order[j]:
            z_out[j] = total.astype(BF16)
            remote(z_out.at[j], z_got.at[zed], z_send.at[j], z_recv.at[zed], (dp, z * 2 + core))

    get_gated = pltpu.make_async_copy(gated_hbm, gl, gated_load.at[0])
    get_gated.start()

    def out_loads(d, slot):
        return pltpu.make_async_copy(wo_hbm.at[d], wg.at[slot], w_load.at[0, slot])

    out_loads(0, 0).start()
    pass_on(0)
    get_gated.wait()

    @pl.loop(0, ndp)
    def _(d):
        slot = lax.rem(d, 2)

        @pl.when(d < ndp - 1)
        def _():
            out_loads(d + 1, 1 - slot).start()

        out_loads(d, slot).wait()
        weight = wg[slot].reshape(nz * c, r)
        for which, buffer in ((1 - core, send_out), (core, keep_out)):
            at = pl.ds(pl.multiple_of(which * n, 128), n)
            left = jnp.concatenate([gl[z, at, :] for z in range(nz)], axis=1)
            buffer[d] = mm(left, weight, 1, 0).astype(buffer.dtype)

    remote(send_out, got_out, out_send.at[0], out_recv.at[0], (dp, zed * 2 + 1 - core))
    pass_on(1)

    total = table_ref[...]
    for k in range(1, ndp):
        wait_for(tables.at[k - 1], table_recv.at[k - 1])
        total = total + tables[k - 1]
    tables[ndp - 1] = total
    for j, z in enumerate(slots[:-1]):
        remote(tables.at[ndp - 1, z], trows.at[zed], trow_send.at[j], trow_recv.at[zed], (dp, z * 2 + core))

    for copy in loads[5:]:
        copy.wait()
    wait_for(got, sib_recv.at[0])
    norm_own[...] = jnp.zeros(norm_own.shape, F32)

    @pl.loop(0, n // 128)
    def _(i):
        at = pl.ds(pl.multiple_of(i * 128, 128), 128)
        full = jnp.concatenate([keep[d, at, :] + got[d, at, :].astype(F32) for d in range(ndp)], axis=1)
        tokens_x = x[at, :].astype(F32)
        inverse = lax.rsqrt(jnp.mean(tokens_x * tokens_x, axis=1, keepdims=True) + EPSILON)
        gained = full * gain_ref[...]
        dots = jnp.sum(gained * tokens_x, axis=1, keepdims=True)
        grad = inverse * gained - tokens_x * (inverse * inverse * inverse / width) * dots
        grad_ref[at, :] = (cot[at, :].astype(F32) + grad).astype(BF16)
        norm_own[0:1] += jnp.sum(full * (tokens_x * inverse), axis=0, keepdims=True)

    for k in range(1, nh):
        remote(
            norm_own, norms.at[k - 1], norm_send.at[k - 1], norm_recv.at[k - 1], (dp, lax.rem(head + k, nh))
        )
    for j in range(2, nz - 1):
        pass_on(j)
    total = norm_own[...]
    for k in range(1, nh):
        wait_for(norms.at[k - 1], norm_recv.at[k - 1])
        total = total + norms[k - 1]
    norm_sum[...] = total
    for k in range(1, ndp):
        remote(
            norm_sum, norm_sums.at[k - 1], plane_send.at[k - 1], plane_recv.at[k - 1],
            (lax.rem(dp + k, ndp), head),
        )
    wait_for(got_out, out_recv.at[0])

    @pl.loop(0, n // 128)
    def _(i):
        at = pl.ds(pl.multiple_of(i * 128, 128), 128)
        inverse = lax.rsqrt(sums_ref[:, at].T[:, 0:1] / (2 * nz * c) + EPSILON)
        branch = jnp.concatenate([keep_out[d, at, :] + got_out[d, at, :].astype(F32) for d in range(ndp)], axis=1)
        out_ref[at, :] = (x[at, :].astype(F32) + branch * inverse).astype(BF16)

    pass_on(nz - 1)
    total = tables[ndp - 1, zed]
    for k in range(1, nz):
        z = lax.rem(zed + k, nz)
        wait_for(trows.at[z], trow_recv.at[z])
        total = total + trows[z]
    row_ref[...] = total
    total = norm_sum[...]
    for k in range(1, ndp):
        wait_for(norm_sums.at[k - 1], plane_recv.at[k - 1])
        total = total + norm_sums[k - 1]
    norm_ref[...] = total
    total = own[nz - 1]
    for k in range(1, nz):
        z = lax.rem(zed + k, nz)
        wait_for(z_got.at[z], z_recv.at[z])
        total = total + z_got[z].astype(F32)
    sum_ref[...] = total

    keep_own.wait()
    for k in range(1, nz):
        z = lax.rem(zed + k, nz)
        wait_for(early_ref.at[z], early_recv.at[z])
        wait_for(plane.at[z], early_send.at[k])
    for j in range(nz):
        for i in range(lo - 1):
            wait_for(got_first.at[i, j], first_send.at[i, j])
            wait_for(got_second.at[i, j], second_send.at[i, j])
            wait_for(got_lo.at[i, j], lo_send.at[i, j])
        wait_for(got_hi.at[j], hi_send.at[j])
    for j in range(nz - 1):
        wait_for(z_out.at[j], z_send.at[j])
        wait_for(trows.at[j], trow_send.at[j])
    for k in range(ndp - 1):
        wait_for(table_ref, table_send.at[k])
        wait_for(norm_sum, plane_send.at[k])
    for k in range(nh - 1):
        wait_for(norm_own, norm_send.at[k])
    wait_for(send, sib_send.at[0])
    wait_for(send_out, out_send.at[0])


def last_steps(ndp, nz, sc, nt, vl, small, gl, wg, wv, ws, x, cot, plane, gated, wo, table, gain, sums):
    nh, lo = 2 * nz, ndp // 2
    width, tokens = nt.shape
    n = tokens // 2
    c = vl.shape[2]
    r = width // ndp
    rows = r + sc + 16
    half = rows // 32 * 16
    anywhere = pl.BlockSpec(memory_space=pl.ANY)
    vmem = pl.BlockSpec(memory_space=pltpu.VMEM)
    dma = pltpu.SemaphoreType.DMA

    def buffer(*dims, dtype=F32):
        return pltpu.VMEM(dims, dtype)

    low = functools.partial(buffer, dtype=BF16)
    return pl.pallas_call(
        functools.partial(last_kernel, ndp, nz, sc),
        in_specs=[anywhere] * 12 + [vmem] * 3,
        out_specs=[vmem] * 5 + [anywhere],
        out_shape=[
            shape((rows, c), F32),
            shape((n, width), BF16),
            shape((8, width), F32),
            shape((16, c), F32),
            shape((n, width), BF16),
            shape(plane.shape, BF16),
        ],
        scratch_shapes=[
            low(width, tokens), low(*vl.shape), low(*small.shape), low(*gl.shape), low(2, nz, c, r), low(2, nz, c, r),
            low(*ws.shape), low(n, width), low(n, width), buffer(ndp, nz * ws.shape[2], r),
            low(ndp - 1, nz, rows, c), buffer(nz, rows, c), buffer(ndp, n, r), low(ndp, n, r), low(ndp, n, r),
            buffer(ndp, n, r), low(ndp, n, r), low(ndp, n, r),
            low(lo - 1, nz, half, c), low(lo - 1, nz, rows - half, c), low(nz, rows, c), low(lo - 1, nz, rows, c),
            low(nz - 1, rows, c), low(nz, rows, c), buffer(ndp, nz, 16, c), buffer(nz, 16, c),
            buffer(8, width), buffer(nh - 1, 8, width), buffer(8, width), buffer(ndp - 1, 8, width),
            dma((7,)), dma((2, 2)),
            dma((lo - 1, nz)), dma((lo - 1, nz)), dma((lo - 1, nz)), dma((lo - 1, nz)),
            dma((nz,)), dma((nz,)), dma((lo - 1, nz)), dma((lo - 1, nz)),
            dma((nz,)), dma((nz,)), dma((ndp - 1,)), dma((ndp - 1,)), dma((nz,)), dma((nz,)),
            dma((1,)), dma((1,)), dma((1,)), dma((1,)), dma((1,)), dma((nh - 1,)), dma((nh - 1,)), dma((ndp - 1,)), dma((ndp - 1,)),
            dma((nz,)), dma((nz,)), dma((1,)),
        ],
        compiler_params=pltpu.CompilerParams(
            collective_id=2, has_side_effects=True, vmem_limit_bytes=63 * MIB
        ),
        cost_estimate=cost(4 * nz * c * tokens * width, 40 * MIB),
    )(nt, vl, small, gl, wg, wv, ws, x, cot, plane, gated, wo, table, gain, sums)

def shards(
    block_input, lengths, norm_gain, in_gate, in_value, in_states, in_steps,
    conv_value, conv_value_bias, conv_states, conv_states_bias,
    step_bias, decay_log, skip_gain, gate_gain, out_proj, cotangent,
):
    ndp, nh = lax.axis_size("dp"), lax.axis_size("head")
    nz, lo = nh // 2, ndp // 2
    own, width = block_input.shape
    tokens = 2 * own
    dp, head = lax.axis_index("dp"), lax.axis_index("head")
    core, zed = head % 2, head // 2
    dhi, dlo = dp // lo, dp % lo
    r, cols = in_gate.shape
    hs, sc, taps = step_bias.shape[0], in_states.shape[1], conv_value.shape[0]
    heads, inner, state, hw = hs * nz, cols * nz, sc * nz, cols // hs
    total = 2 * inner

    def sibling(v):
        return lax.ppermute(v, "head", [(i, i ^ 1) for i in range(nh)])

    def zshift(v, k):
        return lax.ppermute(v, "head", [(i, (i + 2 * k) % nh) for i in range(nh)])

    def zstep(v, k):
        return lax.ppermute(
            v, "head", [(i, i + 2 * k) for i in range(nh) if 0 <= i + 2 * k < nh]
        )

    def lo_shift(v, k):
        return lax.ppermute(
            v, "dp", [(h * lo + i, h * lo + (i + k) % lo) for h in range(2) for i in range(lo)]
        )

    def hi_swap(v):
        return lax.ppermute(v, "dp", [(i, (i + lo) % ndp) for i in range(ndp)])

    def block(g, d, start, count):
        return lax.dynamic_slice(g, (d, 0, start, 0), (1, nz, count, g.shape[3]))[0]

    def slot(k):
        return (dlo + k) % lo

    def scatter_sends(g):
        rows = g.shape[2]
        half = rows // 32 * 16
        diagonal = [(1 - dhi) * lo + slot(k) for k in range(1, lo)]
        return [(block(g, d, 0, half), block(g, d, half, rows - half)) for d in diagonal]

    def scatter_first(sends):
        return [lo_shift(a, k + 1) for k, (a, _) in enumerate(sends)], [hi_swap(b) for _, b in sends]

    def scatter(g, first, second, hold=None):
        rows = g.shape[2]
        half = rows // 32 * 16
        peer = (1 - dhi) * lo + dlo
        top = block(g, peer, 0, half).astype(F32)
        for v in first:
            top = top + v.astype(F32)
        sents = [jnp.concatenate([top.astype(BF16), block(g, peer, half, rows - half)], axis=1)]
        for k in range(1, lo):
            d = dhi * lo + slot(k)
            low = block(g, d, half, rows - half).astype(F32) + second[k - 1].astype(F32)
            sents.append(jnp.concatenate([block(g, d, 0, half), low.astype(BF16)], axis=1))
        if hold is not None:
            sents, hold = lax.optimization_barrier((sents, hold))
        total_here = block(g, dp, 0, rows).astype(F32) + hi_swap(sents[0]).astype(F32)
        for k in range(1, lo):
            total_here = total_here + lo_shift(sents[k], k).astype(F32)
        return total_here.astype(BF16), hold

    heads_par = jnp.stack([step_bias, decay_log, skip_gain])
    (
        g_value, g_small, g_gate, g_out, everyone, normed_t, cot_t, value_pre, gate_pre, x_t, states_pre, bc,
        seg, match, ahead, v_steps, dt, a2, scale_back, rates, whole, sin,
    ) = gather_project(
        ndp, nz, sc, hs, hw, block_input, cotangent, in_value, in_gate, out_proj, in_states, in_steps,
        conv_value, conv_value_bias[None], gate_gain[None], heads_par, conv_states, conv_states_bias[None],
        norm_gain[None, :], lengths,
    )
    sin = sin.reshape(inner, state)
    x_t = x_t.reshape(inner, tokens)
    value_pre = value_pre.reshape(inner, LH + tokens)
    gate_pre = gate_pre.reshape(inner, tokens)
    bm, cm = bc[0], bc[1]
    places = [(i // hs) * 8 + i % hs for i in range(heads)]
    pars = lax.dynamic_index_in_dim(everyone.reshape(nz, 2, 16, cols), core, 1, keepdims=False)
    taps_t = pars[:, :8].transpose(0, 2, 1).reshape(inner, 8)
    gain = taps_t[:, 5:6]
    skip = pars[:, 8, :8].reshape(nz * 8)
    y_t, st = scan_forward(places, x_t, dt, a2, seg, bm, cm, sin, skip[:, None])

    gated, h1, sums = mix(g_out, cot_t, y_t, gate_pre, gain)
    sums = sums + sibling(sums)
    own_sums = lax.dynamic_slice_in_dim(sums, core * own, own, 1)
    out_blocks = weight_grad(ndp, cot_t, gated, sums=sums)
    out_sends = scatter_sends(out_blocks)
    y_late, out_sends = lax.optimization_barrier((y_t, out_sends))
    dy_t, gate_low, mix_cols, gate_blocks, rin = unmix(
        ndp, nz, hs, hw, y_late, gate_pre, h1, x_t, gain, sums, scale_back, cm, whole, normed_t
    )
    rin = rin.reshape(inner, state)
    gate_first = scatter_first(scatter_sends(gate_blocks))
    plane_out, dy_t = scatter(out_blocks, *scatter_first(out_sends), hold=dy_t)
    dx_t, db, dc, xdx, da = scan_backward(
        places, x_t, dy_t, y_t, dt, a2, seg, bm, cm, st, rin, skip[:, None]
    )

    gate_first, dx_t = lax.optimization_barrier((gate_first, dx_t))
    plane_gate, _ = scatter(gate_blocks, *gate_first)
    value_low, small_low, table, early_out = conv_back(
        nz, sc, dx_t, value_pre, db, dc, states_pre, plane_out, everyone, match, ahead, v_steps, dt, xdx, da, rates, mix_cols
    )
    sum_value, input_grad, norm_rows, row, out, early_gate = last_steps(
        ndp, nz, sc, normed_t, value_low, small_low, gate_low, g_gate, g_value, g_small, block_input, cotangent,
        plane_gate, gated, g_out, table, norm_gain[None, :], own_sums,
    )
    sum_out = early_out.astype(F32).sum(axis=0)
    sum_gate = early_gate.astype(F32).sum(axis=0)
    own_lanes = lax.dynamic_slice_in_dim(row[6:14], zed * 8, hs, 1)
    states_row = lax.dynamic_slice_in_dim(row[9:14], core * sc, sc, 1)
    return (
        out,
        input_grad,
        norm_rows[0],
        sum_gate,
        sum_value[:r],
        sum_value[r : r + sc].T,
        sum_value[r + sc : r + sc + hs].T,
        row[:taps],
        row[4],
        states_row[:taps],
        states_row[taps],
        own_lanes[0],
        own_lanes[1],
        row[8].reshape(hs, hw).sum(axis=1),
        row[5],
        sum_out,
    )


def solution(mesh):
    both = P(("dp", "head"), None)
    grid = P("dp", "head")
    return jax.shard_map(
        shards,
        mesh=mesh,
        in_specs=(
            both, P("dp", None), P(), grid, grid, grid, grid,
            P(None, "head"), P("head"), P(None, "head"), P("head"),
            P("head"), P("head"), P("head"), P("head"), grid, both,
        ),
        out_specs=(
            both, both, P(), grid, grid, grid, grid,
            P(None, "head"), P("head"), P(None, "head"), P("head"),
            P("head"), P("head"), P("head"), P("head"), grid,
        ),
        check_vma=False,
    )
```

```python
import functools

import jax
import jax.numpy as jnp
from jax import lax
from jax.experimental import pallas as pl
from jax.experimental.pallas import tpu as pltpu
from jax.sharding import PartitionSpec as P

EPSILON = 1e-05
HALO = 16
LH = 128
QB = 128
LOG2E = 1.4426950408889634
TINY = 1e-30
F32 = jnp.float32
BF16 = jnp.bfloat16
MESH = pl.DeviceIdType.MESH
MIB = 1024 * 1024


def mm(a, b, ca, cb):
    return lax.dot_general(a, b, (((ca,), (cb,)), ((), ())), preferred_element_type=F32)


def shape(dims, dtype):
    return jax.ShapeDtypeStruct(dims, dtype)


def params(limit=48):
    return pltpu.CompilerParams(vmem_limit_bytes=limit * MIB)


def cost(flops, nbytes):
    return pl.CostEstimate(flops=int(flops), transcendentals=0, bytes_accessed=int(nbytes))


def chunk_of(count, most, unit):
    best = unit
    for size in range(unit, most + 1, unit):
        if count % size == 0:
            best = size
    return best


def sigmoid(v):
    return 0.5 * jnp.tanh(0.5 * v) + 0.5


def lane_chunks(count, most=256):
    return [pl.ds(base, most) for base in range(0, count, most)]


def folded(v):
    out = v[:, 0:128]
    for base in range(128, v.shape[1], 128):
        out = out + v[:, base : base + 128]
    return out


def lane_cumsum(v, reverse=False):
    size = v.shape[1]
    lane = lax.broadcasted_iota(jnp.int32, v.shape, 1)
    step = 1
    while step < size:
        if reverse:
            moved = pltpu.roll(v, size - step, 1)
            v = v + jnp.where(lane < size - step, moved, 0.0)
        else:
            moved = pltpu.roll(v, step, 1)
            v = v + jnp.where(lane >= step, moved, 0.0)
        step *= 2
    return v


def block_terms(dt, a2, seg_ref, b):
    cum = lane_cumsum(a2)
    logdt = jnp.log2(jnp.maximum(dt, TINY))
    source = cum - logdt
    q = dt.shape[1]
    prev = seg_ref[0:1, pl.ds(pl.multiple_of(b * q, q), q)][:, q - 1 :]
    segr = seg_ref[0:1, pl.ds(pl.multiple_of(LH + b * q, q), q)]
    segc = jnp.broadcast_to(segr, (q, q)).T
    last = cum[:, q - 1 : q]
    final = segr[:, q - 1 : q]
    reach = jnp.where(segr == prev, jnp.exp2(cum), 0.0)
    tail = jnp.where(segr == final, jnp.exp2(last - source), 0.0)
    kept = jnp.where(final == prev, jnp.exp2(last), 0.0)
    pad = (-dt.shape[0]) % 128
    padded = jnp.concatenate([source, jnp.zeros((pad, q), F32)], axis=0) if pad else source
    columns = padded.T
    row_s = lax.broadcasted_iota(jnp.int32, (q, q), 0)
    col_t = lax.broadcasted_iota(jnp.int32, (q, q), 1)
    bias = jnp.where((row_s <= col_t) & (segc == segr), 0.0, -1e30)
    return cum, columns, reach, tail, kept, bias


def scan_fwd_kernel(
    places, width,
    x_ref, dt_ref, a_ref, seg_ref, b_ref, c_ref, sin_ref, skip_ref,
    y_ref, st_ref, state,
):
    @pl.when(pl.program_id(0) == 0)
    def _():
        state[...] = sin_ref[...].astype(F32)

    cum, columns, reach, tail, kept, bias = block_terms(dt_ref[...], a_ref[...], seg_ref, pl.program_id(0))
    gt = mm(b_ref[...], c_ref[...], 1, 1)
    low = state[...].astype(BF16)
    st_ref[0] = low
    y_ref[...] = mm(low, c_ref[...], 1, 1)
    for i, h in enumerate(places):
        rows = slice(i * width, (i + 1) * width)
        weights = jnp.exp2(cum[h : h + 1] - columns[:, h : h + 1] + bias)
        mix = (gt * weights).astype(BF16)
        xh = x_ref[rows]
        xf = xh.astype(F32)
        y_ref[rows] = mm(xh, mix, 1, 0) + y_ref[rows] * reach[h : h + 1] + skip_ref[h, 0] * xf
        xs = (xf * tail[h : h + 1]).astype(BF16)
        state[rows] = state[rows] * kept[h : h + 1] + mm(xs, b_ref[...], 1, 0)


def scan_bwd_kernel(
    places, width,
    x_ref, dy_ref, y_ref, dt_ref, a_ref, seg_ref, b_ref, c_ref,
    st_ref, rin_ref, skip_ref,
    dx_ref, db_ref, dc_ref, xdx_ref, da_ref,
    adjoint, xs_all, ds_all, rows_v, rows_c, rows_r, rows_e,
):
    @pl.when(pl.program_id(0) == 0)
    def _():
        adjoint[...] = rin_ref[...].astype(F32)

    cum, columns, reach, tail, kept, bias = block_terms(
        dt_ref[...], a_ref[...], seg_ref, pl.num_programs(0) - 1 - pl.program_id(0)
    )
    bk, ck = b_ref[...], c_ref[...]
    gt = mm(bk, ck, 1, 1)
    r_low = adjoint[...].astype(BF16)
    s_low = st_ref[0]
    dx_ref[...] = mm(r_low, bk, 1, 1)
    dg = jnp.zeros(gt.shape, F32)
    for i, h in enumerate(places):
        rows = slice(i * width, (i + 1) * width)
        weights = jnp.exp2(cum[h : h + 1] - columns[:, h : h + 1] + bias)
        mix = (gt * weights).astype(BF16)
        xh, dyh = x_ref[rows], dy_ref[rows]
        xf, dyf = xh.astype(F32), dyh.astype(F32)
        pairs = mm(xh, dyh, 0, 0)
        dg = dg + weights * pairs
        inner = mm(dyh, mix, 1, 1)
        outer = dx_ref[rows] * tail[h : h + 1]
        skip = skip_ref[h, 0]
        rows_v[h : h + 1] = jnp.sum(xf * outer, axis=0, keepdims=True)
        rows_c[h : h + 1] = jnp.sum(xf * inner, axis=0, keepdims=True)
        rows_r[h : h + 1] = jnp.sum(dyf * (y_ref[rows] - skip * xf), axis=0, keepdims=True)
        dx_ref[rows] = inner + outer + skip * dyf
        xs_all[rows] = (xf * tail[h : h + 1]).astype(BF16)
        ds = (dyf * reach[h : h + 1]).astype(BF16)
        ds_all[rows] = ds
        carried = adjoint[rows] * kept[h : h + 1]
        rows_e[h : h + 1] = jnp.sum(carried * s_low[rows].astype(F32), axis=0, keepdims=True)
        adjoint[rows] = carried + mm(ds, ck, 1, 0)
    dgl = dg.astype(BF16)
    db_ref[...] = mm(xs_all[...], r_low, 0, 0) + mm(dgl, ck, 1, 0)
    dc_ref[...] = mm(ds_all[...], s_low, 0, 0) + mm(dgl, bk, 0, 0)
    v, c = rows_v[...], rows_c[...]
    xdx_ref[...] = v + c
    ends = jnp.sum(rows_e[...], axis=1, keepdims=True)
    da_ref[...] = lane_cumsum(rows_r[...] - c, True) + (lane_cumsum(v) - v) + ends


def scan_specs(inner, heads, state, nb, flip):
    def at(b):
        return nb - 1 - b if flip else b

    lanes = pl.BlockSpec((inner, QB), lambda b: (0, at(b)))
    per_head = pl.BlockSpec((heads, QB), lambda b: (0, at(b)))
    seg = pl.BlockSpec((8, LH + nb * QB), lambda b: (0, 0))
    nat = pl.BlockSpec((QB, state), lambda b: (at(b), 0))
    full = pl.BlockSpec((inner, state), lambda b: (0, 0))
    skip = pl.BlockSpec(memory_space=pltpu.SMEM)
    st = pl.BlockSpec((1, inner, state), lambda b: (at(b), 0, 0))
    return lanes, per_head, seg, nat, full, skip, st


def scan_forward(places, x, dt, a2, seg, bm, cm, sin, skip):
    heads, tokens = dt.shape
    inner, state = x.shape[0], bm.shape[1]
    nb = tokens // QB
    lanes, per_head, sg, nat, full, sk, st = scan_specs(inner, heads, state, nb, False)
    return pl.pallas_call(
        functools.partial(scan_fwd_kernel, places, inner // len(places)),
        grid=(nb,),
        in_specs=[lanes, per_head, per_head, sg, nat, nat, full, sk],
        out_specs=[lanes, st],
        out_shape=[
            jax.ShapeDtypeStruct((inner, tokens), F32),
            jax.ShapeDtypeStruct((nb, inner, state), BF16),
        ],
        scratch_shapes=[pltpu.VMEM((inner, state), F32)],
        compiler_params=params(),
        cost_estimate=pl.CostEstimate(
            flops=20 * inner * tokens * state, transcendentals=0, bytes_accessed=10 * x.size
        ),
    )(x, dt, a2, seg, bm, cm, sin, skip)


def scan_backward(places, x, dy, y, dt, a2, seg, bm, cm, st_in, rin, skip):
    heads, tokens = dt.shape
    inner, state = x.shape[0], bm.shape[1]
    nb = tokens // QB
    lanes, per_head, sg, nat, full, sk, st = scan_specs(inner, heads, state, nb, True)
    return pl.pallas_call(
        functools.partial(scan_bwd_kernel, places, inner // len(places)),
        grid=(nb,),
        in_specs=[lanes, lanes, lanes, per_head, per_head, sg, nat, nat, st, full, sk],
        out_specs=[lanes, nat, nat, per_head, per_head],
        out_shape=[
            jax.ShapeDtypeStruct((inner, tokens), F32),
            jax.ShapeDtypeStruct((tokens, state), F32),
            jax.ShapeDtypeStruct((tokens, state), F32),
            jax.ShapeDtypeStruct((heads, tokens), F32),
            jax.ShapeDtypeStruct((heads, tokens), F32),
        ],
        scratch_shapes=[
            pltpu.VMEM((inner, state), F32),
            pltpu.VMEM((inner, QB), BF16),
            pltpu.VMEM((inner, QB), BF16),
            pltpu.VMEM((heads, QB), F32),
            pltpu.VMEM((heads, QB), F32),
            pltpu.VMEM((heads, QB), F32),
            pltpu.VMEM((heads, state), F32),
        ],
        compiler_params=params(),
        cost_estimate=pl.CostEstimate(
            flops=60 * inner * tokens * state, transcendentals=0, bytes_accessed=16 * x.size
        ),
    )(x, dy, y, dt, a2, seg, bm, cm, st_in, rin, skip)

def gather_kernel(
    ndp, nz, sc, hs, hw,
    x_ref, cot_ref, wv_in, wg_in, wo_in,
    states_ref, stepw_ref, cv_ref, cvb_ref, gg1_ref, heads_ref, cs_ref, csb_ref, gain_ref, len_ref,
    gv_ref, gs_ref, gg_ref, go_ref, pars_ref, nt_ref, ct_ref, vpre_ref, gpre_ref, vt_ref, st_ref, bc_ref,
    seg_ref, match_ref, ahead_ref, v_ref, dt_ref, a_ref, scale_ref, rates_ref, whole_ref, sin_ref,
    xbuf, nt, cbuf, ct, wv_ref, wg_ref, wo_ref, ws_ref, small_own, small_sib, par_ref, wvm, wsm, pvm, cols,
    scols, shifts, spre, st_low, vpre, gpre, vt,
    scaled, tails, fresh, hop_out, hop_in,
    z_send, full_recv, near_send, far_send, far_recv, misc_send, misc_recv, par_send, par_recv, local, load, out_sem,
    hop_send, hop_recv,
):
    nh, lo = 2 * nz, ndp // 2
    n, width = x_ref.shape
    tokens = 2 * n
    r, c = wv_in.shape
    dp, head = lax.axis_index("dp"), lax.axis_index("head")
    core, zed = lax.rem(head, 2), lax.div(head, 2)
    dhi, dlo = lax.div(dp, lo), lax.rem(dp, lo)
    sib = zed * 2 + 1 - core
    hi_peer = (1 - dhi) * lo + dlo
    lo_slots = [lax.rem(dlo + k, lo) for k in range(1, lo)]
    lo_peers = [dhi * lo + s for s in lo_slots]

    def half(rows, i):
        return pl.ds(0, rows // 32 * 16) if i == 0 else pl.ds(rows // 32 * 16, rows - rows // 32 * 16)

    order = [1] + [nz - 1] * (nz > 2) + list(range(2, nz - 1))

    barrier = pltpu.get_barrier_semaphore()
    partners = [(dp, lax.rem(head + k, nh)) for k in range(1, nh)]
    partners += [(p, head) for p in lo_peers + [hi_peer]]
    for partner in partners:
        pl.semaphore_signal(barrier, inc=1, device_id=partner, device_id_type=MESH)
    pl.semaphore_wait(barrier, len(partners))

    def remote(src, dst, send, recv, device):
        pltpu.make_async_remote_copy(
            src_ref=src, dst_ref=dst, send_sem=send, recv_sem=recv, device_id=device, device_id_type=MESH
        ).start()

    def wait_for(ref, sem):
        pltpu.make_async_copy(ref, ref, sem).wait()

    def along_z(m, own, slot):
        for k in range(1, nz):
            remote(
                own, slot, z_send.at[m, k], full_recv.at[m, dp, zed], (dp, lax.rem(zed + k, nz) * 2 + core)
            )

    def near(m, slots, zi, own=None):
        z = lax.rem(zed + zi, nz)
        if own is None:
            wait_for(slots.at[dp, z], full_recv.at[m, dp, z])
        src = slots.at[dp, z] if own is None else own
        for i, p in enumerate(lo_peers + [hi_peer]):
            remote(src, slots.at[dp, z], near_send.at[m, zi, i], full_recv.at[m, dp, z], (p, head))

    def far(m, slots, zi):
        z = lax.rem(zed + zi, nz)
        wait_for(slots.at[hi_peer, z], full_recv.at[m, hi_peer, z])
        for i, p in enumerate(lo_peers):
            part = slots.at[hi_peer, z, half(slots.shape[2], 0)]
            remote(part, part, far_send.at[m, zi, i], far_recv.at[m, hi_peer, z, 0], (p, head))
        for i, d in enumerate(lo_peers):
            wait_for(slots.at[d, z], full_recv.at[m, d, z])
            part = slots.at[d, z, half(slots.shape[2], 1)]
            remote(part, part, far_send.at[m, zi, lo - 1 + i], far_recv.at[m, d, z, 1], (hi_peer, head))

    def fetch(m, slots, vm, z):
        for s in lo_slots:
            d = (1 - dhi) * lo + s
            for i in range(2):
                wait_for(slots.at[d, z, half(slots.shape[2], i)], far_recv.at[m, d, z, i])
        for d in range(ndp):
            pltpu.make_async_copy(slots.at[d, z], vm.at[z, d], load.at[m, z, d]).start()

    def fetched(m, slots, vm, z):
        for d in range(ndp):
            pltpu.make_async_copy(slots.at[d, z], vm.at[z, d], load.at[m, z, d]).wait()

    def lanes(v, before):
        parts = [jnp.zeros((v.shape[0], before), F32)] * (before > 0) + [v.astype(F32)]
        return jnp.concatenate(parts + [jnp.zeros((v.shape[0], 128 - before - v.shape[1]), F32)], axis=1)

    wv_ref[...] = wv_in[...].T
    along_z(0, wv_ref, gv_ref.at[dp, zed])
    near(0, gv_ref, 0, wv_ref)
    own_states = states_ref[...].astype(F32)
    first_core = (core == 0).astype(F32)
    ws_ref[...] = jnp.concatenate(
        [own_states * first_core, own_states * (1.0 - first_core), stepw_ref[...].astype(F32),
         jnp.zeros((16 - hs, r), F32)], axis=0,
    ).astype(BF16)
    remote(ws_ref, small_sib, misc_send.at[0], misc_recv.at[0], (dp, sib))
    own_rows = pl.ds(HALO + core * n, n)
    remote(x_ref, xbuf.at[own_rows], misc_send.at[1], misc_recv.at[1], (dp, sib))

    @pl.when((core == 1) & (zed < nz - 1))
    def _():
        for i in range(2):
            remote(
                x_ref.at[pl.ds(n - HALO, HALO)], xbuf.at[pl.ds(0, HALO)], misc_send.at[3 + i], misc_recv.at[3],
                (dp, (zed + 1) * 2 + i),
            )

    wg_ref[...] = wg_in[...].T
    wo_ref[...] = wo_in[...].T
    mine = [
        pltpu.make_async_copy(x_ref, xbuf.at[own_rows], local.at[0]),
        pltpu.make_async_copy(wv_ref, gv_ref.at[dp, zed], local.at[1]),
        pltpu.make_async_copy(wg_ref, gg_ref.at[dp, zed], local.at[2]),
        pltpu.make_async_copy(cot_ref, cbuf.at[pl.ds(core * n, n)], local.at[3]),
        pltpu.make_async_copy(wo_ref, go_ref.at[dp, zed], local.at[4]),
    ]
    for copy in mine:
        copy.start()

    wait_for(small_sib, misc_recv.at[0])
    line = lax.broadcasted_iota(jnp.int32, small_own.shape, 0)
    low_line = (1 - core) * sc
    theirs = (line >= low_line) & (line < low_line + sc)
    small_own[...] = jnp.where(
        theirs, small_sib[...].astype(F32), ws_ref[...].astype(F32)
    ).astype(BF16)
    along_z(1, small_own, gs_ref.at[dp, zed])
    near(1, gs_ref, 0, small_own)
    own_small = pltpu.make_async_copy(small_own, gs_ref.at[dp, zed], local.at[7])
    own_small.start()
    par_ref[...] = jnp.zeros(par_ref.shape, F32)
    par_ref[0:4] = cv_ref[...]
    par_ref[4:5] = cvb_ref[...]
    par_ref[5:6] = gg1_ref[...]
    par_ref[6:9, 0:128] = lanes(heads_ref[...], 0)
    par_ref[9:13, 0:128] = pltpu.roll(lanes(cs_ref[...], 0), core * sc, 1)
    par_ref[13:14, 0:128] = pltpu.roll(lanes(csb_ref[...], 0), core * sc, 1)
    own_par = pltpu.make_async_copy(par_ref, pars_ref.at[head], local.at[5])
    own_par.start()
    for k in range(1, nh):
        remote(par_ref, pars_ref.at[head], par_send.at[k], par_recv.at[head], (dp, lax.rem(head + k, nh)))
    remote(cot_ref, cbuf.at[pl.ds(core * n, n)], misc_send.at[2], misc_recv.at[2], (dp, sib))

    span = LH + tokens
    ends = [len_ref[0, 0]]
    for k in range(1, len_ref.shape[1]):
        ends.append(ends[-1] + len_ref[0, k])

    def segment(at):
        number = sum([(at >= end).astype(F32) for end in ends[1:]], (at >= ends[0]).astype(F32))
        return jnp.where((at < 0) | (at >= nz * tokens), -1.0, number)

    at = zed * tokens - LH + lax.broadcasted_iota(jnp.int32, (8, span), 1)
    tap = lax.broadcasted_iota(jnp.int32, (8, span), 0)
    number = segment(at)
    seg_ref[...] = number
    valid = (tap < 4) & (at >= zed * tokens)
    match_ref[...] = jnp.where(valid & (segment(at - 3 + tap) == number), 1.0, 0.0)
    ahead_ref[...] = jnp.where((tap < 4) & (segment(at + 3 - tap) == number), 1.0, 0.0)[:, LH:]

    def normalise(start, count):
        rows = xbuf[pl.ds(start, count), :].astype(F32)
        inverse = lax.rsqrt(jnp.mean(rows * rows, axis=1, keepdims=True) + EPSILON)
        return (rows * inverse * gain_ref[...]).astype(BF16)

    def normalise_half(which):
        @pl.loop(0, n // 128)
        def _(i):
            at = pl.multiple_of(which * n + i * 128, 128)
            nt[:, pl.ds(pl.multiple_of(LH + at, 128), 128)] = normalise(pl.multiple_of(HALO + at, 16), 128).T

    def turn(which):
        @pl.loop(0, n // 128)
        def _(i):
            at = pl.multiple_of(which * n + i * 128, 128)
            ct[:, pl.ds(at, 128)] = cbuf[pl.ds(at, 128), :].T

    mine[0].wait()
    normalise_half(core)
    near(0, gv_ref, order[0])
    wait_for(x_ref, misc_recv.at[1])
    normalise_half(1 - core)
    for zi in order[1:]:
        near(0, gv_ref, zi)
    along_z(2, wg_ref, gg_ref.at[dp, zed])
    for zi in order:
        near(1, gs_ref, zi)

    @pl.when(zed > 0)
    def _():
        wait_for(xbuf.at[pl.ds(0, HALO)], misc_recv.at[3])

    @pl.when(zed == 0)
    def _():
        xbuf[0:HALO, :] = jnp.zeros((HALO, width), BF16)

    before = normalise(0, HALO).astype(F32)
    nt[:, 0:LH] = jnp.concatenate([jnp.zeros((LH - HALO, width), F32), before], axis=0).astype(BF16).T
    out_nt = pltpu.make_async_copy(nt.at[:, pl.ds(LH, tokens)], nt_ref, out_sem.at[3 * nz])
    out_nt.start()
    far(0, gv_ref, 0)
    far(1, gs_ref, 0)
    mine[3].wait()
    turn(core)
    for zi in order:
        far(0, gv_ref, zi)
        far(1, gs_ref, zi)
    near(2, gg_ref, 0, wg_ref)

    for k in range(1, nh):
        other = lax.rem(head + k, nh)
        wait_for(pars_ref.at[other], par_recv.at[other])
    own_par.wait()
    get_pars = pltpu.make_async_copy(pars_ref, pvm, local.at[5])
    get_pars.start()
    wait_for(cot_ref, misc_recv.at[2])
    turn(1 - core)
    get_pars.wait()
    out_ct = pltpu.make_async_copy(ct, ct_ref, out_sem.at[3 * nz + 1])
    out_ct.start()

    own_small.wait()
    mine[1].wait()
    for z in range(nz):
        fetch(1, gs_ref, wsm, z)
    for z in range(nz):
        fetch(0, gv_ref, wvm, z)
    place = lax.broadcasted_iota(jnp.int32, (256, 128), 0) - lax.broadcasted_iota(jnp.int32, (256, 128), 1)

    @pl.loop(0, tokens // 128)
    def _(b):
        at = pl.ds(pl.multiple_of(LH + b * 128, 128), 128)
        for k in range(3):
            shifts[b, :, k * 128 : k * 128 + 128] = jnp.where(
                place == 125 + k, match_ref[k : k + 1, at], 0.0
            ).astype(BF16)

    lanes_chunk = chunk_of(span, 384, 128)

    def by_width(weights, z):
        return jnp.concatenate([weights[z, d] for d in range(ndp)], axis=1)

    def shift(source, count, rest=None):
        @pl.loop(0, tokens // 128)
        def _(b):
            wide = pl.ds(pl.multiple_of(b * 128, 128), 256)
            moved = mm(source[:, wide], shifts[b], 1, 0)
            if rest is not None:
                moved = moved + mm(rest[:, wide], shifts[b], 1, 0)
            for k in range(3):
                gpre[k, 0:count, pl.ds(pl.multiple_of(b * 128, 128), 128)] = moved[:, k * 128 : k * 128 + 128]

    def convolved(source, taps, rows, base, rest=None):
        at = pl.ds(base, 256)
        here = source[rows, pl.ds(LH + base, 256)].astype(F32)
        if rest is not None:
            here = here + rest[rows, pl.ds(LH + base, 256)].astype(F32)
        pre = taps[:, 3:4] * here + taps[:, 4:5]
        for k in range(3):
            pre = pre + taps[:, k : k + 1] * gpre[k, rows, at]
        return pre * sigmoid(pre)

    for z in range(nz):
        fetched(1, gs_ref, wsm, z)

    @pl.loop(0, span // lanes_chunk)
    def _(i):
        at = pl.ds(pl.multiple_of(i * lanes_chunk, 128), lanes_chunk)
        left = jnp.concatenate([by_width(wsm, z) for z in range(nz)], axis=0)
        spre[:, at] = mm(left, nt[:, at], 1, 0)

    sr = wsm.shape[2]
    for z in range(nz):
        part = slice(z * 2 * sc, (z + 1) * 2 * sc)
        here = spre[z * sr : z * sr + 2 * sc, :]
        high = here.astype(BF16)
        st_ref[part, :] = high
        st_low[part, :] = (here - high.astype(F32)).astype(BF16)
        v_ref[z * 8 : z * 8 + 8, :] = spre[z * sr + 2 * sc : z * sr + 2 * sc + 8, LH:]
        both = pvm[2 * z, 8:16, 0:128] + pvm[2 * z + 1, 8:16, 0:128]
        scols[part, :] = both.T[0 : 2 * sc, 1:6]
    bc_rows = 2 * sc * nz
    shift(st_ref, bc_rows, st_low)

    @pl.loop(0, bc_rows // 32, unroll=2)
    def _(g):
        rows = pl.ds(pl.multiple_of(g * 32, 32), 32)
        taps = scols[rows, :]
        for base in range(0, tokens, 256):
            scaled[rows, pl.ds(base, 256)] = convolved(st_ref, taps, rows, base, st_low).astype(BF16)

    @pl.loop(0, tokens // 128)
    def _(b):
        at = pl.ds(pl.multiple_of(b * 128, 128), 128)
        for i in range(2):
            bc_ref[i, at, :] = scaled[i * 128 : i * 128 + 128, at].T

    columns = [pvm[2 * z + core, 0:16, 0:128].T[0:8] for z in range(nz)]

    def column(k):
        return jnp.concatenate([v[:, k : k + 1] for v in columns], axis=0)

    v = v_ref[...] + column(6)
    v_ref[...] = v
    dt = jnp.maximum(v, 0.0) + jnp.log1p(jnp.exp(-jnp.abs(v)))
    dt_ref[...] = dt
    rates = -jnp.exp(column(7))
    rates_ref[...] = jnp.broadcast_to(rates, rates_ref.shape)
    a2 = dt * (rates * LOG2E)
    a_ref[...] = a2
    segr = seg_ref[0:1, LH:]
    last, first = segr[:, tokens - 1 :], seg_ref[0:1, LH - 1 : LH]
    before = lane_cumsum(a2)
    through = before[:, tokens - 1 :]
    scale_ref[...] = jnp.where(segr == first, jnp.exp2(before), 0.0)
    whole_ref[...] = jnp.broadcast_to(jnp.where(last == first, jnp.exp2(through), 0.0), whole_ref.shape)
    tail = jnp.where(segr == last, jnp.exp2(lane_cumsum(a2, True) - a2) * dt, 0.0)
    tails[...] = tail

    for z in range(nz):
        fetched(0, gv_ref, wvm, z)

    @pl.loop(0, nz)
    def _(z):
        cols[...] = pvm[2 * z + core, 0:8, :].T

        @pl.loop(0, span // lanes_chunk)
        def _(i):
            at = pl.ds(pl.multiple_of(i * lanes_chunk, 128), lanes_chunk)
            vpre[z, :, at] = mm(by_width(wvm, z), nt[:, at], 1, 0).astype(BF16)

        pltpu.make_async_copy(vpre.at[z], vpre_ref.at[z], out_sem.at[z]).start()
        shift(vpre.at[z], c)

        @pl.loop(0, c // 32, unroll=2)
        def _(g):
            rows = pl.ds(pl.multiple_of(g * 32, 32), 32)
            taps = cols[rows, :]
            decay = pl.ds(z * 8 + g // (hw // 32), 1)
            for base in range(0, tokens, 256):
                at = pl.ds(base, 256)
                low = convolved(vpre.at[z], taps, rows, base).astype(BF16)
                vt[z, rows, at] = low
                scaled[rows, at] = (low.astype(F32) * tails[decay, at]).astype(BF16)

        pltpu.make_async_copy(vt.at[z], vt_ref.at[z], out_sem.at[nz + z]).start()
        fresh[z] = mm(scaled[0:c, :], bc_ref[0], 1, 0)

        @pl.when(z < nz - 1)
        def _():
            near(2, gg_ref, z + 1)

        @pl.when(z > 0)
        def _():
            far(2, gg_ref, z - 1)

        @pl.when(z == 1)
        def _():
            along_z(3, wo_ref, go_ref.at[dp, zed])

    far(2, gg_ref, nz - 1)

    mine[2].wait()
    near(3, go_ref, 0, wo_ref)
    for z in range(nz):
        fetch(2, gg_ref, wvm, z)
    gate_chunk = chunk_of(tokens, 512, 128)

    def hop(i):
        if i:
            hop_arrived(i - 1)
            for z in range(nz):
                for h in range(hs):
                    at = slice(h * hw, (h + 1) * hw)
                    state = whole_ref[z * 8 + h : z * 8 + h + 1, :] * hop_in[i - 1, z, at, :].astype(F32)
                    hop_out[i, z, at, :] = (fresh[z, at, :] + state).astype(BF16)
        else:
            hop_out[0] = fresh[...].astype(BF16)

        @pl.when(zed < nz - 1)
        def _():
            remote(hop_out.at[i], hop_in.at[i], hop_send.at[i], hop_recv.at[i], (dp, (zed + 1) * 2 + core))

    def hop_arrived(i):
        @pl.when(zed > 0)
        def _():
            wait_for(hop_in.at[i], hop_recv.at[i])

        @pl.when(zed == 0)
        def _():
            hop_in[i] = jnp.zeros(hop_in.shape[1:], BF16)

    hops = nz // 2
    for i in range(hops):
        hop(i)
        if i == 0:
            for zi in order:
                near(3, go_ref, zi)
        for z in (2 * i, 2 * i + 1):
            fetched(2, gg_ref, wvm, z)

        @pl.loop(2 * i, 2 * i + 2)
        def _(z):
            @pl.loop(0, tokens // gate_chunk)
            def _(i):
                at = pl.multiple_of(i * gate_chunk, 128)
                right = nt[:, pl.ds(pl.multiple_of(LH + at, 128), gate_chunk)]
                gpre[z, 0:c, pl.ds(at, gate_chunk)] = mm(by_width(wvm, z), right, 1, 0)

            pltpu.make_async_copy(gpre.at[z, pl.ds(0, c)], gpre_ref.at[z], out_sem.at[2 * nz + z]).start()

    for zi in [0] + order:
        far(3, go_ref, zi)
    hop_arrived(hops - 1)
    sin_ref[...] = hop_in[hops - 1]

    @pl.when(zed < nz - 1)
    def _():
        for i in range(hops):
            wait_for(hop_out.at[i], hop_send.at[i])

    mine[4].wait()
    for z in range(nz):
        for s in lo_slots:
            d = (1 - dhi) * lo + s
            for i in range(2):
                wait_for(go_ref.at[d, z, half(c, i)], far_recv.at[3, d, z, i])
    sent = [wv_ref, small_own, wg_ref, wo_ref]
    for m in range(4):
        for k in range(1, nz):
            wait_for(sent[m], z_send.at[m, k])
    for m in range(4):
        for zi in range(nz):
            for i in range(lo):
                wait_for(sent[m], near_send.at[m, zi, i])
            for i in range(2 * (lo - 1)):
                wait_for(sent[m].at[half(sent[m].shape[0], i // (lo - 1))], far_send.at[m, zi, i])
    wait_for(ws_ref, misc_send.at[0])
    wait_for(x_ref, misc_send.at[1])
    wait_for(cot_ref, misc_send.at[2])
    for k in range(1, nh):
        wait_for(par_ref, par_send.at[k])

    @pl.when((core == 1) & (zed < nz - 1))
    def _():
        for i in range(2):
            wait_for(x_ref.at[pl.ds(n - HALO, HALO)], misc_send.at[3 + i])

    for z in range(nz):
        pltpu.make_async_copy(vpre.at[z], vpre_ref.at[z], out_sem.at[z]).wait()
        pltpu.make_async_copy(vt.at[z], vt_ref.at[z], out_sem.at[nz + z]).wait()
        pltpu.make_async_copy(gpre.at[z, pl.ds(0, c)], gpre_ref.at[z], out_sem.at[2 * nz + z]).wait()
    out_nt.wait()
    out_ct.wait()


def gather_project(
    ndp, nz, sc, hs, hw, x, cot, wv, wg, wo, states, stepw, cv, cvb, gg, heads, cs, csb, gain, lengths
):
    n, width = x.shape
    tokens = 2 * n
    r, c = wv.shape
    nh, lo, hops = 2 * nz, ndp // 2, nz // 2
    sr, most = 2 * sc + 16, max(c, 2 * sc * nz)
    anywhere = pl.BlockSpec(memory_space=pl.ANY)
    vmem = pl.BlockSpec(memory_space=pltpu.VMEM)
    dma = pltpu.SemaphoreType.DMA
    return pl.pallas_call(
        functools.partial(gather_kernel, ndp, nz, sc, hs, hw),
        in_specs=[anywhere] * 2 + [vmem] * 12 + [pl.BlockSpec(memory_space=pltpu.SMEM)],
        out_specs=[anywhere] * 10 + [vmem] * 12,
        out_shape=[
            shape((ndp, nz, c, r), BF16),
            shape((ndp, nz, sr, r), BF16),
            shape((ndp, nz, c, r), BF16),
            shape((ndp, nz, c, r), BF16),
            shape((nh, 16, c), F32),
            shape((width, tokens), BF16),
            shape((width, tokens), BF16),
            shape((nz, c, LH + tokens), BF16),
            shape((nz, c, tokens), F32),
            shape((nz, c, tokens), BF16),
            shape((2 * sc * nz, LH + tokens), BF16),
            shape((2, tokens, 128), BF16),
            shape((8, LH + tokens), F32),
            shape((8, LH + tokens), F32),
            shape((8, tokens), F32),
            shape((nz * 8, tokens), F32),
            shape((nz * 8, tokens), F32),
            shape((nz * 8, tokens), F32),
            shape((nz * 8, tokens), F32),
            shape((nz * 8, 128), F32),
            shape((nz * 8, 128), F32),
            shape((nz, c, 128), BF16),
        ],
        scratch_shapes=[
            pltpu.VMEM((HALO + tokens, width), BF16),
            pltpu.VMEM((width, LH + tokens), BF16),
            pltpu.VMEM((tokens, width), BF16),
            pltpu.VMEM((width, tokens), BF16),
            pltpu.VMEM((c, r), BF16),
            pltpu.VMEM((c, r), BF16),
            pltpu.VMEM((c, r), BF16),
            pltpu.VMEM((sr, r), BF16),
            pltpu.VMEM((sr, r), BF16),
            pltpu.VMEM((sr, r), BF16),
            pltpu.VMEM((16, c), F32),
            pltpu.VMEM((nz, ndp, c, r), BF16),
            pltpu.VMEM((nz, ndp, sr, r), BF16),
            pltpu.VMEM((nh, 16, c), F32),
            pltpu.VMEM((c, 8), F32),
            pltpu.VMEM((2 * sc * nz, 5), F32),
            pltpu.VMEM((tokens // 128, 256, 384), BF16),
            pltpu.VMEM((nz * sr, LH + tokens), F32),
            pltpu.VMEM((2 * sc * nz, LH + tokens), BF16),
            pltpu.VMEM((nz, c, LH + tokens), BF16),
            pltpu.VMEM((nz, most, tokens), F32),
            pltpu.VMEM((nz, c, tokens), BF16),
            pltpu.VMEM((most, tokens), BF16),
            pltpu.VMEM((nz * 8, tokens), F32),
            pltpu.VMEM((nz, c, 128), F32),
            pltpu.VMEM((hops, nz, c, 128), BF16),
            pltpu.VMEM((hops, nz, c, 128), BF16),
            dma((4, nz)),
            dma((4, ndp, nz)),
            dma((4, nz, lo)),
            dma((4, nz, 2 * (lo - 1))),
            dma((4, ndp, nz, 2)),
            dma((5,)),
            dma((4,)),
            dma((nh,)),
            dma((nh,)),
            dma((8,)),
            dma((3, nz, ndp)),
            dma((3 * nz + 2,)),
            dma((hops,)),
            dma((hops,)),
        ],
        compiler_params=pltpu.CompilerParams(
            collective_id=1, has_side_effects=True, vmem_limit_bytes=60 * MIB
        ),
        cost_estimate=cost(2 * tokens * width * nz * (2 * c + 128), 60 * MIB),
    )(x, cot, wv, wg, wo, states, stepw, cv, cvb, gg, heads, cs, csb, gain, lengths)

def mix_kernel(ndp, wo_ref, ct_ref, y_ref, g_ref, gain_ref, gated_ref, h1_ref, sums_ref, acc, low):
    c, tokens = y_ref.shape
    z = pl.program_id(0)
    chunk = chunk_of(tokens, 512, 128)

    @pl.loop(0, tokens // chunk)
    def _(i):
        at = pl.ds(pl.multiple_of(i * chunk, 128), chunk)
        left = jnp.concatenate([wo_ref[d, 0] for d in range(ndp)], axis=1)
        h1_ref[:, at] = mm(left, ct_ref[:, at], 1, 0)

    @pl.when(z == 0)
    def _():
        acc[...] = jnp.zeros(acc.shape, F32)

    @pl.loop(0, c // 16, unroll=2)
    def _(i):
        rows = pl.ds(pl.multiple_of(i * 16, 16), 16)
        scale = gain_ref[rows, :]
        for at in lane_chunks(tokens):
            g = g_ref[rows, at]
            mixed = y_ref[rows, at] * (g * sigmoid(g))
            gated = (mixed * scale).astype(BF16)
            low[rows, at] = gated
            square = mixed * mixed
            dots = gated.astype(F32) * h1_ref[rows, at]
            acc[0:8, at] += square[0:8] + square[8:16]
            acc[8:16, at] += dots[0:8] + dots[8:16]

    gated_ref[0] = low[...].T

    @pl.when(z == pl.num_programs(0) - 1)
    def _():
        sums_ref[0:1] = jnp.sum(acc[0:8], axis=0, keepdims=True)
        sums_ref[1:2] = jnp.sum(acc[8:16], axis=0, keepdims=True)
        sums_ref[2:8] = jnp.zeros((6, tokens), F32)


def mix(wo, ct, y, g, gain):
    ndp, nz, c, r = wo.shape
    width, tokens = ct.shape
    inner = nz * c
    block = pl.BlockSpec((c, tokens), lambda z: (z, 0))
    return pl.pallas_call(
        functools.partial(mix_kernel, ndp),
        grid=(nz,),
        in_specs=[
            pl.BlockSpec((ndp, 1, c, r), lambda z: (0, z, 0, 0)),
            pl.BlockSpec((width, tokens), lambda z: (0, 0)),
            block, block,
            pl.BlockSpec((c, 1), lambda z: (z, 0)),
        ],
        out_specs=[
            pl.BlockSpec((1, tokens, c), lambda z: (z, 0, 0)), block, pl.BlockSpec((8, tokens), lambda z: (0, 0)),
        ],
        out_shape=[shape((nz, tokens, c), BF16), shape((inner, tokens), F32), shape((8, tokens), F32)],
        scratch_shapes=[pltpu.VMEM((16, tokens), F32), pltpu.VMEM((c, tokens), BF16)],
        compiler_params=params(),
        cost_estimate=cost(2 * inner * tokens * width, 22 * inner * tokens),
    )(wo, ct, y, g, gain)


def unmix_kernel(
    ndp, nz, hs, hw, total,
    y_ref, g_ref, h1_ref, x_ref, gain_ref, sums_ref, scale_ref, cm_ref, whole_ref, nt_ref,
    dy_ref, gl_ref, cols_ref, grad_ref, rin_ref,
    scaled, acc, low, turned, back, hop_out, hop_in, hop_send, hop_recv,
):
    c = y_ref.shape[0]
    hops = nz // 2
    step = pl.program_id(0)
    dp, head = lax.axis_index("dp"), lax.axis_index("head")
    core, zed = lax.rem(head, 2), lax.div(head, 2)

    @pl.when(step == 0)
    def _():
        barrier = pltpu.get_barrier_semaphore()
        for k in range(1, nz):
            pl.semaphore_signal(
                barrier, inc=1, device_id=(dp, lax.rem(zed + k, nz) * 2 + core), device_id_type=MESH
            )
        pl.semaphore_wait(barrier, nz - 1)

    @pl.when(step < nz)
    def _():
        inverse = lax.rsqrt(sums_ref[0:1] / total + EPSILON)
        weight = sums_ref[1:2] * (inverse * inverse * inverse) / total

        @pl.loop(0, c // 16, unroll=2)
        def _(i):
            rows = pl.ds(pl.multiple_of(i * 16, 16), 16)
            gain = gain_ref[rows, :]
            head_row = pl.ds(i // (hw // 16), 1)
            gains, skips = [], []
            for at in lane_chunks(y_ref.shape[1]):
                y, g = y_ref[rows, at], g_ref[rows, at]
                sig = sigmoid(g)
                silu = g * sig
                mixed = y * silu
                gated_grad = h1_ref[rows, at] * inverse[:, at]
                mixed_grad = gated_grad * gain - weight[:, at] * mixed
                dy = (mixed_grad * silu).astype(BF16)
                dy_ref[rows, at] = dy
                low[rows, at] = (mixed_grad * y * (sig + silu * (1.0 - sig))).astype(BF16)
                dyf = dy.astype(F32)
                scaled[rows, at] = (dyf * scale_ref[head_row, at]).astype(BF16)
                gains.append(folded(gated_grad * mixed))
                skips.append(folded(dyf * x_ref[rows, at].astype(F32)))
            acc[0, rows, :] = sum(gains[1:], gains[0])
            acc[1, rows, :] = sum(skips[1:], skips[0])

        for k in range(2):
            cols_ref[0, k : k + 1] = jnp.sum(acc[k].T, axis=0, keepdims=True)
        cols_ref[0, 2:8] = jnp.zeros((6, c), F32)
        flipped = low[...].T
        gl_ref[0] = flipped
        turned[step] = flipped
        back[step] = mm(scaled[...], cm_ref[...], 1, 0)

    def hop_arrived(i, z):
        @pl.when(zed < nz - 1)
        def _():
            pltpu.make_async_copy(hop_in.at[i, z], hop_in.at[i, z], hop_recv.at[i, z]).wait()

        @pl.when(zed == nz - 1)
        def _():
            hop_in[i, z] = jnp.zeros(hop_in.shape[2:], BF16)

    def hop(i, z):
        if i:
            hop_arrived(i - 1, z)
            for h in range(hs):
                at = slice(h * hw, (h + 1) * hw)
                state = whole_ref[pl.ds(z * 8 + h, 1), :] * hop_in[i - 1, z, at, :].astype(F32)
                hop_out[i, z, at, :] = (back[z, at, :] + state).astype(BF16)
        else:
            hop_out[0, z] = back[z].astype(BF16)

        @pl.when(zed > 0)
        def _():
            pltpu.make_async_remote_copy(
                src_ref=hop_out.at[i, z], dst_ref=hop_in.at[i, z],
                send_sem=hop_send.at[i, z], recv_sem=hop_recv.at[i, z],
                device_id=(dp, (zed - 1) * 2 + core), device_id_type=MESH,
            ).start()

    @pl.when(step >= nz)
    def _():
        r = nt_ref.shape[0] // ndp
        right = turned[step - nz]
        for d in range(ndp):
            grad_ref[d, 0] = mm(nt_ref[d * r : (d + 1) * r, :], right, 1, 0).astype(BF16)

    for i in range(hops):
        @pl.when((step >= 2 * i) & (step < nz + 2 * i))
        def _(i=i):
            hop(i, step - 2 * i)

    @pl.when(step == 2 * nz - 1)
    def _():
        for z in range(nz):
            hop_arrived(hops - 1, z)
        rin_ref[...] = hop_in[hops - 1]

        @pl.when(zed > 0)
        def _():
            for i in range(hops):
                for z in range(nz):
                    pltpu.make_async_copy(hop_out.at[i, z], hop_out.at[i, z], hop_send.at[i, z]).wait()


def unmix(ndp, nz, hs, hw, y, g, h1, x, gain, sums, scale, cm, whole, nt):
    inner, tokens = y.shape
    c = inner // nz
    state = cm.shape[1]
    width = nt.shape[0]
    hops = nz // 2

    def first(s):
        return jnp.minimum(s, nz - 1)

    def second(s):
        return jnp.maximum(s - nz, 0)

    block = pl.BlockSpec((c, tokens), lambda s: (first(s), 0))
    dma = pltpu.SemaphoreType.DMA

    def fixed(v):
        return pl.BlockSpec(v.shape, lambda s: (0,) * v.ndim)

    return pl.pallas_call(
        functools.partial(unmix_kernel, ndp, nz, hs, hw, inner * 2),
        grid=(2 * nz,),
        in_specs=[
            block, block, block, block,
            pl.BlockSpec((c, 1), lambda s: (first(s), 0)),
            fixed(sums),
            pl.BlockSpec((8, tokens), lambda s: (first(s), 0)),
            fixed(cm), fixed(whole), fixed(nt),
        ],
        out_specs=[
            block,
            pl.BlockSpec((1, tokens, c), lambda s: (first(s), 0, 0)),
            pl.BlockSpec((1, 8, c), lambda s: (first(s), 0, 0)),
            pl.BlockSpec((ndp, 1, width // ndp, c), lambda s: (0, second(s), 0, 0)),
            pl.BlockSpec((nz, c, state), lambda s: (0, 0, 0)),
        ],
        out_shape=[
            shape((inner, tokens), BF16), shape((nz, tokens, c), BF16), shape((nz, 8, c), F32),
            shape((ndp, nz, width // ndp, c), BF16), shape((nz, c, state), BF16),
        ],
        scratch_shapes=[
            pltpu.VMEM((c, tokens), BF16), pltpu.VMEM((2, c, 128), F32), pltpu.VMEM((c, tokens), BF16),
            pltpu.VMEM((nz, tokens, c), BF16), pltpu.VMEM((nz, c, state), F32),
            pltpu.VMEM((hops, nz, c, state), BF16), pltpu.VMEM((hops, nz, c, state), BF16),
            dma((hops, nz)), dma((hops, nz)),
        ],
        compiler_params=pltpu.CompilerParams(
            collective_id=4, has_side_effects=True, vmem_limit_bytes=56 * MIB
        ),
        cost_estimate=cost(2 * inner * tokens * (state + width), 28 * inner * tokens),
    )(y, g, h1, x, gain, sums, scale, cm, whole, nt)


def weight_grad_kernel(ndp, total, *refs):
    left_ref, right_ref = refs[0], refs[1]
    r = left_ref.shape[0] // ndp
    if total:
        sums_ref, out_ref, left = refs[2:]

        @pl.when(pl.program_id(0) == 0)
        def _():
            inverse = lax.rsqrt(sums_ref[0:1] / total + EPSILON)

            @pl.loop(0, left.shape[0] // 64)
            def _(i):
                rows = pl.ds(pl.multiple_of(i * 64, 64), 64)
                left[rows, :] = (left_ref[rows, :].astype(F32) * inverse).astype(BF16)
    else:
        out_ref, left = refs[2], left_ref
    for d in range(ndp):
        out_ref[d, 0] = mm(left[d * r : (d + 1) * r, :], right_ref[0], 1, 0).astype(BF16)


def weight_grad(ndp, left, right, sums=None):
    width, tokens = left.shape
    nz, _, c = right.shape
    r, inner = width // ndp, nz * c
    operands = [left, right]
    specs = [pl.BlockSpec((width, tokens), lambda z: (0, 0)), pl.BlockSpec((1, tokens, c), lambda z: (z, 0, 0))]
    scratch = []
    if sums is not None:
        operands.append(sums)
        specs.append(pl.BlockSpec((8, tokens), lambda z: (0, 0)))
        scratch = [pltpu.VMEM((width, tokens), BF16)]
    return pl.pallas_call(
        functools.partial(weight_grad_kernel, ndp, 0 if sums is None else inner * 2),
        grid=(nz,),
        in_specs=specs,
        out_specs=pl.BlockSpec((ndp, 1, r, c), lambda z: (0, z, 0, 0)),
        out_shape=shape((ndp, nz, r, c), BF16),
        scratch_shapes=scratch,
        compiler_params=params(),
        cost_estimate=cost(2 * inner * tokens * width, 8 * inner * tokens),
    )(*operands)


def conv_back_kernel(
    nz, sc,
    dx_hbm, p_hbm, db_hbm, dc_hbm, st_hbm, plane,
    pars, match, ahead, v_ref, dt_ref, xdx_ref, da_ref, rates_ref, mix_ref,
    vl, small_t, table_ref, early_ref,
    st, dstates, e2, p2, cols, scols, shifts, moved, acc, queue, squeue, heads, halo, sheads, shalo, turn, slanes,
    load, e_load, ds_send, ds_recv, halo_send, halo_recv, early_send, early_recv, early_own,
):
    nh = 2 * nz
    _, c, wide = queue.shape
    tokens = wide - 128
    sr = 2 * sc + 16
    dp, head = lax.axis_index("dp"), lax.axis_index("head")
    core, zed = lax.rem(head, 2), lax.div(head, 2)

    def column_loads(z):
        at, place = pl.ds(pl.multiple_of(z * c, 16), c), lax.rem(z, 2)
        return [
            pltpu.make_async_copy(dx_hbm.at[at], e2.at[place, pl.ds(0, c)], e_load.at[0, place]),
            pltpu.make_async_copy(p_hbm.at[at], p2.at[place], e_load.at[1, place]),
        ]

    for copy in column_loads(0):
        copy.start()
    loads = [
        pltpu.make_async_copy(a, b, load.at[i])
        for i, (a, b) in enumerate([(st_hbm, st), (db_hbm, dstates.at[0]), (dc_hbm, dstates.at[1])])
    ]
    for copy in loads:
        copy.start()

    barrier = pltpu.get_barrier_semaphore()
    for k in range(1, nh):
        pl.semaphore_signal(barrier, inc=1, device_id=(dp, lax.rem(head + k, nh)), device_id_type=MESH)
    pl.semaphore_wait(barrier, nh - 1)

    def remote(src, dst, send_sem, recv_sem, device):
        pltpu.make_async_remote_copy(
            src_ref=src, dst_ref=dst, send_sem=send_sem, recv_sem=recv_sem, device_id=device, device_id_type=MESH
        ).start()

    def wait_for(ref, sem):
        pltpu.make_async_copy(ref, ref, sem).wait()

    for i, ref in enumerate((db_hbm, dc_hbm)):
        remote(ref, dstates.at[2 + i], ds_send.at[i], ds_recv.at[i], (dp, zed * 2 + 1 - core))

    for k in range(1, nz):
        z = lax.rem(zed + k, nz)
        remote(plane.at[z], early_ref.at[zed], early_send.at[k], early_recv.at[zed], (dp, z * 2 + core))
    keep_own = pltpu.make_async_copy(plane.at[zed], early_ref.at[zed], early_own.at[0])
    keep_own.start()

    place = lax.broadcasted_iota(jnp.int32, (256, 128), 0) - lax.broadcasted_iota(jnp.int32, (256, 128), 1)

    def build_shifts(mask, first, before):
        @pl.loop(0, tokens // 128)
        def _(b):
            at = pl.ds(pl.multiple_of(before + b * 128, 128), 128)
            for k in range(3):
                shifts[b, :, k * 128 : k * 128 + 128] = jnp.where(
                    place == first(k), mask[k : k + 1, at], 0.0
                ).astype(BF16)

    def shift(source, count):
        @pl.loop(0, tokens // 128)
        def _(b):
            at = pl.multiple_of(b * 128, 128)
            out = mm(source[:, pl.ds(at, 256)], shifts[b], 1, 0).astype(BF16)
            for k in range(3):
                moved[k, 0:count, pl.ds(at, 128)] = out[:, k * 128 : k * 128 + 128]

    def slopes(source, taps, rows, base, grad):
        at = pl.ds(base, 256)
        terms = [moved[k, rows, at].astype(F32) for k in range(3)]
        terms.append(source[rows, pl.ds(LH + base, 256)].astype(F32))
        pre = taps[:, 4:5]
        for k in range(4):
            pre = pre + taps[:, k : k + 1] * terms[k]
        sig = sigmoid(pre)
        q = grad * (sig * (1.0 + pre * (1.0 - sig)))
        return q, [folded(q * term) for term in terms] + [folded(q)]

    def line_sums(count, to):
        for k in range(5):
            to(k)[...] = jnp.sum(acc[k, 0:count].T, axis=0, keepdims=True)

    build_shifts(match, lambda k: 125 + k, LH)

    @pl.loop(0, nz)
    def _(z):
        @pl.when(z < nz - 1)
        def _():
            for copy in column_loads(z + 1):
                copy.start()

        for copy in column_loads(z):
            copy.wait()
        e, p = e2.at[lax.rem(z, 2)], p2.at[lax.rem(z, 2)]
        cols[...] = pars[2 * z + core, 0:8, :].T
        shift(p, c)

        @pl.loop(0, c // 16, unroll=2)
        def _(i):
            rows_at = pl.ds(pl.multiple_of(i * 16, 16), 16)
            taps = cols[rows_at, :]
            totals = None
            for base in range(0, tokens, 256):
                q, terms = slopes(p, taps, rows_at, base, e[rows_at, pl.ds(base, 256)])
                queue[z, rows_at, pl.ds(base, 256)] = q.astype(BF16)
                totals = terms if totals is None else [a + b for a, b in zip(totals, terms)]
            for k in range(5):
                acc[k, rows_at, :] = totals[k]

        heads[z] = queue[z, :, 0:128].astype(F32).T[0:8]

        @pl.when(zed > 0)
        def _():
            remote(
                heads.at[z], halo.at[z], halo_send.at[z], halo_recv.at[z], (dp, (zed - 1) * 2 + core)
            )

        line_sums(c, lambda k: table_ref.at[z, k : k + 1])
        table_ref[z, 5:6] = mix_ref[z, 0:1]
        table_ref[z, 6:16] = jnp.zeros((10, c), F32)
        table_ref[z, 8:9] = mix_ref[z, 1:2]

    count = nz * 8
    da, dt, rates = da_ref[...], dt_ref[...], rates_ref[:, 0:1]
    step_grad = jnp.where(dt > TINY, xdx_ref[...] / jnp.maximum(dt, TINY), 0.0) + rates * da
    steps_grad = step_grad * sigmoid(v_ref[...])
    for k, v in ((6, steps_grad), (7, rates * (dt * da))):
        padded = folded(v)
        if count < 128:
            padded = jnp.concatenate([padded, jnp.zeros((128 - count, 128), F32)], axis=0)
        line = jnp.sum(padded.T, axis=0, keepdims=True)
        for z in range(nz):
            table_ref[z, k : k + 1, 0:128] = line[:, 0:128]
    steps_low = steps_grad.astype(BF16)

    for i in range(3):
        loads[i].wait()
    for i in range(2):
        wait_for(dstates.at[2 + i], ds_recv.at[i])
    for z in range(nz):
        both = pars[2 * z, 8:16, 0:128] + pars[2 * z + 1, 8:16, 0:128]
        scols[z * 2 * sc : (z + 1) * 2 * sc, :] = both.T[0 : 2 * sc, 1:6]

    @pl.loop(0, tokens // 128)
    def _(b):
        at = pl.ds(pl.multiple_of(b * 128, 128), 128)
        for i in range(2):
            e2[0, i * 128 : i * 128 + 128, at] = (dstates[i, at, :] + dstates[2 + i, at, :]).T

    bc_rows = 2 * sc * nz
    shift(st, bc_rows)

    @pl.loop(0, bc_rows // 16, unroll=2)
    def _(i):
        rows_at = pl.ds(pl.multiple_of(i * 16, 16), 16)
        taps = scols[rows_at, :]
        totals = None
        for base in range(0, tokens, 256):
            q, terms = slopes(st, taps, rows_at, base, e2[0, rows_at, pl.ds(base, 256)])
            squeue[rows_at, pl.ds(base, 256)] = q.astype(BF16)
            totals = terms if totals is None else [a + b for a, b in zip(totals, terms)]
        for k in range(5):
            acc[k, rows_at, :] = totals[k]

    sheads[...] = squeue[:, 0:128].astype(F32).T[0:8]

    @pl.when(zed > 0)
    def _():
        remote(sheads, shalo, halo_send.at[nz], halo_recv.at[nz], (dp, (zed - 1) * 2 + core))

    for k in range(5):
        line = jnp.sum(acc[k, 0:bc_rows].T, axis=0, keepdims=True)
        for z in range(nz):
            table_ref[z, 9 + k : 10 + k, 0 : 2 * sc] = line[:, z * 2 * sc : (z + 1) * 2 * sc]

    build_shifts(ahead, lambda k: 3 - k, 0)

    @pl.when(zed == nz - 1)
    def _():
        halo[...] = jnp.zeros(halo.shape, F32)
        shalo[...] = jnp.zeros(shalo.shape, F32)

    @pl.when(zed < nz - 1)
    def _():
        wait_for(shalo, halo_recv.at[nz])

    def back_taps(source, taps, rows_at, base):
        at = pl.ds(base, 256)
        grad = taps[:, 3:4] * source[rows_at, at].astype(F32)
        for k in range(3):
            grad = grad + taps[:, k : k + 1] * moved[k, rows_at, at].astype(F32)
        return grad

    squeue[:, tokens:] = jnp.concatenate([shalo[...], jnp.zeros((120, bc_rows), F32)], axis=0).T.astype(BF16)
    shift(squeue, bc_rows)
    for z in range(nz):
        for i in range(2 * sc // 16):
            rows_at = slice(z * 2 * sc + i * 16, z * 2 * sc + i * 16 + 16)
            mine = ((i * 16) // sc == core).astype(F32)
            taps = scols[rows_at, :] * mine
            for base in range(0, tokens, 256):
                slanes[z, i * 16 : i * 16 + 16, pl.ds(base, 256)] = back_taps(
                    squeue, taps, rows_at, base
                ).astype(BF16)
        slanes[z, 2 * sc : 2 * sc + 16, :] = jnp.concatenate(
            [steps_low[z * 8 : z * 8 + 8].astype(F32), jnp.zeros((8, tokens), F32)], axis=0
        ).astype(BF16)

    def values_back(z):
        @pl.when(zed < nz - 1)
        def _():
            wait_for(halo.at[z], halo_recv.at[z])

        queue[z, :, tokens:] = jnp.concatenate([halo[z], jnp.zeros((120, c), F32)], axis=0).T.astype(BF16)
        cols[...] = pars[2 * z + core, 0:8, :].T
        shift(queue.at[z], c)

        @pl.loop(0, c // 16, unroll=2)
        def _(i):
            rows_at = pl.ds(pl.multiple_of(i * 16, 16), 16)
            taps = cols[rows_at, :]
            for base in range(0, tokens, 256):
                turn[rows_at, pl.ds(base, 256)] = back_taps(queue.at[z], taps, rows_at, base).astype(BF16)

        vl[z] = turn[...].T

    @pl.loop(0, nz)
    def _(z):
        values_back(z)

    small_t[...] = slanes[...].reshape(nz * sr, tokens).T
    keep_own.wait()
    for k in range(1, nz):
        z = lax.rem(zed + k, nz)
        wait_for(early_ref.at[z], early_recv.at[z])
        wait_for(plane.at[z], early_send.at[k])
    for i in range(2):
        wait_for(dstates.at[2 + i], ds_send.at[i])

    @pl.when(zed > 0)
    def _():
        for z in range(nz):
            wait_for(heads.at[z], halo_send.at[z])
        wait_for(sheads, halo_send.at[nz])


def conv_back(nz, sc, dx, p, db, dc, st, plane, pars, match, ahead, v, dt, xdx, da, rates, mixed):
    inner, tokens = dx.shape
    c = inner // nz
    sr, most = 2 * sc + 16, max(c, st.shape[0])
    anywhere = pl.BlockSpec(memory_space=pl.ANY)
    vmem = pl.BlockSpec(memory_space=pltpu.VMEM)
    dma = pltpu.SemaphoreType.DMA

    def buffer(*dims, dtype=F32):
        return pltpu.VMEM(dims, dtype)

    low = functools.partial(buffer, dtype=BF16)
    return pl.pallas_call(
        functools.partial(conv_back_kernel, nz, sc),
        in_specs=[anywhere] * 6 + [vmem] * 9,
        out_specs=[vmem] * 3 + [anywhere],
        out_shape=[shape((nz, tokens, c), BF16), shape((tokens, nz * sr), BF16), shape((nz, 16, c), F32), shape(plane.shape, BF16)],
        scratch_shapes=[
            low(*st.shape), buffer(4, tokens, 128), buffer(2, most, tokens), low(2, c, LH + tokens), buffer(c, 8),
            buffer(st.shape[0], 5), low(tokens // 128, 256, 384), low(3, most, tokens), buffer(5, most, 128),
            low(nz, c, tokens + 128), low(st.shape[0], tokens + 128), buffer(nz, 8, c), buffer(nz, 8, c),
            buffer(8, st.shape[0]), buffer(8, st.shape[0]), low(c, tokens), low(nz, sr, tokens),
            dma((3,)), dma((2, 2)), dma((2,)), dma((2,)), dma((nz + 1,)), dma((nz + 1,)), dma((nz,)), dma((nz,)), dma((1,)),
        ],
        compiler_params=pltpu.CompilerParams(
            collective_id=3, has_side_effects=True, vmem_limit_bytes=56 * MIB
        ),
        cost_estimate=cost(8 * inner * tokens * 384, 40 * MIB),
    )(dx, p, db, dc, st, plane, pars, match, ahead, v, dt, xdx, da, rates, mixed)


def last_kernel(
    ndp, nz, sc,
    nt_hbm, vl_hbm, small_hbm, gl_hbm, wg_hbm, wv_hbm, ws_hbm, x_hbm, cot_hbm, plane, gated_hbm, wo_hbm,
    table_ref, gain_ref, sums_ref,
    sum_ref, grad_ref, norm_ref, row_ref, out_ref, early_ref,
    nt, vl, small_t, gl, wg, wv, ws, x, cot, small_g, blocks, own, keep, send, got,
    keep_out, send_out, got_out,
    got_first, got_second, got_hi, got_lo, z_out, z_got, tables, trows, norm_own, norms, norm_sum, norm_sums,
    load, w_load, first_send, first_recv, second_send, second_recv, hi_send, hi_recv, lo_send, lo_recv,
    z_send, z_recv, table_send, table_recv, trow_send, trow_recv, sib_send, sib_recv,
    out_send, out_recv, gated_load,
    norm_send, norm_recv, plane_send, plane_recv, early_send, early_recv, early_own,
):
    nh, lo = 2 * nz, ndp // 2
    width, tokens = nt.shape
    n = tokens // 2
    rows, c = own.shape[1:]
    sr = 2 * sc + 16
    r = width // ndp
    half = rows // 32 * 16
    dp, head = lax.axis_index("dp"), lax.axis_index("head")
    core, zed = lax.rem(head, 2), lax.div(head, 2)
    dhi, dlo = lax.div(dp, lo), lax.rem(dp, lo)
    hi_peer = (1 - dhi) * lo + dlo
    lo_peers = [dhi * lo + lax.rem(dlo + k, lo) for k in range(1, lo)]
    diagonal = [(1 - dhi) * lo + lax.rem(dlo + k, lo) for k in range(1, lo)]
    top, low = pl.ds(0, half), pl.ds(half, rows - half)
    order = [1] + [nz - 1] * (nz > 2) + list(range(2, nz - 1)) + [0]
    slots = [lax.rem(zed + zi, nz) for zi in order]

    loads = [
        pltpu.make_async_copy(a, b, load.at[i])
        for i, (a, b) in enumerate([
            (nt_hbm, nt), (small_hbm, small_t), (vl_hbm, vl), (gl_hbm, gl), (ws_hbm, ws), (x_hbm, x), (cot_hbm, cot),
        ])
    ]
    for copy in loads:
        copy.start()

    barrier = pltpu.get_barrier_semaphore()
    partners = [(dp, lax.rem(head + k, nh)) for k in range(1, nh)]
    partners += [(lax.rem(dp + k, ndp), head) for k in range(1, ndp)]
    for partner in partners:
        pl.semaphore_signal(barrier, inc=1, device_id=partner, device_id_type=MESH)
    pl.semaphore_wait(barrier, len(partners))

    def remote(src, dst, send_sem, recv_sem, device):
        pltpu.make_async_remote_copy(
            src_ref=src, dst_ref=dst, send_sem=send_sem, recv_sem=recv_sem, device_id=device, device_id_type=MESH
        ).start()

    def wait_for(ref, sem):
        pltpu.make_async_copy(ref, ref, sem).wait()

    for k in range(1, nz):
        z = lax.rem(zed + k, nz)
        remote(plane.at[z], early_ref.at[zed], early_send.at[k], early_recv.at[zed], (dp, z * 2 + core))
    keep_own = pltpu.make_async_copy(plane.at[zed], early_ref.at[zed], early_own.at[0])
    keep_own.start()

    for k in range(1, ndp):
        remote(
            table_ref, tables.at[k - 1], table_send.at[k - 1], table_recv.at[k - 1], (lax.rem(dp + k, ndp), head)
        )

    def product(d, z, to):
        left = nt[pl.ds(pl.multiple_of(d * r, 16), r), :]
        to[0:r] = mm(left, vl[z], 1, 0).astype(to.dtype)
        at = pl.multiple_of(z * sr + core * sc, 16)
        to[r : r + sc] = small_g[d, pl.ds(at, sc), :].astype(to.dtype)
        to[r + sc : rows] = small_g[d, pl.ds(pl.multiple_of(z * sr + 2 * sc, 16), 16), :].astype(to.dtype)

    loads[0].wait()
    loads[1].wait()

    @pl.loop(0, ndp)
    def _(d):
        small_g[d] = mm(nt[pl.ds(pl.multiple_of(d * r, 16), r), :], small_t[...], 1, 0).T

    loads[2].wait()
    for j, z in enumerate(slots):
        for i, d in enumerate(diagonal):
            product(d, z, blocks.at[i, j])
            remote(
                blocks.at[i, j, top], got_first.at[i, z], first_send.at[i, j], first_recv.at[i, z],
                (lo_peers[i], head),
            )
            remote(
                blocks.at[i, j, low], got_second.at[i, z], second_send.at[i, j], second_recv.at[i, z],
                (hi_peer, head),
            )

    across = lo - 1
    for j, z in enumerate(slots):
        product(hi_peer, z, blocks.at[across, j])
        for i, d in enumerate(lo_peers):
            product(d, z, blocks.at[lo + i, j])
        product(dp, z, own.at[j])
        total = blocks[across, j, top].astype(F32)
        for i in range(lo - 1):
            wait_for(got_first.at[i, z], first_recv.at[i, z])
            total = total + got_first[i, z].astype(F32)
        blocks[across, j, top] = total.astype(BF16)
        remote(blocks.at[across, j], got_hi.at[z], hi_send.at[j], hi_recv.at[z], (hi_peer, head))
        for i, d in enumerate(lo_peers):
            wait_for(got_second.at[i, z], second_recv.at[i, z])
            blocks[lo + i, j, low] = (
                blocks[lo + i, j, low].astype(F32) + got_second[i, z].astype(F32)
            ).astype(BF16)
            remote(blocks.at[lo + i, j], got_lo.at[i, z], lo_send.at[i, j], lo_recv.at[i, z], (d, head))

    for copy in loads[3:5]:
        copy.wait()

    def weight_loads(d, slot):
        return [
            pltpu.make_async_copy(wg_hbm.at[d], wg.at[slot], w_load.at[0, slot]),
            pltpu.make_async_copy(wv_hbm.at[d], wv.at[slot], w_load.at[1, slot]),
        ]

    for copy in weight_loads(0, 0):
        copy.start()

    @pl.loop(0, ndp)
    def _(d):
        slot = lax.rem(d, 2)

        @pl.when(d < ndp - 1)
        def _():
            for copy in weight_loads(d + 1, 1 - slot):
                copy.start()

        for copy in weight_loads(d, slot):
            copy.wait()
        weights = [weight[slot].reshape(nz * c, r) for weight in (wg, wv)] + [ws[d].reshape(nz * sr, r)]
        for which, buffer in ((1 - core, send), (core, keep)):
            at = pl.ds(pl.multiple_of(which * n, 128), n)
            out = mm(small_t[at, :], weights[2], 1, 0)
            for left, weight in ((gl, weights[0]), (vl, weights[1])):
                out = out + mm(jnp.concatenate([left[z, at, :] for z in range(nz)], axis=1), weight, 1, 0)
            buffer[d] = out.astype(buffer.dtype)

    remote(send, got, sib_send.at[0], sib_recv.at[0], (dp, zed * 2 + 1 - core))

    def pass_on(j):
        z = slots[j]
        wait_for(got_hi.at[z], hi_recv.at[z])
        total = own[j] + got_hi[z].astype(F32)
        for i in range(lo - 1):
            wait_for(got_lo.at[i, z], lo_recv.at[i, z])
            total = total + got_lo[i, z].astype(F32)
        own[j] = total
        if order[j]:
            z_out[j] = total.astype(BF16)
            remote(z_out.at[j], z_got.at[zed], z_send.at[j], z_recv.at[zed], (dp, z * 2 + core))

    get_gated = pltpu.make_async_copy(gated_hbm, gl, gated_load.at[0])
    get_gated.start()

    def out_loads(d, slot):
        return pltpu.make_async_copy(wo_hbm.at[d], wg.at[slot], w_load.at[0, slot])

    out_loads(0, 0).start()
    pass_on(0)
    get_gated.wait()

    @pl.loop(0, ndp)
    def _(d):
        slot = lax.rem(d, 2)

        @pl.when(d < ndp - 1)
        def _():
            out_loads(d + 1, 1 - slot).start()

        out_loads(d, slot).wait()
        weight = wg[slot].reshape(nz * c, r)
        for which, buffer in ((1 - core, send_out), (core, keep_out)):
            at = pl.ds(pl.multiple_of(which * n, 128), n)
            left = jnp.concatenate([gl[z, at, :] for z in range(nz)], axis=1)
            buffer[d] = mm(left, weight, 1, 0).astype(buffer.dtype)

    remote(send_out, got_out, out_send.at[0], out_recv.at[0], (dp, zed * 2 + 1 - core))
    pass_on(1)

    total = table_ref[...]
    for k in range(1, ndp):
        wait_for(tables.at[k - 1], table_recv.at[k - 1])
        total = total + tables[k - 1]
    tables[ndp - 1] = total
    for j, z in enumerate(slots[:-1]):
        remote(tables.at[ndp - 1, z], trows.at[zed], trow_send.at[j], trow_recv.at[zed], (dp, z * 2 + core))

    for copy in loads[5:]:
        copy.wait()
    wait_for(got, sib_recv.at[0])
    norm_own[...] = jnp.zeros(norm_own.shape, F32)

    @pl.loop(0, n // 128)
    def _(i):
        at = pl.ds(pl.multiple_of(i * 128, 128), 128)
        full = jnp.concatenate([keep[d, at, :] + got[d, at, :].astype(F32) for d in range(ndp)], axis=1)
        tokens_x = x[at, :].astype(F32)
        inverse = lax.rsqrt(jnp.mean(tokens_x * tokens_x, axis=1, keepdims=True) + EPSILON)
        gained = full * gain_ref[...]
        dots = jnp.sum(gained * tokens_x, axis=1, keepdims=True)
        grad = inverse * gained - tokens_x * (inverse * inverse * inverse / width) * dots
        grad_ref[at, :] = (cot[at, :].astype(F32) + grad).astype(BF16)
        norm_own[0:1] += jnp.sum(full * (tokens_x * inverse), axis=0, keepdims=True)

    for k in range(1, nh):
        remote(
            norm_own, norms.at[k - 1], norm_send.at[k - 1], norm_recv.at[k - 1], (dp, lax.rem(head + k, nh))
        )
    for j in range(2, nz - 1):
        pass_on(j)
    total = norm_own[...]
    for k in range(1, nh):
        wait_for(norms.at[k - 1], norm_recv.at[k - 1])
        total = total + norms[k - 1]
    norm_sum[...] = total
    for k in range(1, ndp):
        remote(
            norm_sum, norm_sums.at[k - 1], plane_send.at[k - 1], plane_recv.at[k - 1],
            (lax.rem(dp + k, ndp), head),
        )
    wait_for(got_out, out_recv.at[0])

    @pl.loop(0, n // 128)
    def _(i):
        at = pl.ds(pl.multiple_of(i * 128, 128), 128)
        inverse = lax.rsqrt(sums_ref[:, at].T[:, 0:1] / (2 * nz * c) + EPSILON)
        branch = jnp.concatenate([keep_out[d, at, :] + got_out[d, at, :].astype(F32) for d in range(ndp)], axis=1)
        out_ref[at, :] = (x[at, :].astype(F32) + branch * inverse).astype(BF16)

    pass_on(nz - 1)
    total = tables[ndp - 1, zed]
    for k in range(1, nz):
        z = lax.rem(zed + k, nz)
        wait_for(trows.at[z], trow_recv.at[z])
        total = total + trows[z]
    row_ref[...] = total
    total = norm_sum[...]
    for k in range(1, ndp):
        wait_for(norm_sums.at[k - 1], plane_recv.at[k - 1])
        total = total + norm_sums[k - 1]
    norm_ref[...] = total
    total = own[nz - 1]
    for k in range(1, nz):
        z = lax.rem(zed + k, nz)
        wait_for(z_got.at[z], z_recv.at[z])
        total = total + z_got[z].astype(F32)
    sum_ref[...] = total

    keep_own.wait()
    for k in range(1, nz):
        z = lax.rem(zed + k, nz)
        wait_for(early_ref.at[z], early_recv.at[z])
        wait_for(plane.at[z], early_send.at[k])
    for j in range(nz):
        for i in range(lo - 1):
            wait_for(got_first.at[i, j], first_send.at[i, j])
            wait_for(got_second.at[i, j], second_send.at[i, j])
            wait_for(got_lo.at[i, j], lo_send.at[i, j])
        wait_for(got_hi.at[j], hi_send.at[j])
    for j in range(nz - 1):
        wait_for(z_out.at[j], z_send.at[j])
        wait_for(trows.at[j], trow_send.at[j])
    for k in range(ndp - 1):
        wait_for(table_ref, table_send.at[k])
        wait_for(norm_sum, plane_send.at[k])
    for k in range(nh - 1):
        wait_for(norm_own, norm_send.at[k])
    wait_for(send, sib_send.at[0])
    wait_for(send_out, out_send.at[0])


def last_steps(ndp, nz, sc, nt, vl, small, gl, wg, wv, ws, x, cot, plane, gated, wo, table, gain, sums):
    nh, lo = 2 * nz, ndp // 2
    width, tokens = nt.shape
    n = tokens // 2
    c = vl.shape[2]
    r = width // ndp
    rows = r + sc + 16
    half = rows // 32 * 16
    anywhere = pl.BlockSpec(memory_space=pl.ANY)
    vmem = pl.BlockSpec(memory_space=pltpu.VMEM)
    dma = pltpu.SemaphoreType.DMA

    def buffer(*dims, dtype=F32):
        return pltpu.VMEM(dims, dtype)

    low = functools.partial(buffer, dtype=BF16)
    return pl.pallas_call(
        functools.partial(last_kernel, ndp, nz, sc),
        in_specs=[anywhere] * 12 + [vmem] * 3,
        out_specs=[vmem] * 5 + [anywhere],
        out_shape=[
            shape((rows, c), F32),
            shape((n, width), BF16),
            shape((8, width), F32),
            shape((16, c), F32),
            shape((n, width), BF16),
            shape(plane.shape, BF16),
        ],
        scratch_shapes=[
            low(width, tokens), low(*vl.shape), low(*small.shape), low(*gl.shape), low(2, nz, c, r), low(2, nz, c, r),
            low(*ws.shape), low(n, width), low(n, width), buffer(ndp, nz * ws.shape[2], r),
            low(ndp - 1, nz, rows, c), buffer(nz, rows, c), buffer(ndp, n, r), low(ndp, n, r), low(ndp, n, r),
            buffer(ndp, n, r), low(ndp, n, r), low(ndp, n, r),
            low(lo - 1, nz, half, c), low(lo - 1, nz, rows - half, c), low(nz, rows, c), low(lo - 1, nz, rows, c),
            low(nz - 1, rows, c), low(nz, rows, c), buffer(ndp, nz, 16, c), buffer(nz, 16, c),
            buffer(8, width), buffer(nh - 1, 8, width), buffer(8, width), buffer(ndp - 1, 8, width),
            dma((7,)), dma((2, 2)),
            dma((lo - 1, nz)), dma((lo - 1, nz)), dma((lo - 1, nz)), dma((lo - 1, nz)),
            dma((nz,)), dma((nz,)), dma((lo - 1, nz)), dma((lo - 1, nz)),
            dma((nz,)), dma((nz,)), dma((ndp - 1,)), dma((ndp - 1,)), dma((nz,)), dma((nz,)),
            dma((1,)), dma((1,)), dma((1,)), dma((1,)), dma((1,)), dma((nh - 1,)), dma((nh - 1,)), dma((ndp - 1,)), dma((ndp - 1,)),
            dma((nz,)), dma((nz,)), dma((1,)),
        ],
        compiler_params=pltpu.CompilerParams(
            collective_id=2, has_side_effects=True, vmem_limit_bytes=63 * MIB
        ),
        cost_estimate=cost(4 * nz * c * tokens * width, 40 * MIB),
    )(nt, vl, small, gl, wg, wv, ws, x, cot, plane, gated, wo, table, gain, sums)

def shards(
    block_input, lengths, norm_gain, in_gate, in_value, in_states, in_steps,
    conv_value, conv_value_bias, conv_states, conv_states_bias,
    step_bias, decay_log, skip_gain, gate_gain, out_proj, cotangent,
):
    ndp, nh = lax.axis_size("dp"), lax.axis_size("head")
    nz, lo = nh // 2, ndp // 2
    own, width = block_input.shape
    tokens = 2 * own
    dp, head = lax.axis_index("dp"), lax.axis_index("head")
    core, zed = head % 2, head // 2
    dhi, dlo = dp // lo, dp % lo
    r, cols = in_gate.shape
    hs, sc, taps = step_bias.shape[0], in_states.shape[1], conv_value.shape[0]
    heads, inner, state, hw = hs * nz, cols * nz, sc * nz, cols // hs
    total = 2 * inner

    def sibling(v):
        return lax.ppermute(v, "head", [(i, i ^ 1) for i in range(nh)])

    def zshift(v, k):
        return lax.ppermute(v, "head", [(i, (i + 2 * k) % nh) for i in range(nh)])

    def zstep(v, k):
        return lax.ppermute(
            v, "head", [(i, i + 2 * k) for i in range(nh) if 0 <= i + 2 * k < nh]
        )

    def lo_shift(v, k):
        return lax.ppermute(
            v, "dp", [(h * lo + i, h * lo + (i + k) % lo) for h in range(2) for i in range(lo)]
        )

    def hi_swap(v):
        return lax.ppermute(v, "dp", [(i, (i + lo) % ndp) for i in range(ndp)])

    def block(g, d, start, count):
        return lax.dynamic_slice(g, (d, 0, start, 0), (1, nz, count, g.shape[3]))[0]

    def slot(k):
        return (dlo + k) % lo

    def scatter_sends(g):
        rows = g.shape[2]
        half = rows // 32 * 16
        diagonal = [(1 - dhi) * lo + slot(k) for k in range(1, lo)]
        return [(block(g, d, 0, half), block(g, d, half, rows - half)) for d in diagonal]

    def scatter_first(sends):
        return [lo_shift(a, k + 1) for k, (a, _) in enumerate(sends)], [hi_swap(b) for _, b in sends]

    def scatter(g, first, second, hold=None):
        rows = g.shape[2]
        half = rows // 32 * 16
        peer = (1 - dhi) * lo + dlo
        top = block(g, peer, 0, half).astype(F32)
        for v in first:
            top = top + v.astype(F32)
        sents = [jnp.concatenate([top.astype(BF16), block(g, peer, half, rows - half)], axis=1)]
        for k in range(1, lo):
            d = dhi * lo + slot(k)
            low = block(g, d, half, rows - half).astype(F32) + second[k - 1].astype(F32)
            sents.append(jnp.concatenate([block(g, d, 0, half), low.astype(BF16)], axis=1))
        if hold is not None:
            sents, hold = lax.optimization_barrier((sents, hold))
        total_here = block(g, dp, 0, rows).astype(F32) + hi_swap(sents[0]).astype(F32)
        for k in range(1, lo):
            total_here = total_here + lo_shift(sents[k], k).astype(F32)
        return total_here.astype(BF16), hold

    heads_par = jnp.stack([step_bias, decay_log, skip_gain])
    (
        g_value, g_small, g_gate, g_out, everyone, normed_t, cot_t, value_pre, gate_pre, x_t, states_pre, bc,
        seg, match, ahead, v_steps, dt, a2, scale_back, rates, whole, sin,
    ) = gather_project(
        ndp, nz, sc, hs, hw, block_input, cotangent, in_value, in_gate, out_proj, in_states.T, in_steps.T,
        conv_value, conv_value_bias[None], gate_gain[None], heads_par, conv_states, conv_states_bias[None],
        norm_gain[None, :], lengths,
    )
    sin = sin.reshape(inner, state)
    x_t = x_t.reshape(inner, tokens)
    value_pre = value_pre.reshape(inner, LH + tokens)
    gate_pre = gate_pre.reshape(inner, tokens)
    bm, cm = bc[0], bc[1]
    places = [(i // hs) * 8 + i % hs for i in range(heads)]
    pars = lax.dynamic_index_in_dim(everyone.reshape(nz, 2, 16, cols), core, 1, keepdims=False)
    taps_t = pars[:, :8].transpose(0, 2, 1).reshape(inner, 8)
    gain = taps_t[:, 5:6]
    skip = pars[:, 8, :8].reshape(nz * 8)
    y_t, st = scan_forward(places, x_t, dt, a2, seg, bm, cm, sin, skip[:, None])

    gated, h1, sums = mix(g_out, cot_t, y_t, gate_pre, gain)
    sums = sums + sibling(sums)
    own_sums = lax.dynamic_slice_in_dim(sums, core * own, own, 1)
    out_blocks = weight_grad(ndp, cot_t, gated, sums=sums)
    out_sends = scatter_sends(out_blocks)
    y_late, out_sends = lax.optimization_barrier((y_t, out_sends))
    dy_t, gate_low, mix_cols, gate_blocks, rin = unmix(
        ndp, nz, hs, hw, y_late, gate_pre, h1, x_t, gain, sums, scale_back, cm, whole, normed_t
    )
    rin = rin.reshape(inner, state)
    gate_first = scatter_first(scatter_sends(gate_blocks))
    plane_out, dy_t = scatter(out_blocks, *scatter_first(out_sends), hold=dy_t)
    dx_t, db, dc, xdx, da = scan_backward(
        places, x_t, dy_t, y_t, dt, a2, seg, bm, cm, st, rin, skip[:, None]
    )

    gate_first, dx_t = lax.optimization_barrier((gate_first, dx_t))
    plane_gate, _ = scatter(gate_blocks, *gate_first)
    value_low, small_low, table, early_out = conv_back(
        nz, sc, dx_t, value_pre, db, dc, states_pre, plane_out, everyone, match, ahead, v_steps, dt, xdx, da, rates, mix_cols
    )
    sum_value, input_grad, norm_rows, row, out, early_gate = last_steps(
        ndp, nz, sc, normed_t, value_low, small_low, gate_low, g_gate, g_value, g_small, block_input, cotangent,
        plane_gate, gated, g_out, table, norm_gain[None, :], own_sums,
    )
    sum_out = early_out.astype(F32).sum(axis=0)
    sum_gate = early_gate.astype(F32).sum(axis=0)
    own_lanes = lax.dynamic_slice_in_dim(row[6:14], zed * 8, hs, 1)
    states_row = lax.dynamic_slice_in_dim(row[9:14], core * sc, sc, 1)
    return (
        out,
        input_grad,
        norm_rows[0],
        sum_gate,
        sum_value[:r],
        sum_value[r : r + sc].T,
        sum_value[r + sc : r + sc + hs].T,
        row[:taps],
        row[4],
        states_row[:taps],
        states_row[taps],
        own_lanes[0],
        own_lanes[1],
        row[8].reshape(hs, hw).sum(axis=1),
        row[5],
        sum_out,
    )


def solution(mesh):
    both = P(("dp", "head"), None)
    grid = P("dp", "head")
    return jax.shard_map(
        shards,
        mesh=mesh,
        in_specs=(
            both, P("dp", None), P(), grid, grid, grid, grid,
            P(None, "head"), P("head"), P(None, "head"), P("head"),
            P("head"), P("head"), P("head"), P("head"), grid, both,
        ),
        out_specs=(
            both, both, P(), grid, grid, grid, grid,
            P(None, "head"), P("head"), P(None, "head"), P("head"),
            P("head"), P("head"), P("head"), P("head"), grid,
        ),
        check_vma=False,
    )
```
